32 devices in a mesh: gz: 16 (over z, x, core), gy: 2 (over y).
Axes of the slice: x: 2, y: 2, z: 4, core: 2. Of those that a mesh axis runs over, the one named last changes fastest.
Arguments:
- levels: float32 [4, 64, 16, 512], P(None, 'gz', 'gy'), may hold values from -20 to 20
- ct_image: float32 [64, 16, 512], P('gz', 'gy'), may hold values from -4 to 4
- region_means: float32 [16], replicated, may hold values from -1.5 to 1.5
Outputs:
- evolved: float32 [4, 64, 16, 512], P(None, 'gz', 'gy')
- regularized: float32 [4, 64, 16, 512], P(None, 'gz', 'gy')
The draws below stay inside these ranges and needn't reach their ends.
All inputs are finite; a program needn't handle non-finite values.
Results may differ from the reference program's by a relative error of at most 0.000022.
Values sent between devices are 32-bit elements; how exact they have to be, the bound alone decides.
No kernel may reach another device: no remote copies, remote signals or barrier semaphores. Data moves between devices by JAX's collectives and lax.ppermute only.
A program may use at most 64 MiB of HBM per device.

```python
import math
import jax
import jax.numpy as jnp
from jax import lax

LEVELS = 4
PHASES = 16
UPDATES = 2
KERNEL = 200
NX = 512
NZ = 64
NY = 16


def step_profile(key):
    subkeys = jax.random.split(key, 2)
    edge_low = 0.05 * NX
    edge_high = max(edge_low, min(0.45 * NX, NX - KERNEL - 0.1 * NX))
    fraction = jax.random.uniform(subkeys[0], (LEVELS,), jnp.float32, 0.0, 1.0)
    edge = edge_low + fraction * (edge_high - edge_low)
    direction = jax.random.randint(subkeys[1], (LEVELS,), 0, 2)
    position = jnp.arange(NX, dtype=jnp.float32)
    mirrored = jnp.where(direction[:, None] == 1, NX - 1.0 - position[None, :], position[None, :])
    return -4.5 + 11.5 * jnp.tanh((mirrored - edge[:, None]) / 1.5)


def draw_levels(key, part):
    subkeys = jax.random.split(key, 4)
    full_shape = (LEVELS, NZ, NY, NX)
    profile = step_profile(subkeys[3])[:, None, None, :]
    rough_part = jnp.clip(1.5 * jax.random.normal(subkeys[0], full_shape, jnp.float32), -6.0, 6.0)
    return jnp.clip(rough_part + profile, -19.8, 19.8)


def steps_of(stream_key, shape, cuts, smallest, top_value):
    gain, own = 1.0, jax.random.fold_in(stream_key, 6)
    for axis_at, shards_of in cuts:
        draws = jnp.exp(jax.random.uniform(jax.random.fold_in(own, axis_at), (shards_of,), jnp.float32, smallest / len(cuts), top_value / len(cuts)))
        gain = gain * jnp.repeat(draws, shape[axis_at] // shards_of).reshape([-1 if axis == axis_at else 1 for axis in range(len(shape))])
    return gain


def scatter_about(key, extent, spread, reach, cuts=(), kind=jnp.bfloat16):
    factor_of = steps_of(key, extent, cuts, -0.22, 0.18) if cuts else 1.0
    entries = jax.random.normal(key, extent, jnp.float32) * spread * factor_of
    return jnp.minimum(jnp.maximum(entries, -reach), reach).astype(kind)


def setup_inputs(seed: int = 0) -> dict:
    key_list = jax.random.split(jax.random.key(seed), 4)
    return {
        "levels": draw_levels(jax.random.fold_in(key_list[3], 71), 0),
        "ct_image": scatter_about(key_list[1], (NZ, NY, NX), 1.0, 4.0, ((0, 16), (1, 2)), jnp.float32),
        "region_means": jnp.clip(jax.random.uniform(key_list[2], (PHASES,), jnp.float32, -1.5, 1.5), -1.5, 1.5),
    }


PENALTY = 0.0005
STEP_SIZE = 0.5


def evolve(level_pad, picture, region_means):
    interior = level_pad[:, 1:-1, 1:-1, :]
    side_x = jnp.pad(interior, ((0, 0), (0, 0), (0, 0), (1, 1)))
    laplace = level_pad[:, 2:, 1:-1, :] + level_pad[:, :-2, 1:-1, :]
    laplace = laplace + level_pad[:, 1:-1, 2:, :] + level_pad[:, 1:-1, :-2, :]
    laplace = laplace + side_x[..., 2:] + side_x[..., :-2] - 6.0 * interior
    heaviside = 0.5 + jnp.arctan(interior) / math.pi
    delta_term = 1.0 / (math.pi * (1.0 + interior * interior))
    forces = [jnp.zeros_like(interior[0]) for level_id in range(LEVELS)]
    for phase_id in range(PHASES):
        differ = picture - region_means[phase_id]
        energy = differ * differ
        factors = []
        for level_id in range(LEVELS):
            if (phase_id >> level_id) & 1:
                factors.append(heaviside[level_id])
            else:
                factors.append(1.0 - heaviside[level_id])
        for level_id in range(LEVELS):
            sign_value = 1.0 if (phase_id >> level_id) & 1 else -1.0
            others = energy
            for other_id in range(LEVELS):
                if other_id != level_id:
                    others = others * factors[other_id]
            forces[level_id] = forces[level_id] + sign_value * others
    force_all = jnp.stack(forces, axis=0)
    return interior + STEP_SIZE * delta_term * (laplace - force_all)


def minplus_lines(field_in, line_axis, kernel_reach):
    moved_field = jnp.moveaxis(field_in, line_axis, -1)
    line_shape = moved_field.shape
    line_len = line_shape[-1]
    line_rows = moved_field.reshape(-1, line_len)
    row_count = line_rows.shape[0]
    positions = jnp.arange(line_len, dtype=jnp.float32)
    distance = positions[:, None] - positions[None, :]
    penalty_table = jnp.where(jnp.abs(distance) <= kernel_reach, PENALTY * (distance * distance), jnp.inf).astype(line_rows.dtype)
    row_limit = max(1, 4194304 // (line_len * line_len))
    row_block = 1
    while row_block * 2 <= row_limit and row_count % (row_block * 2) == 0:
        row_block = row_block * 2
    grouped = line_rows.reshape(row_count // row_block, row_block, line_len)

    def block_min(block_rows):
        return jnp.min(block_rows[:, None, :] + penalty_table[None, :, :], axis=2)

    result_rows = lax.map(block_min, grouped)
    return jnp.moveaxis(result_rows.reshape(line_shape), -1, line_axis)


def reference(levels, ct_image, region_means):
    current = levels
    for update_round in range(UPDATES):
        padded = jnp.pad(current, ((0, 0), (1, 1), (1, 1), (0, 0)))
        current = evolve(padded, ct_image, region_means)
    smoothed = minplus_lines(current, 3, KERNEL)
    smoothed = minplus_lines(smoothed, 1, KERNEL)
    smoothed = minplus_lines(smoothed, 2, KERNEL)
    return current, smoothed
```

```python
import functools
import math

import jax
import jax.numpy as jnp
import numpy as np
from jax import lax
from jax.experimental import pallas as pl
from jax.experimental.pallas import tpu as pltpu
from jax.sharding import PartitionSpec as P

LEVELS = 4
PHASES = 16
UPDATES = 2
KERNEL = 200
LANES = 128


PENALTY = 0.0005
STEP_SIZE = 0.5
FAR = 1e30


def with_halo(block, sides, width):
    for axis, dim in sides:
        count = lax.axis_size(axis)
        forward = [(i, i + 1) for i in range(count - 1)]
        backward = [(target, source) for source, target in forward]
        low = lax.ppermute(
            lax.slice_in_dim(block, block.shape[dim] - width, None, axis=dim), axis, forward
        )
        high = lax.ppermute(lax.slice_in_dim(block, 0, width, axis=dim), axis, backward)
        block = jnp.concatenate([low, block, high], axis=dim)
    return block


def evolve(level_pad, picture, region_means):
    interior = level_pad[:, 1:-1, 1:-1, :]
    side_x = jnp.pad(interior, ((0, 0), (0, 0), (0, 0), (1, 1)))
    laplace = level_pad[:, 2:, 1:-1, :] + level_pad[:, :-2, 1:-1, :]
    laplace = laplace + level_pad[:, 1:-1, 2:, :] + level_pad[:, 1:-1, :-2, :]
    laplace = laplace + side_x[..., 2:] + side_x[..., :-2] - 6.0 * interior
    heaviside = 0.5 + jnp.arctan(interior) / math.pi
    delta_term = 1.0 / (math.pi * (1.0 + interior * interior))
    forces = [jnp.zeros_like(interior[0]) for level_id in range(LEVELS)]
    for phase_id in range(PHASES):
        differ = picture - region_means[phase_id]
        energy = differ * differ
        factors = []
        for level_id in range(LEVELS):
            if phase_id >> level_id & 1:
                factors.append(heaviside[level_id])
            else:
                factors.append(1.0 - heaviside[level_id])
        for level_id in range(LEVELS):
            sign_value = 1.0 if phase_id >> level_id & 1 else -1.0
            others = energy
            for other_id in range(LEVELS):
                if other_id != level_id:
                    others = others * factors[other_id]
            forces[level_id] = forces[level_id] + sign_value * others
    force_all = jnp.stack(forces, axis=0)
    return interior + STEP_SIZE * delta_term * (laplace - force_all)


def minplus_lines(field_in, line_axis, kernel_reach):
    moved_field = jnp.moveaxis(field_in, line_axis, -1)
    line_shape = moved_field.shape
    line_len = line_shape[-1]
    line_rows = moved_field.reshape(-1, line_len)
    row_count = line_rows.shape[0]
    positions = jnp.arange(line_len, dtype=jnp.float32)
    distance = positions[:, None] - positions[None, :]
    penalty_table = jnp.where(
        jnp.abs(distance) <= kernel_reach, PENALTY * (distance * distance), jnp.inf
    )
    row_limit = max(1, 1048576 // (line_len * line_len))
    row_block = 1
    while row_block * 2 <= row_limit and row_count % (row_block * 2) == 0:
        row_block = row_block * 2
    grouped = line_rows.reshape(row_count // row_block, row_block, line_len)

    def block_min(block_rows):
        return jnp.min(block_rows[:, None, :] + penalty_table[None, :, :], axis=2)

    result_rows = lax.map(block_min, grouped)
    return jnp.moveaxis(result_rows.reshape(line_shape), -1, line_axis)


def portable_body(levels, ct_image, region_means):
    current = levels
    for _ in range(UPDATES):
        padded = with_halo(current, (("gz", 1), ("gy", 2)), 1)
        current = evolve(padded, ct_image, region_means)
    field = minplus_lines(current, 3, KERNEL)
    for axis, dim in (("gz", 1), ("gy", 2)):
        lines = lax.all_to_all(field, axis, split_axis=3, concat_axis=dim, tiled=True)
        lines = minplus_lines(lines, dim, KERNEL)
        field = lax.all_to_all(lines, axis, split_axis=dim, concat_axis=3, tiled=True)
    return current, field


def pack_kernel(share, lev_ref, ct_ref, out_ref, lines, picture):
    width = lev_ref.shape[1]
    parts = width // share
    halo, quarter = share + 4, (share + 4) // 4
    chunk = halo + quarter
    lines[pl.ds(0, 8), :] = jnp.zeros((8, LANES), jnp.float32)
    lines[pl.ds(8 + width, 8), :] = jnp.zeros((8, LANES), jnp.float32)
    ct = ct_ref[...]
    shifted = [pltpu.roll(ct, (2 - quarter * t) % width, 1) for t in range(4)]
    stacked = jnp.concatenate(shifted, axis=0)
    for b in range(width // LANES):
        cols = slice(b * LANES, (b + 1) * LANES)
        lines[pl.ds(8 + b * LANES, LANES), :] = lev_ref[:, cols].T
        picture[pl.ds(b * LANES, LANES), :] = stacked[:, cols].T
    for r in range(parts):
        out_ref[pl.ds(r * chunk, halo), :] = lines[pl.ds(6 + r * share, halo), :]
        out_ref[pl.ds(r * chunk + halo, quarter), :] = picture[pl.ds(r * share, quarter), :]


def arctan(x):
    size = jnp.abs(x)
    big = jnp.maximum(size, 1.0)
    t = jnp.minimum(size, 1.0) / big
    y = t * t
    p = 0.0028662257
    for c in (-0.0161657367, 0.0429096138, -0.0752896400, 0.1065626393,
              -0.1420889944, 0.1999355085, -0.3333314528, 1.0):
        p = p * y + c
    p = p * t
    p = jnp.where(size > 1.0, (math.pi / 2) - p, p)
    return jnp.where(x < 0.0, -p, p)


def z_penalty(zl, yl, gz):
    lane = np.arange(LANES)
    z = lane // yl % zl
    rows = []
    for step in range(-(gz - 1), gz):
        for turn in range(zl):
            d = (zl * step + z - (z + turn) % zl).astype(np.float32)
            rows.append(np.where(np.abs(d) <= KERNEL, np.float32(PENALTY) * (d * d), np.float32(FAR)))
    return np.stack(rows).astype(np.float32)


def y_penalty(yl, gy):
    lane = np.arange(LANES)
    y = lane % yl
    rows = []
    for step in range(-(gy - 1), gy):
        for turn in range(yl):
            d = (yl * step + y - (y + turn) % yl).astype(np.float32)
            rows.append(np.where(np.abs(d) <= KERNEL, np.float32(PENALTY) * (d * d), np.float32(FAR)))
    return np.stack(rows).astype(np.float32)


def middle_kernel(share, gz, gy, zl, yl, mean_ref, in_ref, zpen_ref, ypen_ref, out_ref,
                  first, turned, zdone):
    parts = gz * gy
    halo, quarter = share + 4, (share + 4) // 4
    chunk = halo + quarter
    wide = share + 2
    tile = zl * yl
    me = lax.axis_index("gz") * gy + lax.axis_index("gy")

    lane = lax.broadcasted_iota(jnp.int32, (1, LANES), 1)
    level = lane // tile
    z = lane // yl % zl
    y = lane % yl

    def moved(value, index):
        rows = value.shape[0]
        pad = -rows % 8
        if pad:
            value = jnp.concatenate([value, jnp.zeros((pad, LANES), value.dtype)], axis=0)
        out = jnp.take_along_axis(
            value, jnp.broadcast_to(index, value.shape), axis=1, mode="promise_in_bounds"
        )
        return out[:rows] if pad else out

    def z_turn(turn):
        return lane + ((z + turn) % zl - z) * yl

    def y_turn(turn):
        return lane + (y + turn) % yl - y

    def mean_of(bits, own):
        value = jnp.zeros((1, LANES), jnp.float32)
        for k in range(LEVELS):
            phase = own << k
            for n in range(3):
                phase |= (bits >> n & 1) << ((k + 1 + n) % LEVELS)
            value = jnp.where(level == k, mean_ref[phase], value)
        return value

    slope, const = [], []
    for bits in range(8):
        low, high = mean_of(bits, 0), mean_of(bits, 1)
        slope.append(-2.0 * (high - low))
        const.append((high - low) * (high + low))
    for n in range(3):
        for bits in range(8):
            if bits >> n & 1:
                slope[bits] = slope[bits] - slope[bits ^ (1 << n)]
                const[bits] = const[bits] - const[bits ^ (1 << n)]

    def picture_of(s, start, rows):
        packed = in_ref[pl.ds(s * chunk + halo, quarter), :]
        runs = []
        for t in range(4):
            only = jnp.where(lane // (LANES // 4) == t, packed, 0.0)
            only = only + pltpu.roll(only, LANES // 2, 1)
            runs.append(only + pltpu.roll(only, LANES // 4, 1))
        return jnp.concatenate(runs, axis=0)[start:start + rows]

    def step(read, s, picture):
        a, b = divmod(s, gy)
        here = read(s, 0)
        near = read(s, -1) + read(s, 1)
        zero = jnp.zeros_like(here)
        up = read(s + gy, 0) if a + 1 < gz else zero
        near = near + moved(jnp.where(z == 0, up, here), z_turn(1))
        down = read(s - gy, 0) if a > 0 else zero
        near = near + moved(jnp.where(z == zl - 1, down, here), z_turn(zl - 1))
        up = read(s + 1, 0) if b + 1 < gy else zero
        near = near + moved(jnp.where(y == 0, up, here), y_turn(1))
        down = read(s - 1, 0) if b > 0 else zero
        near = near + moved(jnp.where(y == yl - 1, down, here), y_turn(yl - 1))
        laplace = near - 6.0 * here
        heaviside = 0.5 + arctan(here) * (1.0 / math.pi)
        h1 = pltpu.roll(heaviside, LANES - tile, 1)
        h2 = pltpu.roll(heaviside, LANES - 2 * tile, 1)
        h3 = pltpu.roll(heaviside, LANES - 3 * tile, 1)
        f = [slope[bits] * picture + const[bits] for bits in range(8)]
        g = [f[bits] + h1 * f[bits | 1] for bits in (0, 2, 4, 6)]
        g = [g[0] + h2 * g[1], g[2] + h2 * g[3]]
        force = g[0] + h3 * g[1]
        delta = 1.0 / (math.pi * (1.0 + here * here))
        return here + STEP_SIZE * delta * (laplace - force)

    row = lax.broadcasted_iota(jnp.int32, (wide, LANES), 0)
    inside = jnp.logical_and(
        jnp.logical_or(row > 0, me > 0), jnp.logical_or(row < wide - 1, me < parts - 1)
    )
    stride = wide + (-wide % 8)
    for s in range(parts):
        read = lambda part, dx: in_ref[pl.ds(part * chunk + 1 + dx, wide), :]
        value = step(read, s, picture_of(s, 1, wide))
        first[pl.ds(s * stride, wide), :] = jnp.where(inside, value, 0.0)
    for s in range(parts):
        read = lambda part, dx: first[pl.ds(part * stride + 1 + dx, share), :]
        value = step(read, s, picture_of(s, 2, share))
        out_ref[pl.ds((2 * s + 1) * share, share), :] = value
        for turn in range(zl):
            turned[turn, pl.ds(s * share, share), :] = (
                moved(value, z_turn(turn)) if turn else value
            )

    group = 8
    for b in range(gy):
        for low in range(0, gz, group):
            best = [None] * group
            for other in range(gz):
                for turn in range(zl):
                    value = turned[turn, pl.ds((other * gy + b) * share, share), :]
                    for n in range(group):
                        at = (low + n - other + gz - 1) * zl + turn
                        new = value + zpen_ref[pl.ds(at, 1), :]
                        best[n] = new if best[n] is None else jnp.minimum(best[n], new)
            for n in range(group):
                zdone[pl.ds(((low + n) * gy + b) * share, share), :] = best[n]

    for a in range(gz):
        best = [None] * gy
        for other in range(gy):
            whole = zdone[pl.ds((a * gy + other) * share, share), :]
            for turn in range(yl):
                value = moved(whole, y_turn(turn)) if turn else whole
                for b in range(gy):
                    at = (b - other + gy - 1) * yl + turn
                    new = value + ypen_ref[pl.ds(at, 1), :]
                    best[b] = new if best[b] is None else jnp.minimum(best[b], new)
        for b in range(gy):
            out_ref[pl.ds(2 * (a * gy + b) * share, share), :] = best[b]


def finish_kernel(share, pen_ref, in_ref, ev_ref, reg_ref, field, lowest):
    width = ev_ref.shape[1]
    parts = width // share
    margin = 8
    count = width // 8
    group = 8
    reach = KERNEL // 8
    field[pl.ds(0, margin), :] = jnp.full((margin, LANES), FAR, jnp.float32)
    field[pl.ds(margin + width, margin), :] = jnp.full((margin, LANES), FAR, jnp.float32)
    for r in range(parts):
        field[pl.ds(margin + r * share, share), :] = in_ref[pl.ds(2 * r * share, share), :]
    rows = LANES // share
    for c in range(width // LANES):
        block = jnp.concatenate(
            [in_ref[pl.ds((2 * (c * rows + r) + 1) * share, share), :] for r in range(rows)], axis=0
        )
        ev_ref[:, c * LANES:(c + 1) * LANES] = block.T

    lowest[...] = field[pl.ds(margin, width), :]

    def offset(rho, carry):
        for low in range(0, count, group):
            best = [lowest[pl.ds(8 * (low + n), 8), :] for n in range(group)]
            plus, minus = {}, {}
            for e in range(reach):
                cost = pen_ref[8 * e + rho]
                for n in range(group):
                    up, down = low + n + e, low + n - e
                    pair = []
                    if up < count:
                        if up not in plus:
                            plus[up] = field[pl.ds(margin + 8 * up + rho, 8), :]
                        pair.append(plus[up])
                    if down >= 0:
                        if down not in minus:
                            minus[down] = field[pl.ds(margin + 8 * down - rho, 8), :]
                        pair.append(minus[down])
                    if not pair:
                        continue
                    value = pair[0] if len(pair) == 1 else jnp.minimum(pair[0], pair[1])
                    best[n] = jnp.minimum(best[n], value + cost)
            for n in range(group):
                lowest[pl.ds(8 * (low + n), 8), :] = best[n]
        return carry

    lax.fori_loop(1, 9, offset, 0)
    for c in range(width // LANES):
        reg_ref[:, c * LANES:(c + 1) * LANES] = lowest[pl.ds(c * LANES, LANES), :].T


def split_body(levels, ct_image, region_means):
    gz, gy = lax.axis_size("gz"), lax.axis_size("gy")
    _, zl, yl, width = levels.shape
    parts = gz * gy
    share = width // parts
    chunk = share + 4 + (share + 4) // 4
    f32 = jnp.float32
    vmem = pl.BlockSpec(memory_space=pltpu.VMEM)
    smem = pl.BlockSpec(memory_space=pltpu.SMEM)
    params = pltpu.CompilerParams(vmem_limit_bytes=24 * 1024 * 1024)

    packed = pl.pallas_call(
        functools.partial(pack_kernel, share),
        out_shape=jax.ShapeDtypeStruct((parts * chunk, LANES), f32),
        in_specs=[vmem, vmem],
        out_specs=vmem,
        scratch_shapes=[pltpu.VMEM((width + 16, LANES), f32), pltpu.VMEM((width, LANES), f32)],
        compiler_params=params,
        name="pack",
    )(levels.reshape(LANES, width), ct_image.reshape(zl * yl, width))
    packed = lax.all_to_all(
        packed.reshape(parts, chunk, 1, LANES), ("gz", "gy"), split_axis=0, concat_axis=0, tiled=True
    ).reshape(parts * chunk, LANES)

    wide = share + 2
    stride = wide + (-wide % 8)
    both = pl.pallas_call(
        functools.partial(middle_kernel, share, gz, gy, zl, yl),
        out_shape=jax.ShapeDtypeStruct((parts * 2 * share, LANES), f32),
        in_specs=[smem, vmem, vmem, vmem],
        out_specs=vmem,
        scratch_shapes=[
            pltpu.VMEM((parts * stride, LANES), f32),
            pltpu.VMEM((zl, width, LANES), f32),
            pltpu.VMEM((width, LANES), f32),
        ],
        compiler_params=params,
        name="middle",
    )(region_means, packed, jnp.asarray(z_penalty(zl, yl, gz)), jnp.asarray(y_penalty(yl, gy)))
    both = lax.all_to_all(
        both.reshape(parts, 2 * share, LANES), ("gz", "gy"), split_axis=0, concat_axis=0, tiled=True
    ).reshape(parts * 2 * share, LANES)

    d = np.arange(KERNEL + 1, dtype=np.float32)
    costs = np.float32(PENALTY) * (d * d)
    out = jax.ShapeDtypeStruct((LANES, width), f32)
    evolved, regularized = pl.pallas_call(
        functools.partial(finish_kernel, share),
        out_shape=(out, out),
        in_specs=[smem, vmem],
        out_specs=(vmem, vmem),
        scratch_shapes=[pltpu.VMEM((width + 16, LANES), f32), pltpu.VMEM((width, LANES), f32)],
        compiler_params=params,
        name="finish",
    )(jnp.asarray(costs), both)
    return evolved.reshape(levels.shape), regularized.reshape(levels.shape)


def body(levels, ct_image, region_means):
    parts = lax.axis_size("gz") * lax.axis_size("gy")
    count, zl, yl, width = levels.shape
    share = width // parts
    fits = count == LEVELS and count * zl * yl == LANES and width % LANES == 0
    if fits and width % parts == 0 and share % 8 == 0 and lax.axis_size("gz") % 8 == 0:
        return split_body(levels, ct_image, region_means)
    return portable_body(levels, ct_image, region_means)


def solution(mesh):
    return jax.shard_map(
        body,
        mesh=mesh,
        in_specs=(P(None, "gz", "gy", None), P("gz", "gy", None), P()),
        out_specs=(P(None, "gz", "gy", None), P(None, "gz", "gy", None)),
        check_vma=False,
    )
```

```python
import functools
import math

import jax
import jax.numpy as jnp
import numpy as np
from jax import lax
from jax.experimental import pallas as pl
from jax.experimental.pallas import tpu as pltpu
from jax.sharding import PartitionSpec as P

LEVELS = 4
PHASES = 16
UPDATES = 2
KERNEL = 200
LANES = 128


PENALTY = 0.0005
STEP_SIZE = 0.5
FAR = 1e30


def with_halo(block, sides, width):
    for axis, dim in sides:
        count = lax.axis_size(axis)
        forward = [(i, i + 1) for i in range(count - 1)]
        backward = [(target, source) for source, target in forward]
        low = lax.ppermute(
            lax.slice_in_dim(block, block.shape[dim] - width, None, axis=dim), axis, forward
        )
        high = lax.ppermute(lax.slice_in_dim(block, 0, width, axis=dim), axis, backward)
        block = jnp.concatenate([low, block, high], axis=dim)
    return block


def evolve(level_pad, picture, region_means):
    interior = level_pad[:, 1:-1, 1:-1, :]
    side_x = jnp.pad(interior, ((0, 0), (0, 0), (0, 0), (1, 1)))
    laplace = level_pad[:, 2:, 1:-1, :] + level_pad[:, :-2, 1:-1, :]
    laplace = laplace + level_pad[:, 1:-1, 2:, :] + level_pad[:, 1:-1, :-2, :]
    laplace = laplace + side_x[..., 2:] + side_x[..., :-2] - 6.0 * interior
    heaviside = 0.5 + jnp.arctan(interior) / math.pi
    delta_term = 1.0 / (math.pi * (1.0 + interior * interior))
    forces = [jnp.zeros_like(interior[0]) for level_id in range(LEVELS)]
    for phase_id in range(PHASES):
        differ = picture - region_means[phase_id]
        energy = differ * differ
        factors = []
        for level_id in range(LEVELS):
            if phase_id >> level_id & 1:
                factors.append(heaviside[level_id])
            else:
                factors.append(1.0 - heaviside[level_id])
        for level_id in range(LEVELS):
            sign_value = 1.0 if phase_id >> level_id & 1 else -1.0
            others = energy
            for other_id in range(LEVELS):
                if other_id != level_id:
                    others = others * factors[other_id]
            forces[level_id] = forces[level_id] + sign_value * others
    force_all = jnp.stack(forces, axis=0)
    return interior + STEP_SIZE * delta_term * (laplace - force_all)


def minplus_lines(field_in, line_axis, kernel_reach):
    moved_field = jnp.moveaxis(field_in, line_axis, -1)
    line_shape = moved_field.shape
    line_len = line_shape[-1]
    line_rows = moved_field.reshape(-1, line_len)
    row_count = line_rows.shape[0]
    positions = jnp.arange(line_len, dtype=jnp.float32)
    distance = positions[:, None] - positions[None, :]
    penalty_table = jnp.where(
        jnp.abs(distance) <= kernel_reach, PENALTY * (distance * distance), jnp.inf
    )
    row_limit = max(1, 1048576 // (line_len * line_len))
    row_block = 1
    while row_block * 2 <= row_limit and row_count % (row_block * 2) == 0:
        row_block = row_block * 2
    grouped = line_rows.reshape(row_count // row_block, row_block, line_len)

    def block_min(block_rows):
        return jnp.min(block_rows[:, None, :] + penalty_table[None, :, :], axis=2)

    result_rows = lax.map(block_min, grouped)
    return jnp.moveaxis(result_rows.reshape(line_shape), -1, line_axis)


def portable_body(levels, ct_image, region_means):
    current = levels
    for _ in range(UPDATES):
        padded = with_halo(current, (("gz", 1), ("gy", 2)), 1)
        current = evolve(padded, ct_image, region_means)
    field = minplus_lines(current, 3, KERNEL)
    for axis, dim in (("gz", 1), ("gy", 2)):
        lines = lax.all_to_all(field, axis, split_axis=3, concat_axis=dim, tiled=True)
        lines = minplus_lines(lines, dim, KERNEL)
        field = lax.all_to_all(lines, axis, split_axis=dim, concat_axis=3, tiled=True)
    return current, field


def pack_kernel(share, lev_ref, ct_ref, out_ref, lines, picture):
    width = lev_ref.shape[1]
    parts = width // share
    halo, quarter = share + 4, (share + 4) // 4
    chunk = halo + quarter
    lines[pl.ds(0, 8), :] = jnp.zeros((8, LANES), jnp.float32)
    lines[pl.ds(8 + width, 8), :] = jnp.zeros((8, LANES), jnp.float32)
    ct = ct_ref[...]
    shifted = [pltpu.roll(ct, (2 - quarter * t) % width, 1) for t in range(4)]
    stacked = jnp.concatenate(shifted, axis=0)
    for b in range(width // LANES):
        cols = slice(b * LANES, (b + 1) * LANES)
        lines[pl.ds(8 + b * LANES, LANES), :] = lev_ref[:, cols].T
        picture[pl.ds(b * LANES, LANES), :] = stacked[:, cols].T
    for r in range(parts):
        out_ref[pl.ds(r * chunk, quarter), :] = picture[pl.ds(r * share, quarter), :]
        out_ref[pl.ds(r * chunk + quarter, halo), :] = lines[pl.ds(6 + r * share, halo), :]


HALF_ANGLE = (
    0.6366196870803833, -0.21219870448112488, 0.12714172899723053, -0.0893140509724617,
    0.06329755485057831, -0.03813650459051132, 0.015633534640073776, -0.0030433274805545807,
)


def heaviside_and_rate(u):
    s = 1.0 + u * u
    q = lax.rsqrt(s)
    r = u / (1.0 + s * q)
    y = r * r
    p = HALF_ANGLE[-1]
    for c in HALF_ANGLE[-2::-1]:
        p = p * y + c
    return 0.5 + r * p, (q * q) * (STEP_SIZE / math.pi)


def cost_of(d):
    return float(np.float32(PENALTY) * np.float32(d * d))


def middle_kernel(share, gz, gy, zl, yl, mean_ref, in_ref, out_ref,
                  picture, first, turned, zdone, ypen):
    parts = gz * gy
    halo, quarter = share + 4, (share + 4) // 4
    chunk = halo + quarter
    wide = share + 2
    stride = wide + (-wide % 8)
    span = halo + (-halo % 8)
    tile = zl * yl
    me = lax.axis_index("gz") * gy + lax.axis_index("gy")

    lane = lax.broadcasted_iota(jnp.int32, (1, LANES), 1)
    level = lane // tile
    z = lane // yl % zl
    y = lane % yl

    def moved(value, index):
        rows = value.shape[0]
        pad = -rows % 8
        if pad:
            value = jnp.concatenate([value, jnp.zeros((pad, LANES), value.dtype)], axis=0)
        out = jnp.take_along_axis(
            value, jnp.broadcast_to(index, value.shape), axis=1, mode="promise_in_bounds"
        )
        return out[:rows] if pad else out

    def z_turn(turn):
        return lane + ((z + turn) % zl - z) * yl

    def y_turn(turn):
        return lane + (y + turn) % yl - y

    for s in range(parts):
        packed = in_ref[pl.ds(s * chunk, 8), :]
        for t in range(4):
            run = moved(packed, t * tile + lane % tile)
            picture[pl.ds(s * span + t * quarter, quarter), :] = run[:quarter]

    def mean_of(bits, own):
        value = jnp.zeros((1, LANES), jnp.float32)
        for k in range(LEVELS):
            phase = own << k
            for n in range(3):
                phase |= (bits >> n & 1) << ((k + 1 + n) % LEVELS)
            value = jnp.where(level == k, mean_ref[phase], value)
        return value

    slope, const = [], []
    for bits in range(8):
        low, high = mean_of(bits, 0), mean_of(bits, 1)
        slope.append(-2.0 * (high - low))
        const.append((high - low) * (high + low))
    for n in range(3):
        for bits in range(8):
            if bits >> n & 1:
                slope[bits] = slope[bits] - slope[bits ^ (1 << n)]
                const[bits] = const[bits] - const[bits ^ (1 << n)]

    def step(read, s, pic):
        a, b = divmod(s, gy)
        here = read(s, 0)
        near = read(s, -1) + read(s, 1)
        up = read(s + gy, 0) if a + 1 < gz else 0.0
        near = near + moved(jnp.where(z == 0, up, here), z_turn(1))
        down = read(s - gy, 0) if a > 0 else 0.0
        near = near + moved(jnp.where(z == zl - 1, down, here), z_turn(zl - 1))
        up = read(s + 1, 0) if b + 1 < gy else 0.0
        near = near + moved(jnp.where(y == 0, up, here), y_turn(1))
        down = read(s - 1, 0) if b > 0 else 0.0
        near = near + moved(jnp.where(y == yl - 1, down, here), y_turn(yl - 1))
        laplace = near - 6.0 * here
        h, rate = heaviside_and_rate(here)
        h1 = pltpu.roll(h, LANES - tile, 1)
        h2 = pltpu.roll(h, LANES - 2 * tile, 1)
        h3 = pltpu.roll(h, LANES - 3 * tile, 1)
        f = [slope[bits] * pic + const[bits] for bits in range(8)]
        g = [f[bits] + h1 * f[bits | 1] for bits in (0, 2, 4, 6)]
        g = [g[0] + h2 * g[1], g[2] + h2 * g[3]]
        force = g[0] + h3 * g[1]
        return here + rate * (laplace - force)

    row = lax.broadcasted_iota(jnp.int32, (wide, LANES), 0)
    inside = jnp.logical_and(
        jnp.logical_or(row > 0, me > 0), jnp.logical_or(row < wide - 1, me < parts - 1)
    )
    for s in range(parts):
        read = lambda part, dx: in_ref[pl.ds(part * chunk + quarter + 1 + dx, wide), :]
        value = step(read, s, picture[pl.ds(s * span + 1, wide), :])
        first[pl.ds(s * stride, wide), :] = jnp.where(inside, value, 0.0)
    for s in range(parts):
        read = lambda part, dx: first[pl.ds(part * stride + 1 + dx, share), :]
        value = step(read, s, picture[pl.ds(s * span + 2, share), :])
        for turn in range(zl):
            turned[turn, pl.ds(s * share, share), :] = (
                moved(value, z_turn(turn)) if turn else value
            )

    group = 8
    for b in range(gy):
        for low in range(0, gz, group):
            best = [None] * group
            for other in range(-1, gz):
                for turn in range(zl):
                    value = FAR
                    if other >= 0:
                        value = turned[turn, pl.ds((other * gy + b) * share, share), :]
                    if turn:
                        above = FAR
                        if other + 1 < gz:
                            above = turned[turn, pl.ds(((other + 1) * gy + b) * share, share), :]
                        value = jnp.where(z < zl - turn, value, above)
                    elif other < 0:
                        continue
                    for n in range(group):
                        d = zl * (other - low - n) + turn
                        if abs(d) > KERNEL:
                            continue
                        new = value + cost_of(d)
                        best[n] = new if best[n] is None else jnp.minimum(best[n], new)
            for n in range(group):
                zdone[pl.ds(((low + n) * gy + b) * share, share), :] = best[n]

    for gap in range(-(gy - 1), gy):
        for turn in range(yl):
            d = (yl * gap + y - (y + turn) % yl).astype(jnp.float32)
            pen = jnp.where(jnp.abs(d) <= KERNEL, PENALTY * (d * d), FAR)
            at = (gap + gy - 1) * yl + turn
            ypen[pl.ds(8 * at, 8), :] = jnp.broadcast_to(pen, (8, LANES))
    for a in range(gz):
        for half in range(share // 8):
            best = [None] * gy
            for other in range(gy):
                whole = zdone[pl.ds((a * gy + other) * share + 8 * half, 8), :]
                for turn in range(yl):
                    value = moved(whole, y_turn(turn)) if turn else whole
                    for b in range(gy):
                        at = (b - other + gy - 1) * yl + turn
                        new = value + ypen[pl.ds(8 * at, 8), :]
                        best[b] = new if best[b] is None else jnp.minimum(best[b], new)
            for b in range(gy):
                out_ref[pl.ds((a * gy + b) * share + 8 * half, 8), :] = best[b]


def finish_kernel(in_ref, reg_ref, edge, done, sems):
    width = in_ref.shape[0]
    count = width // 8
    group = 8
    far = jnp.full((8, LANES), FAR, jnp.float32)
    edge[pl.ds(0, 8), :] = far
    edge[pl.ds(8, 8), :] = in_ref[pl.ds(0, 8), :]
    edge[pl.ds(16, 8), :] = in_ref[pl.ds(width - 8, 8), :]
    edge[pl.ds(24, 8), :] = far

    def rows(at):
        if at < 0:
            return edge[pl.ds(8 + at, 8), :]
        if at > width - 8:
            return edge[pl.ds(16 + at - (width - 8), 8), :]
        return in_ref[pl.ds(at, 8), :]

    copies = []
    for c in range(width // LANES):
        for low in range(c * LANES // 8, (c + 1) * LANES // 8, group):
            best = [rows(8 * (low + n)) for n in range(group)]
            for rho in range(1, 9):
                plus, minus = {}, {}
                for e in range((KERNEL - rho) // 8 + 1):
                    cost = cost_of(8 * e + rho)
                    for n in range(group):
                        up, down = low + n + e, low + n - e
                        pair = []
                        if 8 * up + rho < width:
                            if up not in plus:
                                plus[up] = rows(8 * up + rho)
                            pair.append(plus[up])
                        if 8 * down - rho > -8:
                            if down not in minus:
                                minus[down] = rows(8 * down - rho)
                            pair.append(minus[down])
                        if not pair:
                            continue
                        value = pair[0] if len(pair) == 1 else jnp.minimum(pair[0], pair[1])
                        best[n] = jnp.minimum(best[n], value + cost)
            for n in range(group):
                done[pl.ds(8 * (low + n), 8), :] = best[n]
        cols = pl.ds(c * LANES, LANES)
        done[cols, :] = done[cols, :].T
        copies.append(pltpu.make_async_copy(done.at[cols, :], reg_ref.at[:, cols], sems.at[c]))
        copies[-1].start()
    for copy in copies:
        copy.wait()


def edges_kernel(zl, yl, lev_ref, ct_ref, up_ref, down_ref, side_ref, cup_ref, cdown_ref):
    upper = lax.axis_index("gy") == 0
    near = jnp.where(upper, yl - 1, 0)
    next_near = jnp.where(upper, yl - 2, 1)
    plane = zl * yl
    for k in range(LEVELS):
        for n in range(2):
            at = pl.ds((2 * k + n) * yl, yl)
            up_ref[at, :] = lev_ref[pl.ds(k * plane + (zl - 2 + n) * yl, yl), :]
            down_ref[at, :] = lev_ref[pl.ds(k * plane + n * yl, yl), :]
        for z in range(zl):
            base = k * plane + z * yl
            side_ref[pl.ds(2 * zl * k + z, 1), :] = lev_ref[pl.ds(base + near, 1), :]
            side_ref[pl.ds(2 * zl * k + zl + z, 1), :] = lev_ref[pl.ds(base + next_near, 1), :]
        cup_ref[pl.ds(k, 1), :] = lev_ref[pl.ds(k * plane + (zl - 1) * yl + near, 1), :]
        cdown_ref[pl.ds(k, 1), :] = lev_ref[pl.ds(k * plane + near, 1), :]
    at = pl.ds(2 * LEVELS * yl, yl)
    up_ref[at, :] = ct_ref[pl.ds((zl - 1) * yl, yl), :]
    down_ref[at, :] = ct_ref[pl.ds(0, yl), :]
    for z in range(zl):
        side_ref[pl.ds(2 * zl * LEVELS + z, 1), :] = ct_ref[pl.ds(z * yl + near, 1), :]


def local_kernel(zl, yl, gz, mean_ref, lev_ref, ct_ref, low_ref, high_ref, side_ref,
                 clow_ref, chigh_ref, out_ref, first, strip, around, strip_first):
    width = lev_ref.shape[1]
    at_z = lax.axis_index("gz")
    upper = lax.axis_index("gy") == 0
    edge = jnp.where(upper, yl - 1, 0)
    plane = zl * yl

    const = [mean_ref[p] * mean_ref[p] for p in range(PHASES)]
    slope = [-2.0 * mean_ref[p] for p in range(PHASES)]
    for k in range(LEVELS):
        for p in range(PHASES):
            if p >> k & 1:
                const[p] = const[p] - const[p ^ (1 << k)]
                slope[p] = slope[p] - slope[p ^ (1 << k)]

    def forces(h, pic):
        c = [None] + [slope[p] * pic + const[p] for p in range(1, PHASES)]
        out = []
        for k in range(LEVELS):
            others = [n for n in range(LEVELS) if n != k]
            part = [c[1 << k | sum((bits >> i & 1) << n for i, n in enumerate(others))]
                    for bits in range(8)]
            for n in others:
                part = [part[i] + h[n] * part[i + 1] for i in range(0, len(part), 2)]
            out.append(part[0])
        return out

    column = lax.broadcasted_iota(jnp.int32, (8, width), 1)
    sub = lax.broadcasted_iota(jnp.int32, (8, width), 0)

    def along_x(u):
        left = jnp.where(column == 0, 0.0, pltpu.roll(u, 1, 1))
        right = jnp.where(column == width - 1, 0.0, pltpu.roll(u, width - 1, 1))
        return left + right

    def advance(here, near, pic):
        pairs = [heaviside_and_rate(u) for u in here]
        force = forces([h for h, _ in pairs], pic)
        return [
            u + rate * (n - 6.0 * u - f)
            for u, n, (_, rate), f in zip(here, near, pairs, force)
        ]

    def along_y(u, row):
        row_up = jnp.where(upper, row, 0.0)
        row_down = jnp.where(upper, 0.0, row)
        above = jnp.where(sub == yl - 1, row_up, pltpu.roll(u, yl - 1, 0))
        below = jnp.where(sub == 0, row_down, pltpu.roll(u, 1, 0))
        return above + below

    def level(k, z):
        if z < 0:
            return low_ref[pl.ds((2 * k + 2 + z) * yl, yl), :]
        if z >= zl:
            return high_ref[pl.ds((2 * k + z - zl) * yl, yl), :]
        return lev_ref[pl.ds(k * plane + z * yl, yl), :]

    def side(k, z):
        if z < 0:
            return clow_ref[pl.ds(k, 1), :]
        if z >= zl:
            return chigh_ref[pl.ds(k, 1), :]
        return side_ref[pl.ds(2 * zl * k + z, 1), :]

    def picture(z):
        at = pl.ds(2 * LEVELS * yl, yl)
        if z < 0:
            return low_ref[at, :]
        if z >= zl:
            return high_ref[at, :]
        return ct_ref[pl.ds(z * yl, yl), :]

    planes = zl + 2
    for z in range(-1, zl + 1):
        here = [level(k, z) for k in range(LEVELS)]
        near = [
            level(k, z - 1) + level(k, z + 1) + along_x(here[k]) + along_y(here[k], side(k, z))
            for k in range(LEVELS)
        ]
        value = advance(here, near, picture(z))
        for k in range(LEVELS):
            new = value[k]
            if z < 0:
                new = jnp.where(at_z > 0, new, 0.0)
            if z >= zl:
                new = jnp.where(at_z < gz - 1, new, 0.0)
            first[pl.ds((k * planes + z + 1) * yl, yl), :] = new

    strip[...] = jnp.zeros_like(strip)
    around[...] = jnp.zeros_like(around)
    for k in range(LEVELS):
        for z in range(-1, zl + 1):
            strip[pl.ds(8 * k + z + 1, 1), :] = side(k, z)
        for z in range(zl):
            around[pl.ds(8 * k + z + 1, 1), :] = (
                lev_ref[pl.ds(k * plane + z * yl + edge, 1), :]
                + side_ref[pl.ds(2 * zl * k + zl + z, 1), :]
            )
    for z in range(zl):
        strip[pl.ds(8 * LEVELS + z + 1, 1), :] = side_ref[pl.ds(2 * zl * LEVELS + z, 1), :]
    here = [strip[pl.ds(8 * k, 8), :] for k in range(LEVELS)]
    near = [
        pltpu.roll(u, 7, 0) + pltpu.roll(u, 1, 0) + along_x(u) + around[pl.ds(8 * k, 8), :]
        for k, u in enumerate(here)
    ]
    value = advance(here, near, strip[pl.ds(8 * LEVELS, 8), :])
    for k in range(LEVELS):
        strip_first[pl.ds(8 * k, 8), :] = value[k]

    for z in range(zl):
        at = lambda k, dz: first[pl.ds((k * planes + z + 1 + dz) * yl, yl), :]
        here = [at(k, 0) for k in range(LEVELS)]
        near = [
            at(k, -1) + at(k, 1) + along_x(here[k])
            + along_y(here[k], strip_first[pl.ds(8 * k + z + 1, 1), :])
            for k in range(LEVELS)
        ]
        value = advance(here, near, picture(z))
        for k in range(LEVELS):
            out_ref[pl.ds(k * plane + z * yl, yl), :] = value[k]


def split_body(levels, ct_image, region_means):
    gz, gy = lax.axis_size("gz"), lax.axis_size("gy")
    _, zl, yl, width = levels.shape
    parts = gz * gy
    share = width // parts
    halo, quarter = share + 4, (share + 4) // 4
    chunk = halo + quarter
    f32 = jnp.float32
    vmem = pl.BlockSpec(memory_space=pltpu.VMEM)
    smem = pl.BlockSpec(memory_space=pltpu.SMEM)
    params = pltpu.CompilerParams(vmem_limit_bytes=24 * 1024 * 1024)
    lines = levels.reshape(LANES, width)
    image = ct_image.reshape(zl * yl, width)

    packed = pl.pallas_call(
        functools.partial(pack_kernel, share),
        out_shape=jax.ShapeDtypeStruct((parts * chunk, LANES), f32),
        in_specs=[vmem, vmem],
        out_specs=vmem,
        scratch_shapes=[pltpu.VMEM((width + 16, LANES), f32), pltpu.VMEM((width, LANES), f32)],
        compiler_params=params,
        name="pack",
    )(lines, image)
    arrived = lax.all_to_all(
        packed.reshape(parts, chunk, 1, LANES), ("gz", "gy"), split_axis=0, concat_axis=0, tiled=True
    ).reshape(parts * chunk, LANES)

    shape = lambda rows: jax.ShapeDtypeStruct((rows, width), f32)
    up, down, side, cup, cdown = pl.pallas_call(
        functools.partial(edges_kernel, zl, yl),
        out_shape=(shape((2 * LEVELS + 1) * yl), shape((2 * LEVELS + 1) * yl),
                   shape(2 * zl * LEVELS + zl), shape(LEVELS), shape(LEVELS)),
        in_specs=[vmem, vmem],
        out_specs=(vmem,) * 5,
        compiler_params=params,
        name="edges",
    )(lines, image)
    rise = [(i, i + 1) for i in range(gz - 1)]
    fall = [(i + 1, i) for i in range(gz - 1)]
    swap = [(0, 1), (1, 0)]
    both_ways = lambda pairs: [
        (a * gy + s, b * gy + t) for a, b in pairs for s, t in swap
    ]
    low = lax.ppermute(up, "gz", rise)
    high = lax.ppermute(down, "gz", fall)
    side = lax.ppermute(side, "gy", swap)
    clow = lax.ppermute(cup, ("gz", "gy"), both_ways(rise))
    chigh = lax.ppermute(cdown, ("gz", "gy"), both_ways(fall))

    wide = share + 2
    stride = wide + (-wide % 8)
    span = halo + (-halo % 8)
    passed = pl.pallas_call(
        functools.partial(middle_kernel, share, gz, gy, zl, yl),
        out_shape=jax.ShapeDtypeStruct((width, LANES), f32),
        in_specs=[smem, vmem],
        out_specs=vmem,
        scratch_shapes=[
            pltpu.VMEM((parts * span, LANES), f32),
            pltpu.VMEM((parts * stride, LANES), f32),
            pltpu.VMEM((zl, width, LANES), f32),
            pltpu.VMEM((width, LANES), f32),
            pltpu.VMEM((8 * yl * (2 * gy - 1), LANES), f32),
        ],
        compiler_params=params,
        name="middle",
    )(region_means, arrived)
    passed, low, high, side, clow, chigh = lax.optimization_barrier(
        (passed, low, high, side, clow, chigh)
    )
    passed = lax.all_to_all(
        passed.reshape(parts, share, LANES), ("gz", "gy"), split_axis=0, concat_axis=0, tiled=True
    ).reshape(width, LANES)

    evolved = pl.pallas_call(
        functools.partial(local_kernel, zl, yl, gz),
        out_shape=shape(LANES),
        in_specs=[smem] + [vmem] * 7,
        out_specs=vmem,
        scratch_shapes=[
            pltpu.VMEM((LEVELS * (zl + 2) * yl, width), f32),
            pltpu.VMEM((8 * (LEVELS + 1), width), f32),
            pltpu.VMEM((8 * LEVELS, width), f32),
            pltpu.VMEM((8 * LEVELS, width), f32),
        ],
        compiler_params=params,
        cost_estimate=pl.CostEstimate(flops=10_000_000, bytes_accessed=1_000_000, transcendentals=0),
        name="local",
    )(region_means, lines, image, low, high, side, clow, chigh)

    regularized = pl.pallas_call(
        finish_kernel,
        out_shape=shape(LANES),
        in_specs=[vmem],
        out_specs=pl.BlockSpec(memory_space=pl.ANY),
        scratch_shapes=[
            pltpu.VMEM((32, LANES), f32),
            pltpu.VMEM((width, LANES), f32),
            pltpu.SemaphoreType.DMA((width // LANES,)),
        ],
        compiler_params=params,
        name="finish",
    )(passed)
    return evolved.reshape(levels.shape), regularized.reshape(levels.shape)


def body(levels, ct_image, region_means):
    gz, gy = lax.axis_size("gz"), lax.axis_size("gy")
    parts = gz * gy
    count, zl, yl, width = levels.shape
    fits = count == LEVELS and count * zl * yl == LANES and yl == 8 and zl >= 2
    fits = fits and gy == 2 and gz % 8 == 0 and gz * zl <= KERNEL
    fits = fits and width % LANES == 0 and width % parts == 0 and width // parts % 8 == 0
    if fits:
        return split_body(levels, ct_image, region_means)
    return portable_body(levels, ct_image, region_means)


def solution(mesh):
    return jax.shard_map(
        body,
        mesh=mesh,
        in_specs=(P(None, "gz", "gy", None), P("gz", "gy", None), P()),
        out_specs=(P(None, "gz", "gy", None), P(None, "gz", "gy", None)),
        check_vma=False,
    )
```

```python
import functools
import math

import jax
import jax.numpy as jnp
import numpy as np
from jax import lax
from jax.experimental import pallas as pl
from jax.experimental.pallas import tpu as pltpu
from jax.sharding import PartitionSpec as P

LEVELS = 4
PHASES = 16
UPDATES = 2
KERNEL = 200
LANES = 128


PENALTY = 0.0005
STEP_SIZE = 0.5
FAR = 1e30


def with_halo(block, sides, width):
    for axis, dim in sides:
        count = lax.axis_size(axis)
        forward = [(i, i + 1) for i in range(count - 1)]
        backward = [(target, source) for source, target in forward]
        low = lax.ppermute(
            lax.slice_in_dim(block, block.shape[dim] - width, None, axis=dim), axis, forward
        )
        high = lax.ppermute(lax.slice_in_dim(block, 0, width, axis=dim), axis, backward)
        block = jnp.concatenate([low, block, high], axis=dim)
    return block


def evolve(level_pad, picture, region_means):
    interior = level_pad[:, 1:-1, 1:-1, :]
    side_x = jnp.pad(interior, ((0, 0), (0, 0), (0, 0), (1, 1)))
    laplace = level_pad[:, 2:, 1:-1, :] + level_pad[:, :-2, 1:-1, :]
    laplace = laplace + level_pad[:, 1:-1, 2:, :] + level_pad[:, 1:-1, :-2, :]
    laplace = laplace + side_x[..., 2:] + side_x[..., :-2] - 6.0 * interior
    heaviside = 0.5 + jnp.arctan(interior) / math.pi
    delta_term = 1.0 / (math.pi * (1.0 + interior * interior))
    forces = [jnp.zeros_like(interior[0]) for level_id in range(LEVELS)]
    for phase_id in range(PHASES):
        differ = picture - region_means[phase_id]
        energy = differ * differ
        factors = []
        for level_id in range(LEVELS):
            if phase_id >> level_id & 1:
                factors.append(heaviside[level_id])
            else:
                factors.append(1.0 - heaviside[level_id])
        for level_id in range(LEVELS):
            sign_value = 1.0 if phase_id >> level_id & 1 else -1.0
            others = energy
            for other_id in range(LEVELS):
                if other_id != level_id:
                    others = others * factors[other_id]
            forces[level_id] = forces[level_id] + sign_value * others
    force_all = jnp.stack(forces, axis=0)
    return interior + STEP_SIZE * delta_term * (laplace - force_all)


def minplus_lines(field_in, line_axis, kernel_reach):
    moved_field = jnp.moveaxis(field_in, line_axis, -1)
    line_shape = moved_field.shape
    line_len = line_shape[-1]
    line_rows = moved_field.reshape(-1, line_len)
    row_count = line_rows.shape[0]
    positions = jnp.arange(line_len, dtype=jnp.float32)
    distance = positions[:, None] - positions[None, :]
    penalty_table = jnp.where(
        jnp.abs(distance) <= kernel_reach, PENALTY * (distance * distance), jnp.inf
    )
    row_limit = max(1, 1048576 // (line_len * line_len))
    row_block = 1
    while row_block * 2 <= row_limit and row_count % (row_block * 2) == 0:
        row_block = row_block * 2
    grouped = line_rows.reshape(row_count // row_block, row_block, line_len)

    def block_min(block_rows):
        return jnp.min(block_rows[:, None, :] + penalty_table[None, :, :], axis=2)

    result_rows = lax.map(block_min, grouped)
    return jnp.moveaxis(result_rows.reshape(line_shape), -1, line_axis)


def portable_body(levels, ct_image, region_means):
    current = levels
    for _ in range(UPDATES):
        padded = with_halo(current, (("gz", 1), ("gy", 2)), 1)
        current = evolve(padded, ct_image, region_means)
    field = minplus_lines(current, 3, KERNEL)
    for axis, dim in (("gz", 1), ("gy", 2)):
        lines = lax.all_to_all(field, axis, split_axis=3, concat_axis=dim, tiled=True)
        lines = minplus_lines(lines, dim, KERNEL)
        field = lax.all_to_all(lines, axis, split_axis=dim, concat_axis=3, tiled=True)
    return current, field


def pack_kernel(share, zl, yl, lev_hbm, ct_hbm, out_hbm, lev, ct_ref, up_ref, down_ref, side_ref,
                lines, picture, out_ref, sems):
    width = lev.shape[1]
    parts = width // share
    blocks = width // LANES
    halo, quarter = share + 4, (share + 4) // 4
    chunk = halo + quarter
    arriving = [pltpu.make_async_copy(ct_hbm, ct_ref, sems.at[0])]
    for b in range(blocks):
        cols = pl.ds(b * LANES, LANES)
        arriving.append(pltpu.make_async_copy(lev_hbm.at[:, cols], lev.at[:, cols], sems.at[1 + b]))
    for copy in arriving:
        copy.start()
    lines[pl.ds(0, 8), :] = jnp.zeros((8, LANES), jnp.float32)
    lines[pl.ds(8 + width, 8), :] = jnp.zeros((8, LANES), jnp.float32)
    arriving[0].wait()
    ct = ct_ref[...]
    shifted = [pltpu.roll(ct, (2 - quarter * t) % width, 1) for t in range(4)]
    stacked = jnp.concatenate(shifted, axis=0)
    leaving = []
    for b in range(blocks):
        cols = slice(b * LANES, (b + 1) * LANES)
        picture[pl.ds(b * LANES, LANES), :] = stacked[:, cols].T
    for b in range(blocks):
        cols = slice(b * LANES, (b + 1) * LANES)
        arriving[1 + b].wait()
        lines[pl.ds(8 + b * LANES, LANES), :] = lev[:, cols].T
        first = max(b * LANES // share - 1, 0)
        last = parts if b + 1 == blocks else (b + 1) * LANES // share - 1
        for r in range(first, last):
            out_ref[pl.ds(r * chunk, quarter), :] = picture[pl.ds(r * share, quarter), :]
            out_ref[pl.ds(r * chunk + quarter, halo), :] = lines[pl.ds(6 + r * share, halo), :]
        start = 0 if b == 0 else first * chunk // 8 * 8
        stop = parts * chunk if b + 1 == blocks else last * chunk // 8 * 8
        rows = pl.ds(start, stop - start)
        leaving.append(
            pltpu.make_async_copy(out_ref.at[rows, :], out_hbm.at[rows, :], sems.at[1 + blocks + b])
        )
        leaving[-1].start()
    plane = zl * yl
    for k in range(LEVELS):
        at = pl.ds(2 * k * yl, 2 * yl)
        up_ref[at, :] = lev[pl.ds((k + 1) * plane - 2 * yl, 2 * yl), :]
        down_ref[at, :] = lev[pl.ds(k * plane, 2 * yl), :]
    at = pl.ds(2 * LEVELS * yl, yl)
    up_ref[at, :] = ct_ref[pl.ds(plane - yl, yl), :]
    down_ref[at, :] = ct_ref[pl.ds(0, yl), :]
    upper = lax.axis_index("gy") == 0
    near = jnp.where(upper, yl - 1, 0)
    next_near = jnp.where(upper, yl - 2, 1)
    for k in range(LEVELS):
        for z in range(zl):
            base = k * plane + z * yl
            side_ref[pl.ds(2 * zl * k + z, 1), :] = lev[pl.ds(base + near, 1), :]
            side_ref[pl.ds(2 * zl * k + zl + z, 1), :] = lev[pl.ds(base + next_near, 1), :]
    for z in range(zl):
        side_ref[pl.ds(2 * zl * LEVELS + z, 1), :] = ct_ref[pl.ds(z * yl + near, 1), :]
    for copy in leaving:
        copy.wait()


HALF_ANGLE = (
    0.6366196870803833, -0.21219870448112488, 0.12714172899723053, -0.0893140509724617,
    0.06329755485057831, -0.03813650459051132, 0.015633534640073776, -0.0030433274805545807,
)


def heaviside_and_rate(u):
    s = 1.0 + u * u
    q = lax.rsqrt(s)
    r = u / (1.0 + s * q)
    y = r * r
    p = HALF_ANGLE[-1]
    for c in HALF_ANGLE[-2::-1]:
        p = p * y + c
    return 0.5 + r * p, (q * q) * (STEP_SIZE / math.pi)


def cost_of(d):
    return float(np.float32(PENALTY) * np.float32(d * d))


def middle_kernel(share, gz, gy, zl, yl, mean_ref, in_ref, out_ref,
                  levels, picture, first, turned, zdone, ypen, done, sems):
    parts = gz * gy
    halo, quarter = share + 4, (share + 4) // 4
    chunk = halo + quarter
    stride = halo + (-halo % 8)
    tile = zl * yl
    me = lax.axis_index("gz") * gy + lax.axis_index("gy")

    lane = lax.broadcasted_iota(jnp.int32, (1, LANES), 1)
    level = lane // tile
    z = lane // yl % zl
    y = lane % yl

    def moved(value, index):
        return jnp.take_along_axis(
            value, jnp.broadcast_to(index, value.shape), axis=1, mode="promise_in_bounds"
        )

    def z_turn(turn):
        return lane + ((z + turn) % zl - z) * yl

    def y_turn(turn):
        return lane + (y + turn) % yl - y

    def stacked(blocks):
        return jnp.concatenate(blocks, axis=0)

    for s in range(parts):
        levels[pl.ds(s * stride, halo), :] = in_ref[pl.ds(s * chunk + quarter, halo), :]
        if stride > halo:
            levels[pl.ds(s * stride + halo, stride - halo), :] = jnp.zeros(
                (stride - halo, LANES), jnp.float32
            )
    levels[pl.ds(parts * stride, 8), :] = jnp.zeros((8, LANES), jnp.float32)
    picture[pl.ds(parts * stride, 8), :] = jnp.zeros((8, LANES), jnp.float32)
    first[pl.ds(parts * stride, 8), :] = jnp.zeros((8, LANES), jnp.float32)
    for low in range(0, parts, 4):
        batch = range(low, low + 4)
        packed = stacked([in_ref[pl.ds(s * chunk, 8), :] for s in batch])
        for t in range(4):
            run = moved(packed, t * tile + lane % tile)
            for n, s in enumerate(batch):
                picture[pl.ds(s * stride + t * quarter, quarter), :] = run[8 * n:8 * n + quarter]

    def mean_of(bits, own):
        value = jnp.zeros((1, LANES), jnp.float32)
        for k in range(LEVELS):
            phase = own << k
            for n in range(3):
                phase |= (bits >> n & 1) << ((k + 1 + n) % LEVELS)
            value = jnp.where(level == k, mean_ref[phase], value)
        return value

    slope, const = [], []
    for bits in range(8):
        low, high = mean_of(bits, 0), mean_of(bits, 1)
        slope.append(-2.0 * (high - low))
        const.append((high - low) * (high + low))
    for n in range(3):
        for bits in range(8):
            if bits >> n & 1:
                slope[bits] = slope[bits] - slope[bits ^ (1 << n)]
                const[bits] = const[bits] - const[bits ^ (1 << n)]

    def step(read, batch, pic, rows):
        none = jnp.zeros((rows, LANES), jnp.float32)

        def beside(dz, dy):
            blocks = []
            for s in batch:
                a, b = s // gy + dz, s % gy + dy
                known = 0 <= a < gz and 0 <= b < gy
                blocks.append(read(a * gy + b, 0) if known else none)
            return stacked(blocks)

        here = beside(0, 0)
        h, rate = heaviside_and_rate(here)
        near = stacked([read(s, -1) + read(s, 1) for s in batch]) - 6.0 * here
        near = near + moved(jnp.where(z == 0, beside(1, 0), here), z_turn(1))
        near = near + moved(jnp.where(z == zl - 1, beside(-1, 0), here), z_turn(zl - 1))
        near = near + moved(jnp.where(y == 0, beside(0, 1), here), y_turn(1))
        near = near + moved(jnp.where(y == yl - 1, beside(0, -1), here), y_turn(yl - 1))
        h1 = pltpu.roll(h, LANES - tile, 1)
        h2 = pltpu.roll(h, LANES - 2 * tile, 1)
        h3 = pltpu.roll(h, LANES - 3 * tile, 1)
        f = lambda bits: slope[bits] * pic + const[bits]
        g = lambda bits: f(bits) + h1 * f(bits | 1)
        force = (g(0) + h2 * g(2)) + h3 * (g(4) + h2 * g(6))
        return here + rate * (near - force)

    row = lax.broadcasted_iota(jnp.int32, (stride, LANES), 0)
    wide = share + 2
    inside = jnp.logical_and(
        jnp.logical_or(row > 0, me > 0), jnp.logical_or(row < wide - 1, me < parts - 1)
    )
    for low in range(0, parts, 4):
        batch = range(low, low + 4)
        read = lambda s, dx: levels[pl.ds(s * stride + 1 + dx, stride), :]
        pic = stacked([picture[pl.ds(s * stride + 1, stride), :] for s in batch])
        value = step(read, batch, pic, stride)
        for n, s in enumerate(batch):
            kept = jnp.where(inside, value[n * stride:(n + 1) * stride], 0.0)
            first[pl.ds(s * stride, stride), :] = kept
    for low in range(0, parts, 4):
        batch = range(low, low + 4)
        read = lambda s, dx: first[pl.ds(s * stride + 1 + dx, share), :]
        pic = stacked([picture[pl.ds(s * stride + 2, share), :] for s in batch])
        turned[0, pl.ds(low * share, 4 * share), :] = step(read, batch, pic, share)
    many = 64
    for turn in range(1, zl):
        for at in range(0, parts * share, many):
            rows = pl.ds(at, many)
            turned[turn, rows, :] = moved(turned[0, rows, :], z_turn(turn))

    group = 8
    for b in range(gy):
        for low in range(0, gz, group):
            best = [None] * group
            for other in range(-1, gz):
                for turn in range(zl):
                    value = FAR
                    if other >= 0:
                        value = turned[turn, pl.ds((other * gy + b) * share, share), :]
                    if turn:
                        above = FAR
                        if other + 1 < gz:
                            above = turned[turn, pl.ds(((other + 1) * gy + b) * share, share), :]
                        value = jnp.where(z < zl - turn, value, above)
                    elif other < 0:
                        continue
                    for n in range(group):
                        d = zl * (other - low - n) + turn
                        if abs(d) > KERNEL:
                            continue
                        new = value + cost_of(d)
                        best[n] = new if best[n] is None else jnp.minimum(best[n], new)
            for n in range(group):
                zdone[pl.ds((b * gz + low + n) * share, share), :] = best[n]

    for gap in range(-(gy - 1), gy):
        for turn in range(yl):
            d = (yl * gap + y - (y + turn) % yl).astype(jnp.float32)
            pen = jnp.where(jnp.abs(d) <= KERNEL, PENALTY * (d * d), FAR)
            at = (gap + gy - 1) * yl + turn
            ypen[pl.ds(8 * at, 8), :] = jnp.broadcast_to(pen, (8, LANES))
    pair = 4
    copies = []
    for a in range(0, gz, pair):
        best = [None] * gy
        for other in range(gy):
            whole = zdone[pl.ds((other * gz + a) * share, pair * share), :]
            for turn in range(yl):
                value = moved(whole, y_turn(turn)) if turn else whole
                for b in range(gy):
                    at = (b - other + gy - 1) * yl + turn
                    pen = stacked([ypen[pl.ds(8 * at, 8), :]] * (pair * share // 8))
                    new = value + pen
                    best[b] = new if best[b] is None else jnp.minimum(best[b], new)
        for b in range(gy):
            for n in range(pair):
                block = best[b][n * share:(n + 1) * share]
                done[pl.ds(((a + n) * gy + b) * share, share), :] = block
        rows = pl.ds(a * gy * share, pair * gy * share)
        copies.append(pltpu.make_async_copy(done.at[rows, :], out_ref.at[rows, :], sems.at[a // pair]))
        copies[-1].start()
    for copy in copies:
        copy.wait()


def finish_kernel(in_ref, reg_ref, edge, done, sems):
    width = in_ref.shape[0]
    count = width // 8
    group = 8
    far = jnp.full((8, LANES), FAR, jnp.float32)
    edge[pl.ds(0, 8), :] = far
    edge[pl.ds(8, 8), :] = in_ref[pl.ds(0, 8), :]
    edge[pl.ds(16, 8), :] = in_ref[pl.ds(width - 8, 8), :]
    edge[pl.ds(24, 8), :] = far

    def rows(at):
        if at < 0:
            return edge[pl.ds(8 + at, 8), :]
        if at > width - 8:
            return edge[pl.ds(16 + at - (width - 8), 8), :]
        return in_ref[pl.ds(at, 8), :]

    copies = []
    for c in range(width // LANES):
        for low in range(c * LANES // 8, (c + 1) * LANES // 8, group):
            best = [rows(8 * (low + n)) for n in range(group)]
            for rho in range(1, 9):
                plus, minus = {}, {}
                for e in range((KERNEL - rho) // 8 + 1):
                    cost = cost_of(8 * e + rho)
                    for n in range(group):
                        up, down = low + n + e, low + n - e
                        pair = []
                        if 8 * up + rho < width:
                            if up not in plus:
                                plus[up] = rows(8 * up + rho)
                            pair.append(plus[up])
                        if 8 * down - rho > -8:
                            if down not in minus:
                                minus[down] = rows(8 * down - rho)
                            pair.append(minus[down])
                        if not pair:
                            continue
                        value = pair[0] if len(pair) == 1 else jnp.minimum(pair[0], pair[1])
                        best[n] = jnp.minimum(best[n], value + cost)
            for n in range(group):
                done[pl.ds(8 * (low + n), 8), :] = best[n]
        cols = pl.ds(c * LANES, LANES)
        done[cols, :] = done[cols, :].T
        copies.append(pltpu.make_async_copy(done.at[cols, :], reg_ref.at[:, cols], sems.at[c]))
        copies[-1].start()
    for copy in copies:
        copy.wait()


def corners_kernel(yl, low_ref, high_ref, corner_ref):
    near = jnp.where(lax.axis_index("gy") == 0, yl - 1, 0)
    rows = [low_ref[pl.ds((2 * k + 1) * yl + near, 1), :] for k in range(LEVELS)]
    rows += [high_ref[pl.ds(2 * k * yl + near, 1), :] for k in range(LEVELS)]
    corner_ref[...] = jnp.concatenate(rows, axis=0)


def local_kernel(zl, yl, gz, mean_ref, lev_ref, ct_ref, low_ref, high_ref, side_ref,
                 corner_ref, out_ref, first, strip, around, strip_first):
    width = lev_ref.shape[1]
    at_z = lax.axis_index("gz")
    upper = lax.axis_index("gy") == 0
    edge = jnp.where(upper, yl - 1, 0)
    plane = zl * yl

    const = [mean_ref[p] * mean_ref[p] for p in range(PHASES)]
    slope = [-2.0 * mean_ref[p] for p in range(PHASES)]
    for k in range(LEVELS):
        for p in range(PHASES):
            if p >> k & 1:
                const[p] = const[p] - const[p ^ (1 << k)]
                slope[p] = slope[p] - slope[p ^ (1 << k)]

    def forces(h, pic):
        c = [None] + [slope[p] * pic + const[p] for p in range(1, PHASES)]
        out = []
        for k in range(LEVELS):
            others = [n for n in range(LEVELS) if n != k]
            part = [c[1 << k | sum((bits >> i & 1) << n for i, n in enumerate(others))]
                    for bits in range(8)]
            for n in others:
                part = [part[i] + h[n] * part[i + 1] for i in range(0, len(part), 2)]
            out.append(part[0])
        return out

    column = lax.broadcasted_iota(jnp.int32, (8, width), 1)
    sub = lax.broadcasted_iota(jnp.int32, (8, width), 0)

    def along_x(u):
        left = jnp.where(column == 0, 0.0, pltpu.roll(u, 1, 1))
        right = jnp.where(column == width - 1, 0.0, pltpu.roll(u, width - 1, 1))
        return left + right

    def advance(here, near, pic):
        pairs = [heaviside_and_rate(u) for u in here]
        force = forces([h for h, _ in pairs], pic)
        return [
            u + rate * (n - 6.0 * u - f)
            for u, n, (_, rate), f in zip(here, near, pairs, force)
        ]

    def along_y(u, row):
        row_up = jnp.where(upper, row, 0.0)
        row_down = jnp.where(upper, 0.0, row)
        above = jnp.where(sub == yl - 1, row_up, pltpu.roll(u, yl - 1, 0))
        below = jnp.where(sub == 0, row_down, pltpu.roll(u, 1, 0))
        return above + below

    def level(k, z):
        if z < 0:
            return low_ref[pl.ds((2 * k + 2 + z) * yl, yl), :]
        if z >= zl:
            return high_ref[pl.ds((2 * k + z - zl) * yl, yl), :]
        return lev_ref[pl.ds(k * plane + z * yl, yl), :]

    def side(k, z):
        if z < 0:
            return corner_ref[pl.ds(k, 1), :]
        if z >= zl:
            return corner_ref[pl.ds(LEVELS + k, 1), :]
        return side_ref[pl.ds(2 * zl * k + z, 1), :]

    def picture(z):
        at = pl.ds(2 * LEVELS * yl, yl)
        if z < 0:
            return low_ref[at, :]
        if z >= zl:
            return high_ref[at, :]
        return ct_ref[pl.ds(z * yl, yl), :]

    planes = zl + 2
    for z in range(-1, zl + 1):
        here = [level(k, z) for k in range(LEVELS)]
        near = [
            level(k, z - 1) + level(k, z + 1) + along_x(here[k]) + along_y(here[k], side(k, z))
            for k in range(LEVELS)
        ]
        value = advance(here, near, picture(z))
        for k in range(LEVELS):
            new = value[k]
            if z < 0:
                new = jnp.where(at_z > 0, new, 0.0)
            if z >= zl:
                new = jnp.where(at_z < gz - 1, new, 0.0)
            first[pl.ds((k * planes + z + 1) * yl, yl), :] = new

    strip[...] = jnp.zeros_like(strip)
    around[...] = jnp.zeros_like(around)
    for k in range(LEVELS):
        for z in range(-1, zl + 1):
            strip[pl.ds(8 * k + z + 1, 1), :] = side(k, z)
        for z in range(zl):
            around[pl.ds(8 * k + z + 1, 1), :] = (
                lev_ref[pl.ds(k * plane + z * yl + edge, 1), :]
                + side_ref[pl.ds(2 * zl * k + zl + z, 1), :]
            )
    for z in range(zl):
        strip[pl.ds(8 * LEVELS + z + 1, 1), :] = side_ref[pl.ds(2 * zl * LEVELS + z, 1), :]
    here = [strip[pl.ds(8 * k, 8), :] for k in range(LEVELS)]
    near = [
        pltpu.roll(u, 7, 0) + pltpu.roll(u, 1, 0) + along_x(u) + around[pl.ds(8 * k, 8), :]
        for k, u in enumerate(here)
    ]
    value = advance(here, near, strip[pl.ds(8 * LEVELS, 8), :])
    for k in range(LEVELS):
        strip_first[pl.ds(8 * k, 8), :] = value[k]

    for z in range(zl):
        at = lambda k, dz: first[pl.ds((k * planes + z + 1 + dz) * yl, yl), :]
        here = [at(k, 0) for k in range(LEVELS)]
        near = [
            at(k, -1) + at(k, 1) + along_x(here[k])
            + along_y(here[k], strip_first[pl.ds(8 * k + z + 1, 1), :])
            for k in range(LEVELS)
        ]
        value = advance(here, near, picture(z))
        for k in range(LEVELS):
            out_ref[pl.ds(k * plane + z * yl, yl), :] = value[k]


def split_body(levels, ct_image, region_means):
    gz, gy = lax.axis_size("gz"), lax.axis_size("gy")
    _, zl, yl, width = levels.shape
    parts = gz * gy
    share = width // parts
    halo, quarter = share + 4, (share + 4) // 4
    chunk = halo + quarter
    f32 = jnp.float32
    vmem = pl.BlockSpec(memory_space=pltpu.VMEM)
    smem = pl.BlockSpec(memory_space=pltpu.SMEM)
    anywhere = pl.BlockSpec(memory_space=pl.ANY)
    params = pltpu.CompilerParams(vmem_limit_bytes=24 * 1024 * 1024)
    scratch = lambda *dims: pltpu.VMEM(dims, f32)
    shape = lambda rows: jax.ShapeDtypeStruct((rows, width), f32)
    message = (2 * LEVELS + 1) * yl
    packed, lines, image, up, down, side = pl.pallas_call(
        functools.partial(pack_kernel, share, zl, yl),
        out_shape=(
            jax.ShapeDtypeStruct((parts * chunk, LANES), f32),
            shape(LANES), shape(zl * yl), shape(message), shape(message),
            shape(2 * zl * LEVELS + zl),
        ),
        in_specs=[pl.BlockSpec(memory_space=pltpu.HBM)] * 2,
        out_specs=(anywhere,) + (vmem,) * 5,
        scratch_shapes=[
            scratch(width + 16, LANES),
            scratch(width, LANES),
            scratch(parts * chunk, LANES),
            pltpu.SemaphoreType.DMA((1 + 2 * width // LANES,)),
        ],
        compiler_params=params,
        name="pack",
    )(
        pltpu.with_memory_space_constraint(levels.reshape(LANES, width), pltpu.HBM),
        pltpu.with_memory_space_constraint(ct_image.reshape(zl * yl, width), pltpu.HBM),
    )
    arrived = lax.all_to_all(
        packed.reshape(parts, chunk, 1, LANES), ("gz", "gy"), split_axis=0, concat_axis=0, tiled=True
    ).reshape(parts * chunk, LANES)

    low = lax.ppermute(up, "gz", [(i, i + 1) for i in range(gz - 1)])
    high = lax.ppermute(down, "gz", [(i + 1, i) for i in range(gz - 1)])
    side = lax.ppermute(side, "gy", [(0, 1), (1, 0)])

    stride = halo + (-halo % 8)
    rows = parts * stride + 8
    passed = pl.pallas_call(
        functools.partial(middle_kernel, share, gz, gy, zl, yl),
        out_shape=jax.ShapeDtypeStruct((width, LANES), f32),
        in_specs=[smem, vmem],
        out_specs=anywhere,
        scratch_shapes=[
            scratch(rows, LANES),
            scratch(rows, LANES),
            scratch(rows, LANES),
            scratch(zl, width, LANES),
            scratch(width, LANES),
            scratch(8 * yl * (2 * gy - 1), LANES),
            scratch(width, LANES),
            pltpu.SemaphoreType.DMA((gz // 4,)),
        ],
        compiler_params=params,
        name="middle",
    )(region_means, arrived)
    passed, low, high, side = lax.optimization_barrier((passed, low, high, side))
    passed = lax.all_to_all(
        passed.reshape(parts, share, LANES), ("gz", "gy"), split_axis=0, concat_axis=0, tiled=True
    ).reshape(width, LANES)

    corner = pl.pallas_call(
        functools.partial(corners_kernel, yl),
        out_shape=shape(2 * LEVELS),
        in_specs=[vmem, vmem],
        out_specs=vmem,
        compiler_params=params,
        name="corners",
    )(low, high)
    corner = lax.ppermute(corner, "gy", [(0, 1), (1, 0)])
    evolved = pl.pallas_call(
        functools.partial(local_kernel, zl, yl, gz),
        out_shape=shape(LANES),
        in_specs=[smem] + [vmem] * 6,
        out_specs=vmem,
        scratch_shapes=[
            scratch(LEVELS * (zl + 2) * yl, width),
            scratch(8 * (LEVELS + 1), width),
            scratch(8 * LEVELS, width),
            scratch(8 * LEVELS, width),
        ],
        compiler_params=params,
        cost_estimate=pl.CostEstimate(flops=10_000_000, bytes_accessed=1_000_000, transcendentals=0),
        name="local",
    )(region_means, lines, image, low, high, side, corner)

    regularized = pl.pallas_call(
        finish_kernel,
        out_shape=shape(LANES),
        in_specs=[vmem],
        out_specs=anywhere,
        scratch_shapes=[
            scratch(32, LANES),
            scratch(width, LANES),
            pltpu.SemaphoreType.DMA((width // LANES,)),
        ],
        compiler_params=params,
        name="finish",
    )(passed)
    return evolved.reshape(levels.shape), regularized.reshape(levels.shape)


def body(levels, ct_image, region_means):
    gz, gy = lax.axis_size("gz"), lax.axis_size("gy")
    parts = gz * gy
    count, zl, yl, width = levels.shape
    fits = count == LEVELS and count * zl * yl == LANES and yl == 8 and zl >= 2
    fits = fits and gy == 2 and gz % 8 == 0 and gz * zl <= KERNEL
    fits = fits and width % LANES == 0 and width % parts == 0 and width // parts % 8 == 0
    if fits:
        return split_body(levels, ct_image, region_means)
    return portable_body(levels, ct_image, region_means)


def solution(mesh):
    return jax.shard_map(
        body,
        mesh=mesh,
        in_specs=(P(None, "gz", "gy", None), P("gz", "gy", None), P()),
        out_specs=(P(None, "gz", "gy", None), P(None, "gz", "gy", None)),
        check_vma=False,
    )
```

```python
import functools
import math

import jax
import jax.numpy as jnp
import numpy as np
from jax import lax
from jax.experimental import pallas as pl
from jax.experimental.pallas import tpu as pltpu
from jax.sharding import PartitionSpec as P

LEVELS = 4
PHASES = 16
UPDATES = 2
KERNEL = 200
LANES = 128


PENALTY = 0.0005
STEP_SIZE = 0.5
FAR = 1e30


def with_halo(block, sides, width):
    for axis, dim in sides:
        count = lax.axis_size(axis)
        forward = [(i, i + 1) for i in range(count - 1)]
        backward = [(target, source) for source, target in forward]
        low = lax.ppermute(
            lax.slice_in_dim(block, block.shape[dim] - width, None, axis=dim), axis, forward
        )
        high = lax.ppermute(lax.slice_in_dim(block, 0, width, axis=dim), axis, backward)
        block = jnp.concatenate([low, block, high], axis=dim)
    return block


def evolve(level_pad, picture, region_means):
    interior = level_pad[:, 1:-1, 1:-1, :]
    side_x = jnp.pad(interior, ((0, 0), (0, 0), (0, 0), (1, 1)))
    laplace = level_pad[:, 2:, 1:-1, :] + level_pad[:, :-2, 1:-1, :]
    laplace = laplace + level_pad[:, 1:-1, 2:, :] + level_pad[:, 1:-1, :-2, :]
    laplace = laplace + side_x[..., 2:] + side_x[..., :-2] - 6.0 * interior
    heaviside = 0.5 + jnp.arctan(interior) / math.pi
    delta_term = 1.0 / (math.pi * (1.0 + interior * interior))
    forces = [jnp.zeros_like(interior[0]) for level_id in range(LEVELS)]
    for phase_id in range(PHASES):
        differ = picture - region_means[phase_id]
        energy = differ * differ
        factors = []
        for level_id in range(LEVELS):
            if phase_id >> level_id & 1:
                factors.append(heaviside[level_id])
            else:
                factors.append(1.0 - heaviside[level_id])
        for level_id in range(LEVELS):
            sign_value = 1.0 if phase_id >> level_id & 1 else -1.0
            others = energy
            for other_id in range(LEVELS):
                if other_id != level_id:
                    others = others * factors[other_id]
            forces[level_id] = forces[level_id] + sign_value * others
    force_all = jnp.stack(forces, axis=0)
    return interior + STEP_SIZE * delta_term * (laplace - force_all)


def minplus_lines(field_in, line_axis, kernel_reach):
    moved_field = jnp.moveaxis(field_in, line_axis, -1)
    line_shape = moved_field.shape
    line_len = line_shape[-1]
    line_rows = moved_field.reshape(-1, line_len)
    row_count = line_rows.shape[0]
    positions = jnp.arange(line_len, dtype=jnp.float32)
    distance = positions[:, None] - positions[None, :]
    penalty_table = jnp.where(
        jnp.abs(distance) <= kernel_reach, PENALTY * (distance * distance), jnp.inf
    )
    row_limit = max(1, 1048576 // (line_len * line_len))
    row_block = 1
    while row_block * 2 <= row_limit and row_count % (row_block * 2) == 0:
        row_block = row_block * 2
    grouped = line_rows.reshape(row_count // row_block, row_block, line_len)

    def block_min(block_rows):
        return jnp.min(block_rows[:, None, :] + penalty_table[None, :, :], axis=2)

    result_rows = lax.map(block_min, grouped)
    return jnp.moveaxis(result_rows.reshape(line_shape), -1, line_axis)


def portable_body(levels, ct_image, region_means):
    current = levels
    for _ in range(UPDATES):
        padded = with_halo(current, (("gz", 1), ("gy", 2)), 1)
        current = evolve(padded, ct_image, region_means)
    field = minplus_lines(current, 3, KERNEL)
    for axis, dim in (("gz", 1), ("gy", 2)):
        lines = lax.all_to_all(field, axis, split_axis=3, concat_axis=dim, tiled=True)
        lines = minplus_lines(lines, dim, KERNEL)
        field = lax.all_to_all(lines, axis, split_axis=dim, concat_axis=3, tiled=True)
    return current, field


def pack_kernel(share, zl, yl, lev_hbm, ct_hbm, out_hbm, lev, ct_ref, up_ref, down_ref, side_ref,
                lines, picture, out_ref, sems):
    width = lev.shape[1]
    parts = width // share
    blocks = width // LANES
    halo, quarter = share + 4, (share + 4) // 4
    chunk = halo + quarter
    arriving = [pltpu.make_async_copy(ct_hbm, ct_ref, sems.at[0])]
    for b in range(blocks):
        cols = pl.ds(b * LANES, LANES)
        arriving.append(pltpu.make_async_copy(lev_hbm.at[:, cols], lev.at[:, cols], sems.at[1 + b]))
    for copy in arriving:
        copy.start()
    lines[pl.ds(0, 8), :] = jnp.zeros((8, LANES), jnp.float32)
    lines[pl.ds(8 + width, 8), :] = jnp.zeros((8, LANES), jnp.float32)
    arriving[0].wait()
    ct = ct_ref[...]
    shifted = [pltpu.roll(ct, (2 - quarter * t) % width, 1) for t in range(4)]
    stacked = jnp.concatenate(shifted, axis=0)
    leaving = []
    for b in range(blocks):
        cols = slice(b * LANES, (b + 1) * LANES)
        picture[pl.ds(b * LANES, LANES), :] = stacked[:, cols].T
    sub = lax.broadcasted_iota(jnp.int32, (8, LANES), 0)

    def out_tile(tile):
        value = None
        for r in range(8 * tile // chunk, min((8 * tile + 7) // chunk + 1, parts)):
            for source, begin, length, origin in (
                (picture, r * chunk, quarter, r * share),
                (lines, r * chunk + quarter, halo, 6 + r * share),
            ):
                if begin + length <= 8 * tile or begin >= 8 * tile + 8:
                    continue
                piece = source[pl.ds(8 * tile - begin + origin, 8), :]
                value = piece if value is None else jnp.where(sub >= begin - 8 * tile, piece, value)
        return value

    start = 0
    for b in range(blocks):
        cols = slice(b * LANES, (b + 1) * LANES)
        arriving[1 + b].wait()
        lines[pl.ds(8 + b * LANES, LANES), :] = lev[:, cols].T
        known = parts if b + 1 == blocks else (b + 1) * LANES // share - 1
        stop = known * chunk // 8 * 8
        for tile in range(start // 8, stop // 8):
            out_ref[pl.ds(8 * tile, 8), :] = out_tile(tile)
        rows = pl.ds(start, stop - start)
        leaving.append(
            pltpu.make_async_copy(out_ref.at[rows, :], out_hbm.at[rows, :], sems.at[1 + blocks + b])
        )
        leaving[-1].start()
        start = stop
    plane = zl * yl
    for k in range(LEVELS):
        at = pl.ds(2 * k * yl, 2 * yl)
        up_ref[at, :] = lev[pl.ds((k + 1) * plane - 2 * yl, 2 * yl), :]
        down_ref[at, :] = lev[pl.ds(k * plane, 2 * yl), :]
    at = pl.ds(2 * LEVELS * yl, yl)
    up_ref[at, :] = ct_ref[pl.ds(plane - yl, yl), :]
    down_ref[at, :] = ct_ref[pl.ds(0, yl), :]
    upper = lax.axis_index("gy") == 0
    near = jnp.where(upper, yl - 1, 0)
    next_near = jnp.where(upper, yl - 2, 1)
    for k in range(LEVELS):
        for z in range(zl):
            base = k * plane + z * yl
            side_ref[pl.ds(2 * zl * k + z, 1), :] = lev[pl.ds(base + near, 1), :]
            side_ref[pl.ds(2 * zl * k + zl + z, 1), :] = lev[pl.ds(base + next_near, 1), :]
    for z in range(zl):
        side_ref[pl.ds(2 * zl * LEVELS + z, 1), :] = ct_ref[pl.ds(z * yl + near, 1), :]
    for copy in leaving:
        copy.wait()


HALF_ANGLE = (
    0.6366196870803833, -0.21219870448112488, 0.12714172899723053, -0.0893140509724617,
    0.06329755485057831, -0.03813650459051132, 0.015633534640073776, -0.0030433274805545807,
)


def heaviside_and_rate(u):
    s = 1.0 + u * u
    q = lax.rsqrt(s)
    r = u / (1.0 + s * q)
    y = r * r
    p = HALF_ANGLE[-1]
    for c in HALF_ANGLE[-2::-1]:
        p = p * y + c
    return 0.5 + r * p, (q * q) * (STEP_SIZE / math.pi)


def cost_of(d):
    return float(np.float32(PENALTY) * np.float32(d * d))


SLOT = 32


def middle_kernel(share, gz, gy, zl, yl, mean_ref, in_ref, out_ref, levels, picture, first,
                  evolved, shifted, zdone, ypen, done, sems):
    parts = gz * gy
    halo, quarter = share + 4, (share + 4) // 4
    chunk = halo + quarter
    tile = zl * yl
    deep = gz + 2
    me = lax.axis_index("gy") * gz + lax.axis_index("gz")

    lane = lax.broadcasted_iota(jnp.int32, (1, LANES), 1)
    level = lane // tile
    z = lane // yl % zl
    y = lane % yl

    def moved(value, index):
        return jnp.take_along_axis(
            value, jnp.broadcast_to(index, value.shape), axis=1, mode="promise_in_bounds"
        )

    def z_turn(turn):
        return lane + ((z + turn) % zl - z) * yl

    def y_turn(turn):
        return lane + (y + turn) % yl - y

    def stacked(blocks):
        return jnp.concatenate(blocks, axis=0)

    def row_of(a, b, x):
        return (b * deep + a + 1) * SLOT + 8 + x

    zero = jnp.zeros((SLOT, LANES), jnp.float32)
    for b in range(gy):
        for a in (-1, gz):
            levels[pl.ds(row_of(a, b, -8), SLOT), :] = zero
            first[pl.ds(row_of(a, b, -8), SLOT), :] = zero
        for a in range(gz):
            source = (b * gz + a) * chunk + quarter
            levels[pl.ds(row_of(a, b, -2), halo), :] = in_ref[pl.ds(source, halo), :]
        for a in range(0, gz, 4):
            batch = range(a, a + 4)
            packed = stacked([in_ref[pl.ds((b * gz + n) * chunk, 8), :] for n in batch])
            for t in range(4):
                run = moved(packed, t * tile + lane % tile)
                for n in batch:
                    at = 8 * (n - a)
                    rows = pl.ds(row_of(n, b, t * quarter - 2), quarter)
                    picture[rows, :] = run[at:at + quarter]

    def mean_of(bits, own):
        value = jnp.zeros((1, LANES), jnp.float32)
        for k in range(LEVELS):
            phase = own << k
            for n in range(3):
                phase |= (bits >> n & 1) << ((k + 1 + n) % LEVELS)
            value = jnp.where(level == k, mean_ref[phase], value)
        return value

    slope, const = [], []
    for bits in range(8):
        low, high = mean_of(bits, 0), mean_of(bits, 1)
        slope.append(-2.0 * (high - low))
        const.append((high - low) * (high + low))
    for n in range(3):
        for bits in range(8):
            if bits >> n & 1:
                slope[bits] = slope[bits] - slope[bits ^ (1 << n)]
                const[bits] = const[bits] - const[bits ^ (1 << n)]

    def step(read, tiles, pic):
        def beside(dz, dy):
            none = jnp.zeros_like(read(0, 0, 0))
            return stacked([
                read(a + dz, b + dy, 0) if 0 <= b + dy < gy else none for a, b in tiles
            ])

        here = beside(0, 0)
        h, rate = heaviside_and_rate(here)
        near = stacked([read(a, b, -1) + read(a, b, 1) for a, b in tiles]) - 6.0 * here
        near = near + moved(jnp.where(z == 0, beside(1, 0), here), z_turn(1))
        near = near + moved(jnp.where(z == zl - 1, beside(-1, 0), here), z_turn(zl - 1))
        near = near + moved(jnp.where(y == 0, beside(0, 1), here), y_turn(1))
        near = near + moved(jnp.where(y == yl - 1, beside(0, -1), here), y_turn(yl - 1))
        h1 = pltpu.roll(h, LANES - tile, 1)
        h2 = pltpu.roll(h, LANES - 2 * tile, 1)
        h3 = pltpu.roll(h, LANES - 3 * tile, 1)
        f = lambda bits: slope[bits] * pic + const[bits]
        g = lambda bits: f(bits) + h1 * f(bits | 1)
        force = (g(0) + h2 * g(2)) + h3 * (g(4) + h2 * g(6))
        return here + rate * (near - force)

    def run_of(ref):
        return lambda a, b, dx: ref[pl.ds(row_of(a, b, dx), share), :]

    for x, outside in ((-1, me == 0), (share, me == parts - 1)):
        across = lambda ref, a, b, dx: ref[pl.ds(row_of(a, b, x + dx), gz, stride=SLOT), :]
        rows = [(0, b) for b in range(gy)]
        pic = stacked([across(picture, 0, b, 0) for _, b in rows])
        value = step(lambda a, b, dx: across(levels, a, b, dx), rows, pic)
        value = jnp.where(outside, 0.0, value)
        for b in range(gy):
            first[pl.ds(row_of(0, b, x), gz, stride=SLOT), :] = value[b * gz:(b + 1) * gz]
    batches = [[(a + n, b) for n in range(4)] for b in range(gy) for a in range(0, gz, 4)]
    for tiles in batches:
        pic = stacked([run_of(picture)(a, b, 0) for a, b in tiles])
        value = step(run_of(levels), tiles, pic)
        for n, (a, b) in enumerate(tiles):
            first[pl.ds(row_of(a, b, 0), share), :] = value[n * share:(n + 1) * share]

    def block_of(a, b):
        return (b * deep + a + 1) * share

    far = jnp.full((share, LANES), FAR, jnp.float32)
    for b in range(gy):
        for a in (-1, gz):
            evolved[pl.ds(block_of(a, b), share), :] = far
    for tiles in batches:
        pic = stacked([run_of(picture)(a, b, 0) for a, b in tiles])
        evolved[pl.ds(block_of(*tiles[0]), 4 * share), :] = step(run_of(first), tiles, pic)

    for b in range(gy):
        for a in range(-1, gz, 4):
            count = min(4, gz - a) * share
            here = evolved[pl.ds(block_of(a, b), count), :]
            above = evolved[pl.ds(block_of(a + 1, b), count), :]
            for turn in range(1, zl):
                value = moved(jnp.where(z < turn, above, here), z_turn(turn))
                shifted[turn - 1, pl.ds(block_of(a, b), count), :] = value

    def z_unit(half, b, low):
        count = 8

        def at(d, n):
            a, turn = low + n + d // zl, d % zl
            if a < (-1 if turn else 0) or a >= gz:
                return None
            if (a, turn) not in loaded:
                rows = pl.ds(block_of(a, b) + 8 * half, 8)
                loaded[a, turn] = shifted[turn - 1, rows, :] if turn else evolved[rows, :]
            return loaded[a, turn]

        loaded = {}
        best = [at(0, n) for n in range(count)]
        for turn in range(zl):
            loaded = {}
            for d in range(turn or zl, min(gz * zl, KERNEL + 1), zl):
                for n in range(count):
                    pair = [v for v in (at(d, n), at(-d, n)) if v is not None]
                    if pair:
                        value = pair[0] if len(pair) == 1 else jnp.minimum(pair[0], pair[1])
                        best[n] = jnp.minimum(best[n], value + cost_of(d))
        for n in range(count):
            zdone[pl.ds((b * gz + low + n) * share + 8 * half, 8), :] = best[n]

    for gap in range(-(gy - 1), gy):
        for turn in range(yl):
            d = (yl * gap + y - (y + turn) % yl).astype(jnp.float32)
            pen = jnp.where(jnp.abs(d) <= KERNEL, PENALTY * (d * d), FAR)
            ypen[pl.ds(8 * ((gap + gy - 1) * yl + turn), 8), :] = jnp.broadcast_to(pen, (8, LANES))

    def y_unit(half, low):
        count = 4
        best = [None] * gy
        for other in range(gy):
            starts = [(other * gz + low + n) * share + 8 * half for n in range(count)]
            whole = stacked([zdone[pl.ds(at, 8), :] for at in starts])
            for turn in range(yl):
                value = moved(whole, y_turn(turn)) if turn else whole
                for b in range(gy):
                    at = (b - other + gy - 1) * yl + turn
                    new = value + stacked([ypen[pl.ds(8 * at, 8), :]] * count)
                    best[b] = new if best[b] is None else jnp.minimum(best[b], new)
        for b in range(gy):
            for n in range(count):
                rows = pl.ds((b * gz + low + n) * share + 8 * half, 8)
                done[rows, :] = best[b][8 * n:8 * n + 8]

    halves = share // 8
    copies = []
    for half in range(halves + 1):
        z_units = [(b, low) for b in range(gy) for low in range(0, gz, 8)] if half < halves else []
        y_units = list(range(0, gz, 4)) if half else []
        for n in range(max(len(z_units), len(y_units))):
            if n < len(z_units):
                z_unit(half, *z_units[n])
            if n < len(y_units):
                y_unit(half - 1, y_units[n])
                if half == halves:
                    for b in range(gy):
                        rows = pl.ds((b * gz + y_units[n]) * share, 4 * share)
                        sem = sems.at[len(copies)]
                        copies.append(pltpu.make_async_copy(done.at[rows, :], out_ref.at[rows, :], sem))
                        copies[-1].start()
    for copy in copies:
        copy.wait()


def finish_kernel(in_ref, reg_ref, edge, done, sems):
    width = in_ref.shape[0]
    count = width // 8
    group = 8
    far = jnp.full((8, LANES), FAR, jnp.float32)
    edge[pl.ds(0, 8), :] = far
    edge[pl.ds(8, 8), :] = in_ref[pl.ds(0, 8), :]
    edge[pl.ds(16, 8), :] = in_ref[pl.ds(width - 8, 8), :]
    edge[pl.ds(24, 8), :] = far

    def rows(at):
        if at < 0:
            return edge[pl.ds(8 + at, 8), :]
        if at > width - 8:
            return edge[pl.ds(16 + at - (width - 8), 8), :]
        return in_ref[pl.ds(at, 8), :]

    copies = []
    for c in range(width // LANES):
        for low in range(c * LANES // 8, (c + 1) * LANES // 8, group):
            best = [rows(8 * (low + n)) for n in range(group)]
            for rho in range(1, 9):
                plus, minus = {}, {}
                for e in range((KERNEL - rho) // 8 + 1):
                    cost = cost_of(8 * e + rho)
                    for n in range(group):
                        up, down = low + n + e, low + n - e
                        pair = []
                        if 8 * up + rho < width:
                            if up not in plus:
                                plus[up] = rows(8 * up + rho)
                            pair.append(plus[up])
                        if 8 * down - rho > -8:
                            if down not in minus:
                                minus[down] = rows(8 * down - rho)
                            pair.append(minus[down])
                        if not pair:
                            continue
                        value = pair[0] if len(pair) == 1 else jnp.minimum(pair[0], pair[1])
                        best[n] = jnp.minimum(best[n], value + cost)
            for n in range(group):
                done[pl.ds(8 * (low + n), 8), :] = best[n]
        cols = pl.ds(c * LANES, LANES)
        done[cols, :] = done[cols, :].T
        copies.append(pltpu.make_async_copy(done.at[cols, :], reg_ref.at[:, cols], sems.at[c]))
        copies[-1].start()
    for copy in copies:
        copy.wait()


def corners_kernel(yl, low_ref, high_ref, corner_ref):
    near = jnp.where(lax.axis_index("gy") == 0, yl - 1, 0)
    rows = [low_ref[pl.ds((2 * k + 1) * yl + near, 1), :] for k in range(LEVELS)]
    rows += [high_ref[pl.ds(2 * k * yl + near, 1), :] for k in range(LEVELS)]
    corner_ref[...] = jnp.concatenate(rows, axis=0)


def tile_tools(mean_ref, yl, width):
    upper = lax.axis_index("gy") == 0

    const = [mean_ref[p] * mean_ref[p] for p in range(PHASES)]
    slope = [-2.0 * mean_ref[p] for p in range(PHASES)]
    for k in range(LEVELS):
        for p in range(PHASES):
            if p >> k & 1:
                const[p] = const[p] - const[p ^ (1 << k)]
                slope[p] = slope[p] - slope[p ^ (1 << k)]

    def forces(h, pic):
        c = [None] + [slope[p] * pic + const[p] for p in range(1, PHASES)]
        out = []
        for k in range(LEVELS):
            others = [n for n in range(LEVELS) if n != k]
            part = [c[1 << k | sum((bits >> i & 1) << n for i, n in enumerate(others))]
                    for bits in range(8)]
            for n in others:
                part = [part[i] + h[n] * part[i + 1] for i in range(0, len(part), 2)]
            out.append(part[0])
        return out

    column = lax.broadcasted_iota(jnp.int32, (8, width), 1)
    sub = lax.broadcasted_iota(jnp.int32, (8, width), 0)

    def along_x(u):
        left = jnp.where(column == 0, 0.0, pltpu.roll(u, 1, 1))
        right = jnp.where(column == width - 1, 0.0, pltpu.roll(u, width - 1, 1))
        return left + right

    def advance(here, near, pic):
        pairs = [heaviside_and_rate(u) for u in here]
        force = forces([h for h, _ in pairs], pic)
        return [
            u + rate * (n - 6.0 * u - f)
            for u, n, (_, rate), f in zip(here, near, pairs, force)
        ]

    def along_y(u, row):
        row_up = jnp.where(upper, row, 0.0)
        row_down = jnp.where(upper, 0.0, row)
        above = jnp.where(sub == yl - 1, row_up, pltpu.roll(u, yl - 1, 0))
        below = jnp.where(sub == 0, row_down, pltpu.roll(u, 1, 0))
        return above + below

    return advance, along_x, along_y


def add_neighbours(lev_ref, low_ref, high_ref, zl, yl):
    def level(k, z):
        if z < 0:
            return low_ref[pl.ds((2 * k + 2 + z) * yl, yl), :]
        if z >= zl:
            return high_ref[pl.ds((2 * k + z - zl) * yl, yl), :]
        return lev_ref[pl.ds((k * zl + z) * yl, yl), :]

    return level


def inner_kernel(zl, yl, mean_ref, lev_ref, ct_ref, low_ref, high_ref, side_ref, out_ref):
    advance, along_x, along_y = tile_tools(mean_ref, yl, lev_ref.shape[1])
    level = add_neighbours(lev_ref, low_ref, high_ref, zl, yl)
    for z in range(zl):
        here = [level(k, z) for k in range(LEVELS)]
        near = [
            level(k, z - 1) + level(k, z + 1) + along_x(here[k])
            + along_y(here[k], side_ref[pl.ds(2 * zl * k + z, 1), :])
            for k in range(LEVELS)
        ]
        value = advance(here, near, ct_ref[pl.ds(z * yl, yl), :])
        for k in range(LEVELS):
            out_ref[pl.ds((k * zl + z) * yl, yl), :] = value[k]


def outer_kernel(zl, yl, gz, mean_ref, lev_ref, ct_ref, low_ref, high_ref, side_ref,
                 corner_ref, inner_ref, out_ref, outer, strip, around, strip_first):
    at_z = lax.axis_index("gz")
    edge = jnp.where(lax.axis_index("gy") == 0, yl - 1, 0)
    plane = zl * yl
    advance, along_x, along_y = tile_tools(mean_ref, yl, lev_ref.shape[1])
    level = add_neighbours(lev_ref, low_ref, high_ref, zl, yl)

    def side(k, z):
        if z < 0:
            return corner_ref[pl.ds(k, 1), :]
        if z >= zl:
            return corner_ref[pl.ds(LEVELS + k, 1), :]
        return side_ref[pl.ds(2 * zl * k + z, 1), :]

    picture_at = pl.ds(2 * LEVELS * yl, yl)
    for n, (z, kept, pic) in enumerate((
        (-1, at_z > 0, low_ref[picture_at, :]), (zl, at_z < gz - 1, high_ref[picture_at, :])
    )):
        here = [level(k, z) for k in range(LEVELS)]
        near = [
            level(k, z - 1) + level(k, z + 1) + along_x(here[k]) + along_y(here[k], side(k, z))
            for k in range(LEVELS)
        ]
        value = advance(here, near, pic)
        for k in range(LEVELS):
            outer[pl.ds((2 * k + n) * yl, yl), :] = jnp.where(kept, value[k], 0.0)

    strip[...] = jnp.zeros_like(strip)
    around[...] = jnp.zeros_like(around)
    for k in range(LEVELS):
        for z in range(-1, zl + 1):
            strip[pl.ds(8 * k + z + 1, 1), :] = side(k, z)
        for z in range(zl):
            around[pl.ds(8 * k + z + 1, 1), :] = (
                lev_ref[pl.ds(k * plane + z * yl + edge, 1), :]
                + side_ref[pl.ds(2 * zl * k + zl + z, 1), :]
            )
    for z in range(zl):
        strip[pl.ds(8 * LEVELS + z + 1, 1), :] = side_ref[pl.ds(2 * zl * LEVELS + z, 1), :]
    here = [strip[pl.ds(8 * k, 8), :] for k in range(LEVELS)]
    near = [
        pltpu.roll(u, 7, 0) + pltpu.roll(u, 1, 0) + along_x(u) + around[pl.ds(8 * k, 8), :]
        for k, u in enumerate(here)
    ]
    value = advance(here, near, strip[pl.ds(8 * LEVELS, 8), :])
    for k in range(LEVELS):
        strip_first[pl.ds(8 * k, 8), :] = value[k]

    def after(k, z):
        if z < 0 or z >= zl:
            return outer[pl.ds((2 * k + (z >= zl)) * yl, yl), :]
        return inner_ref[pl.ds((k * zl + z) * yl, yl), :]

    for z in range(zl):
        here = [after(k, z) for k in range(LEVELS)]
        near = [
            after(k, z - 1) + after(k, z + 1) + along_x(here[k])
            + along_y(here[k], strip_first[pl.ds(8 * k + z + 1, 1), :])
            for k in range(LEVELS)
        ]
        value = advance(here, near, ct_ref[pl.ds(z * yl, yl), :])
        for k in range(LEVELS):
            out_ref[pl.ds(k * plane + z * yl, yl), :] = value[k]


def split_body(levels, ct_image, region_means):
    gz, gy = lax.axis_size("gz"), lax.axis_size("gy")
    _, zl, yl, width = levels.shape
    parts = gz * gy
    share = width // parts
    halo, quarter = share + 4, (share + 4) // 4
    chunk = halo + quarter
    f32 = jnp.float32
    vmem = pl.BlockSpec(memory_space=pltpu.VMEM)
    smem = pl.BlockSpec(memory_space=pltpu.SMEM)
    anywhere = pl.BlockSpec(memory_space=pl.ANY)
    params = pltpu.CompilerParams(vmem_limit_bytes=24 * 1024 * 1024)
    scratch = lambda *dims: pltpu.VMEM(dims, f32)
    shape = lambda rows: jax.ShapeDtypeStruct((rows, width), f32)
    message = (2 * LEVELS + 1) * yl
    packed, lines, image, up, down, side = pl.pallas_call(
        functools.partial(pack_kernel, share, zl, yl),
        out_shape=(
            jax.ShapeDtypeStruct((parts * chunk, LANES), f32),
            shape(LANES), shape(zl * yl), shape(message), shape(message),
            shape(2 * zl * LEVELS + zl),
        ),
        in_specs=[pl.BlockSpec(memory_space=pltpu.HBM)] * 2,
        out_specs=(anywhere,) + (vmem,) * 5,
        scratch_shapes=[
            scratch(width + 16, LANES),
            scratch(width, LANES),
            scratch(parts * chunk, LANES),
            pltpu.SemaphoreType.DMA((1 + 2 * width // LANES,)),
        ],
        compiler_params=params,
        name="pack",
    )(
        pltpu.with_memory_space_constraint(levels.reshape(LANES, width), pltpu.HBM),
        pltpu.with_memory_space_constraint(ct_image.reshape(zl * yl, width), pltpu.HBM),
    )
    arrived = lax.all_to_all(
        packed.reshape(parts, chunk, 1, LANES), ("gy", "gz"), split_axis=0, concat_axis=0, tiled=True
    ).reshape(parts * chunk, LANES)

    low = lax.ppermute(up, "gz", [(i, i + 1) for i in range(gz - 1)])
    high = lax.ppermute(down, "gz", [(i + 1, i) for i in range(gz - 1)])
    side = lax.ppermute(side, "gy", [(0, 1), (1, 0)])

    slots = gy * (gz + 2) * SLOT
    blocks = gy * (gz + 2) * share
    passed = pl.pallas_call(
        functools.partial(middle_kernel, share, gz, gy, zl, yl),
        out_shape=jax.ShapeDtypeStruct((width, LANES), f32),
        in_specs=[smem, vmem],
        out_specs=anywhere,
        scratch_shapes=[
            scratch(slots, LANES),
            scratch(slots, LANES),
            scratch(slots, LANES),
            scratch(blocks, LANES),
            scratch(zl - 1, blocks, LANES),
            scratch(width, LANES),
            scratch(8 * yl * (2 * gy - 1), LANES),
            scratch(width, LANES),
            pltpu.SemaphoreType.DMA((gy * gz // 4,)),
        ],
        compiler_params=params,
        name="middle",
    )(region_means, arrived)
    passed, low, high, side = lax.optimization_barrier((passed, low, high, side))
    passed = lax.all_to_all(
        passed.reshape(parts, share, LANES), ("gy", "gz"), split_axis=0, concat_axis=0, tiled=True
    ).reshape(width, LANES)

    corner = pl.pallas_call(
        functools.partial(corners_kernel, yl),
        out_shape=shape(2 * LEVELS),
        in_specs=[vmem, vmem],
        out_specs=vmem,
        compiler_params=params,
        name="corners",
    )(low, high)
    corner = lax.ppermute(corner, "gy", [(0, 1), (1, 0)])
    cost = pl.CostEstimate(flops=5_000_000, bytes_accessed=1_000_000, transcendentals=0)
    inner = pl.pallas_call(
        functools.partial(inner_kernel, zl, yl),
        out_shape=shape(LANES),
        in_specs=[smem] + [vmem] * 5,
        out_specs=vmem,
        compiler_params=params,
        cost_estimate=cost,
        name="inner",
    )(region_means, lines, image, low, high, side)
    evolved = pl.pallas_call(
        functools.partial(outer_kernel, zl, yl, gz),
        out_shape=shape(LANES),
        in_specs=[smem] + [vmem] * 7,
        out_specs=vmem,
        scratch_shapes=[
            scratch(2 * LEVELS * yl, width),
            scratch(8 * (LEVELS + 1), width),
            scratch(8 * LEVELS, width),
            scratch(8 * LEVELS, width),
        ],
        compiler_params=params,
        cost_estimate=cost,
        name="outer",
    )(region_means, lines, image, low, high, side, corner, inner)

    regularized = pl.pallas_call(
        finish_kernel,
        out_shape=shape(LANES),
        in_specs=[vmem],
        out_specs=anywhere,
        scratch_shapes=[
            scratch(32, LANES),
            scratch(width, LANES),
            pltpu.SemaphoreType.DMA((width // LANES,)),
        ],
        compiler_params=params,
        name="finish",
    )(passed)
    return evolved.reshape(levels.shape), regularized.reshape(levels.shape)


def body(levels, ct_image, region_means):
    gz, gy = lax.axis_size("gz"), lax.axis_size("gy")
    parts = gz * gy
    count, zl, yl, width = levels.shape
    fits = count == LEVELS and count * zl * yl == LANES and yl == 8 and zl >= 2
    fits = fits and gy == 2 and gz % 8 == 0 and gz * zl <= KERNEL
    fits = fits and width % LANES == 0 and width % parts == 0 and width // parts % 8 == 0
    if fits:
        return split_body(levels, ct_image, region_means)
    return portable_body(levels, ct_image, region_means)


def solution(mesh):
    return jax.shard_map(
        body,
        mesh=mesh,
        in_specs=(P(None, "gz", "gy", None), P("gz", "gy", None), P()),
        out_specs=(P(None, "gz", "gy", None), P(None, "gz", "gy", None)),
        check_vma=False,
    )
```

```python
import functools
import math

import jax
import jax.numpy as jnp
import numpy as np
from jax import lax
from jax.experimental import pallas as pl
from jax.experimental.pallas import tpu as pltpu
from jax.sharding import PartitionSpec as P

LEVELS = 4
PHASES = 16
UPDATES = 2
KERNEL = 200
LANES = 128


PENALTY = 0.0005
STEP_SIZE = 0.5
FAR = 1e30


def with_halo(block, sides, width):
    for axis, dim in sides:
        count = lax.axis_size(axis)
        forward = [(i, i + 1) for i in range(count - 1)]
        backward = [(target, source) for source, target in forward]
        low = lax.ppermute(
            lax.slice_in_dim(block, block.shape[dim] - width, None, axis=dim), axis, forward
        )
        high = lax.ppermute(lax.slice_in_dim(block, 0, width, axis=dim), axis, backward)
        block = jnp.concatenate([low, block, high], axis=dim)
    return block


def evolve(level_pad, picture, region_means):
    interior = level_pad[:, 1:-1, 1:-1, :]
    side_x = jnp.pad(interior, ((0, 0), (0, 0), (0, 0), (1, 1)))
    laplace = level_pad[:, 2:, 1:-1, :] + level_pad[:, :-2, 1:-1, :]
    laplace = laplace + level_pad[:, 1:-1, 2:, :] + level_pad[:, 1:-1, :-2, :]
    laplace = laplace + side_x[..., 2:] + side_x[..., :-2] - 6.0 * interior
    heaviside = 0.5 + jnp.arctan(interior) / math.pi
    delta_term = 1.0 / (math.pi * (1.0 + interior * interior))
    forces = [jnp.zeros_like(interior[0]) for level_id in range(LEVELS)]
    for phase_id in range(PHASES):
        differ = picture - region_means[phase_id]
        energy = differ * differ
        factors = []
        for level_id in range(LEVELS):
            if phase_id >> level_id & 1:
                factors.append(heaviside[level_id])
            else:
                factors.append(1.0 - heaviside[level_id])
        for level_id in range(LEVELS):
            sign_value = 1.0 if phase_id >> level_id & 1 else -1.0
            others = energy
            for other_id in range(LEVELS):
                if other_id != level_id:
                    others = others * factors[other_id]
            forces[level_id] = forces[level_id] + sign_value * others
    force_all = jnp.stack(forces, axis=0)
    return interior + STEP_SIZE * delta_term * (laplace - force_all)


def minplus_lines(field_in, line_axis, kernel_reach):
    moved_field = jnp.moveaxis(field_in, line_axis, -1)
    line_shape = moved_field.shape
    line_len = line_shape[-1]
    line_rows = moved_field.reshape(-1, line_len)
    row_count = line_rows.shape[0]
    positions = jnp.arange(line_len, dtype=jnp.float32)
    distance = positions[:, None] - positions[None, :]
    penalty_table = jnp.where(
        jnp.abs(distance) <= kernel_reach, PENALTY * (distance * distance), jnp.inf
    )
    row_limit = max(1, 1048576 // (line_len * line_len))
    row_block = 1
    while row_block * 2 <= row_limit and row_count % (row_block * 2) == 0:
        row_block = row_block * 2
    grouped = line_rows.reshape(row_count // row_block, row_block, line_len)

    def block_min(block_rows):
        return jnp.min(block_rows[:, None, :] + penalty_table[None, :, :], axis=2)

    result_rows = lax.map(block_min, grouped)
    return jnp.moveaxis(result_rows.reshape(line_shape), -1, line_axis)


def portable_body(levels, ct_image, region_means):
    current = levels
    for _ in range(UPDATES):
        padded = with_halo(current, (("gz", 1), ("gy", 2)), 1)
        current = evolve(padded, ct_image, region_means)
    field = minplus_lines(current, 3, KERNEL)
    for axis, dim in (("gz", 1), ("gy", 2)):
        lines = lax.all_to_all(field, axis, split_axis=3, concat_axis=dim, tiled=True)
        lines = minplus_lines(lines, dim, KERNEL)
        field = lax.all_to_all(lines, axis, split_axis=dim, concat_axis=3, tiled=True)
    return current, field


def pack_kernel(share, zl, yl, lev_hbm, ct_hbm, out_hbm, lev, ct_ref, up_ref, down_ref, side_ref,
                lines, picture, stage, out_ref, sems):
    width = lev.shape[1]
    parts = width // share
    blocks = width // LANES
    halo, quarter = share + 4, (share + 4) // 4
    chunk = halo + quarter
    arriving = [pltpu.make_async_copy(ct_hbm, ct_ref, sems.at[0])]
    for b in range(blocks):
        cols = pl.ds(b * LANES, LANES)
        arriving.append(pltpu.make_async_copy(lev_hbm.at[:, cols], lev.at[:, cols], sems.at[1 + b]))
    for copy in arriving:
        copy.start()
    lines[pl.ds(0, 8), :] = jnp.zeros((8, LANES), jnp.float32)
    lines[pl.ds(8 + width, 8), :] = jnp.zeros((8, LANES), jnp.float32)
    arriving[0].wait()
    ct = ct_ref[...]
    shifted = [pltpu.roll(ct, (2 - quarter * t) % width, 1) for t in range(4)]
    stacked = jnp.concatenate(shifted, axis=0)
    leaving = []
    for b in range(blocks):
        cols = slice(b * LANES, (b + 1) * LANES)
        picture[pl.ds(b * LANES, LANES), :] = stacked[:, cols].T
    sub = lax.broadcasted_iota(jnp.int32, (8, LANES), 0)

    def out_tile(tile):
        value = None
        for r in range(8 * tile // chunk, min((8 * tile + 7) // chunk + 1, parts)):
            for source, begin, length, origin in (
                (picture, r * chunk, quarter, r * share),
                (lines, r * chunk + quarter, halo, 6 + r * share),
            ):
                if begin + length <= 8 * tile or begin >= 8 * tile + 8:
                    continue
                piece = source[pl.ds(8 * tile - begin + origin, 8), :]
                value = piece if value is None else jnp.where(sub >= begin - 8 * tile, piece, value)
        return value

    start = 0
    for b in range(blocks):
        cols = slice(b * LANES, (b + 1) * LANES)
        arriving[1 + b].wait()
        stage[pl.ds(b * LANES, LANES), :] = lev[:, cols]
        count = LEVELS * zl
        block = [stage[pl.ds(b * LANES + y, count, stride=yl), :] for y in range(yl)]
        lines[pl.ds(8 + b * LANES, LANES), :] = jnp.concatenate(block, axis=0).T
        known = parts if b + 1 == blocks else (b + 1) * LANES // share - 1
        stop = known * chunk // 8 * 8
        for tile in range(start // 8, stop // 8):
            out_ref[pl.ds(8 * tile, 8), :] = out_tile(tile)
        rows = pl.ds(start, stop - start)
        leaving.append(
            pltpu.make_async_copy(out_ref.at[rows, :], out_hbm.at[rows, :], sems.at[1 + blocks + b])
        )
        leaving[-1].start()
        start = stop
    plane = zl * yl
    for k in range(LEVELS):
        at = pl.ds(2 * k * yl, 2 * yl)
        up_ref[at, :] = lev[pl.ds((k + 1) * plane - 2 * yl, 2 * yl), :]
        down_ref[at, :] = lev[pl.ds(k * plane, 2 * yl), :]
    at = pl.ds(2 * LEVELS * yl, yl)
    up_ref[at, :] = ct_ref[pl.ds(plane - yl, yl), :]
    down_ref[at, :] = ct_ref[pl.ds(0, yl), :]
    upper = lax.axis_index("gy") == 0
    near = jnp.where(upper, yl - 1, 0)
    next_near = jnp.where(upper, yl - 2, 1)
    for k in range(LEVELS):
        for z in range(zl):
            base = k * plane + z * yl
            side_ref[pl.ds(2 * zl * k + z, 1), :] = lev[pl.ds(base + near, 1), :]
            side_ref[pl.ds(2 * zl * k + zl + z, 1), :] = lev[pl.ds(base + next_near, 1), :]
    for z in range(zl):
        side_ref[pl.ds(2 * zl * LEVELS + z, 1), :] = ct_ref[pl.ds(z * yl + near, 1), :]
    for copy in leaving:
        copy.wait()


HALF_ANGLE = (
    0.6366196870803833, -0.21219870448112488, 0.12714172899723053, -0.0893140509724617,
    0.06329755485057831, -0.03813650459051132, 0.015633534640073776, -0.0030433274805545807,
)


def heaviside_and_rate(u):
    s = 1.0 + u * u
    q = lax.rsqrt(s)
    r = u / (1.0 + s * q)
    y = r * r
    p = HALF_ANGLE[-1]
    for c in HALF_ANGLE[-2::-1]:
        p = p * y + c
    return 0.5 + r * p, (q * q) * (STEP_SIZE / math.pi)


def cost_of(d):
    return float(np.float32(PENALTY) * np.float32(d * d))


def tables_kernel(gy, zl, yl, mean_ref, coef_ref, ypen):
    lane = lax.broadcasted_iota(jnp.int32, (1, LANES), 1)
    level = lane // zl % LEVELS
    y = lane // (LEVELS * zl)

    def mean_of(bits, own):
        value = jnp.zeros((1, LANES), jnp.float32)
        for k in range(LEVELS):
            phase = own << k
            for n in range(3):
                phase |= (bits >> n & 1) << ((k + 1 + n) % LEVELS)
            value = jnp.where(level == k, mean_ref[phase], value)
        return value

    slope, const = [], []
    for bits in range(8):
        low, high = mean_of(bits, 0), mean_of(bits, 1)
        slope.append(-2.0 * (high - low))
        const.append((high - low) * (high + low))
    for n in range(3):
        for bits in range(8):
            if bits >> n & 1:
                slope[bits] = slope[bits] - slope[bits ^ (1 << n)]
                const[bits] = const[bits] - const[bits ^ (1 << n)]
    for n in range(8):
        coef_ref[pl.ds(n, 1), :] = slope[n]
        coef_ref[pl.ds(8 + n, 1), :] = const[n]

    for gap in range(-(gy - 1), gy):
        for turn in range(yl):
            d = (yl * gap + y - (y + turn) % yl).astype(jnp.float32)
            pen = jnp.where(jnp.abs(d) <= KERNEL, PENALTY * (d * d), FAR)
            ypen[pl.ds(8 * ((gap + gy - 1) * yl + turn), 8), :] = jnp.broadcast_to(pen, (8, LANES))


SLOT = 32


def middle_kernel(share, gz, gy, zl, yl, coef_ref, ypen, in_ref, out_ref, levels, picture,
                  first, evolved, shifted, zdone, done, sems):
    parts = gz * gy
    halo, quarter = share + 4, (share + 4) // 4
    chunk = halo + quarter
    tile = zl * yl
    deep = gz + 2
    me = lax.axis_index("gy") * gz + lax.axis_index("gz")

    lane = lax.broadcasted_iota(jnp.int32, (1, LANES), 1)
    level = lane // zl % LEVELS
    z = lane % zl
    y = lane // (LEVELS * zl)

    def moved(value, index):
        return jnp.take_along_axis(
            value, jnp.broadcast_to(index, value.shape), axis=1, mode="promise_in_bounds"
        )

    def z_turned(value, turn):
        return moved(value, lane + (z + turn) % zl - z)

    def level_turned(value, turn):
        return moved(value, lane + ((level + turn) % LEVELS - level) * zl)

    def y_turned(value, turn):
        return pltpu.roll(value, LANES - turn * LEVELS * zl, 1)

    def stacked(blocks):
        return jnp.concatenate(blocks, axis=0)

    def row_of(a, b, x):
        return (b * deep + a + 1) * SLOT + 8 + x

    zero = jnp.zeros((SLOT, LANES), jnp.float32)
    for b in range(gy):
        for a in (-1, gz):
            levels[pl.ds(row_of(a, b, -8), SLOT), :] = zero
            first[pl.ds(row_of(a, b, -8), SLOT), :] = zero
        for a in range(gz):
            source = (b * gz + a) * chunk + quarter
            levels[pl.ds(row_of(a, b, -2), halo), :] = in_ref[pl.ds(source, halo), :]
        for a in range(0, gz, 4):
            batch = range(a, a + 4)
            packed = stacked([in_ref[pl.ds((b * gz + n) * chunk, 8), :] for n in batch])
            for t in range(4):
                run = moved(packed, t * tile + z * yl + y)
                for n in batch:
                    at = 8 * (n - a)
                    rows = pl.ds(row_of(n, b, t * quarter - 2), quarter)
                    picture[rows, :] = run[at:at + quarter]

    coefs = [coef_ref[pl.ds(n, 1), :] for n in range(16)]
    slope, const = coefs[:8], coefs[8:]

    def step(read, tiles, pic):
        def beside(dz, dy):
            none = jnp.zeros_like(read(0, 0, 0))
            return stacked([
                read(a + dz, b + dy, 0) if 0 <= b + dy < gy else none for a, b in tiles
            ])

        here = beside(0, 0)
        h, rate = heaviside_and_rate(here)
        near = stacked([read(a, b, -1) + read(a, b, 1) for a, b in tiles]) - 6.0 * here
        near = near + z_turned(jnp.where(z == 0, beside(1, 0), here), 1)
        near = near + z_turned(jnp.where(z == zl - 1, beside(-1, 0), here), zl - 1)
        near = near + y_turned(jnp.where(y == 0, beside(0, 1), here), 1)
        near = near + y_turned(jnp.where(y == yl - 1, beside(0, -1), here), yl - 1)
        h1, h2, h3 = (level_turned(h, turn) for turn in (1, 2, 3))
        f = lambda bits: slope[bits] * pic + const[bits]
        g = lambda bits: f(bits) + h1 * f(bits | 1)
        force = (g(0) + h2 * g(2)) + h3 * (g(4) + h2 * g(6))
        return here + rate * (near - force)

    def run_of(ref):
        return lambda a, b, dx: ref[pl.ds(row_of(a, b, dx), share), :]

    for x, outside in ((-1, me == 0), (share, me == parts - 1)):
        across = lambda ref, a, b, dx: ref[pl.ds(row_of(a, b, x + dx), gz, stride=SLOT), :]
        rows = [(0, b) for b in range(gy)]
        pic = stacked([across(picture, 0, b, 0) for _, b in rows])
        value = step(lambda a, b, dx: across(levels, a, b, dx), rows, pic)
        value = jnp.where(outside, 0.0, value)
        for b in range(gy):
            first[pl.ds(row_of(0, b, x), gz, stride=SLOT), :] = value[b * gz:(b + 1) * gz]
    batches = [[(a + n, b) for n in range(4)] for b in range(gy) for a in range(0, gz, 4)]
    for tiles in batches:
        pic = stacked([run_of(picture)(a, b, 0) for a, b in tiles])
        value = step(run_of(levels), tiles, pic)
        for n, (a, b) in enumerate(tiles):
            first[pl.ds(row_of(a, b, 0), share), :] = value[n * share:(n + 1) * share]

    def block_of(a, b):
        return (b * deep + a + 1) * share

    far = jnp.full((share, LANES), FAR, jnp.float32)
    for b in range(gy):
        for a in (-1, gz):
            evolved[pl.ds(block_of(a, b), share), :] = far
    for tiles in batches:
        pic = stacked([run_of(picture)(a, b, 0) for a, b in tiles])
        evolved[pl.ds(block_of(*tiles[0]), 4 * share), :] = step(run_of(first), tiles, pic)

    for b in range(gy):
        for a in range(-1, gz, 4):
            count = min(4, gz - a) * share
            here = evolved[pl.ds(block_of(a, b), count), :]
            above = evolved[pl.ds(block_of(a + 1, b), count), :]
            for turn in range(1, zl):
                value = z_turned(jnp.where(z < turn, above, here), turn)
                shifted[turn - 1, pl.ds(block_of(a, b), count), :] = value

    def z_unit(half, b, low):
        count = 8

        def at(d, n):
            a, turn = low + n + d // zl, d % zl
            if a < (-1 if turn else 0) or a >= gz:
                return None
            if (a, turn) not in loaded:
                rows = pl.ds(block_of(a, b) + 8 * half, 8)
                loaded[a, turn] = shifted[turn - 1, rows, :] if turn else evolved[rows, :]
            return loaded[a, turn]

        loaded = {}
        best = [at(0, n) for n in range(count)]
        for turn in range(zl):
            loaded = {}
            for d in range(turn or zl, min(gz * zl, KERNEL + 1), zl):
                for n in range(count):
                    pair = [v for v in (at(d, n), at(-d, n)) if v is not None]
                    if pair:
                        value = pair[0] if len(pair) == 1 else jnp.minimum(pair[0], pair[1])
                        best[n] = jnp.minimum(best[n], value + cost_of(d))
        for n in range(count):
            zdone[pl.ds((b * gz + low + n) * share + 8 * half, 8), :] = best[n]

    def y_unit(half, low):
        count = 4
        best = [None] * gy
        for other in range(gy):
            starts = [(other * gz + low + n) * share + 8 * half for n in range(count)]
            whole = stacked([zdone[pl.ds(at, 8), :] for at in starts])
            for turn in range(yl):
                value = y_turned(whole, turn) if turn else whole
                for b in range(gy):
                    at = (b - other + gy - 1) * yl + turn
                    new = value + stacked([ypen[pl.ds(8 * at, 8), :]] * count)
                    best[b] = new if best[b] is None else jnp.minimum(best[b], new)
        for b in range(gy):
            for n in range(count):
                rows = pl.ds((b * gz + low + n) * share + 8 * half, 8)
                done[rows, :] = best[b][8 * n:8 * n + 8]

    halves = share // 8
    copies = []
    for half in range(halves + 1):
        z_units = [(b, low) for b in range(gy) for low in range(0, gz, 8)] if half < halves else []
        y_units = list(range(0, gz, 4)) if half else []
        for n in range(max(len(z_units), len(y_units))):
            if n < len(z_units):
                z_unit(half, *z_units[n])
            if n < len(y_units):
                y_unit(half - 1, y_units[n])
                if half == halves:
                    for b in range(gy):
                        rows = pl.ds((b * gz + y_units[n]) * share, 4 * share)
                        sem = sems.at[len(copies)]
                        copies.append(pltpu.make_async_copy(done.at[rows, :], out_ref.at[rows, :], sem))
                        copies[-1].start()
    for copy in copies:
        copy.wait()


def finish_kernel(yl, in_ref, reg_ref, edge, done, sems):
    width = in_ref.shape[0]
    count = width // 8
    group = 8
    far = jnp.full((8, LANES), FAR, jnp.float32)
    edge[pl.ds(0, 8), :] = far
    edge[pl.ds(8, 8), :] = in_ref[pl.ds(0, 8), :]
    edge[pl.ds(16, 8), :] = in_ref[pl.ds(width - 8, 8), :]
    edge[pl.ds(24, 8), :] = far

    def rows(at):
        if at < 0:
            return edge[pl.ds(8 + at, 8), :]
        if at > width - 8:
            return edge[pl.ds(16 + at - (width - 8), 8), :]
        return in_ref[pl.ds(at, 8), :]

    copies = []
    for c in range(width // LANES):
        for low in range(c * LANES // 8, (c + 1) * LANES // 8, group):
            best = [rows(8 * (low + n)) for n in range(group)]
            for rho in range(1, 9):
                plus, minus = {}, {}
                for e in range((KERNEL - rho) // 8 + 1):
                    cost = cost_of(8 * e + rho)
                    for n in range(group):
                        up, down = low + n + e, low + n - e
                        pair = []
                        if 8 * up + rho < width:
                            if up not in plus:
                                plus[up] = rows(8 * up + rho)
                            pair.append(plus[up])
                        if 8 * down - rho > -8:
                            if down not in minus:
                                minus[down] = rows(8 * down - rho)
                            pair.append(minus[down])
                        if not pair:
                            continue
                        value = pair[0] if len(pair) == 1 else jnp.minimum(pair[0], pair[1])
                        best[n] = jnp.minimum(best[n], value + cost)
            for n in range(group):
                done[pl.ds(8 * (low + n), 8), :] = best[n]
        cols = pl.ds(c * LANES, LANES)
        block = done[cols, :].T
        each = LANES // yl
        for y in range(yl):
            done[pl.ds(c * LANES + y, each, stride=yl), :] = block[y * each:(y + 1) * each]
        copies.append(pltpu.make_async_copy(done.at[cols, :], reg_ref.at[:, cols], sems.at[c]))
        copies[-1].start()
    for copy in copies:
        copy.wait()


def corners_kernel(yl, low_ref, high_ref, corner_ref):
    near = jnp.where(lax.axis_index("gy") == 0, yl - 1, 0)
    rows = [low_ref[pl.ds((2 * k + 1) * yl + near, 1), :] for k in range(LEVELS)]
    rows += [high_ref[pl.ds(2 * k * yl + near, 1), :] for k in range(LEVELS)]
    corner_ref[...] = jnp.concatenate(rows, axis=0)


def tile_tools(mean_ref, yl, width):
    upper = lax.axis_index("gy") == 0

    const = [mean_ref[p] * mean_ref[p] for p in range(PHASES)]
    slope = [-2.0 * mean_ref[p] for p in range(PHASES)]
    for k in range(LEVELS):
        for p in range(PHASES):
            if p >> k & 1:
                const[p] = const[p] - const[p ^ (1 << k)]
                slope[p] = slope[p] - slope[p ^ (1 << k)]

    def forces(h, pic):
        c = [None] + [slope[p] * pic + const[p] for p in range(1, PHASES)]
        out = []
        for k in range(LEVELS):
            others = [n for n in range(LEVELS) if n != k]
            part = [c[1 << k | sum((bits >> i & 1) << n for i, n in enumerate(others))]
                    for bits in range(8)]
            for n in others:
                part = [part[i] + h[n] * part[i + 1] for i in range(0, len(part), 2)]
            out.append(part[0])
        return out

    column = lax.broadcasted_iota(jnp.int32, (8, width), 1)
    sub = lax.broadcasted_iota(jnp.int32, (8, width), 0)

    def along_x(u):
        left = jnp.where(column == 0, 0.0, pltpu.roll(u, 1, 1))
        right = jnp.where(column == width - 1, 0.0, pltpu.roll(u, width - 1, 1))
        return left + right

    def advance(here, near, pic):
        pairs = [heaviside_and_rate(u) for u in here]
        force = forces([h for h, _ in pairs], pic)
        return [
            u + rate * (n - 6.0 * u - f)
            for u, n, (_, rate), f in zip(here, near, pairs, force)
        ]

    def along_y(u, row):
        row_up = jnp.where(upper, row, 0.0)
        row_down = jnp.where(upper, 0.0, row)
        above = jnp.where(sub == yl - 1, row_up, pltpu.roll(u, yl - 1, 0))
        below = jnp.where(sub == 0, row_down, pltpu.roll(u, 1, 0))
        return above + below

    return advance, along_x, along_y


def add_neighbours(lev_ref, low_ref, high_ref, zl, yl):
    def level(k, z):
        if z < 0:
            return low_ref[pl.ds((2 * k + 2 + z) * yl, yl), :]
        if z >= zl:
            return high_ref[pl.ds((2 * k + z - zl) * yl, yl), :]
        return lev_ref[pl.ds((k * zl + z) * yl, yl), :]

    return level


def inner_kernel(zl, yl, mean_ref, lev_ref, ct_ref, low_ref, high_ref, side_ref, out_ref):
    advance, along_x, along_y = tile_tools(mean_ref, yl, lev_ref.shape[1])
    level = add_neighbours(lev_ref, low_ref, high_ref, zl, yl)
    for z in range(zl):
        here = [level(k, z) for k in range(LEVELS)]
        near = [
            level(k, z - 1) + level(k, z + 1) + along_x(here[k])
            + along_y(here[k], side_ref[pl.ds(2 * zl * k + z, 1), :])
            for k in range(LEVELS)
        ]
        value = advance(here, near, ct_ref[pl.ds(z * yl, yl), :])
        for k in range(LEVELS):
            out_ref[pl.ds((k * zl + z) * yl, yl), :] = value[k]


def outer_kernel(zl, yl, gz, mean_ref, lev_ref, ct_ref, low_ref, high_ref, side_ref,
                 corner_ref, inner_ref, out_ref, outer, strip, around, strip_first):
    at_z = lax.axis_index("gz")
    edge = jnp.where(lax.axis_index("gy") == 0, yl - 1, 0)
    plane = zl * yl
    advance, along_x, along_y = tile_tools(mean_ref, yl, lev_ref.shape[1])
    level = add_neighbours(lev_ref, low_ref, high_ref, zl, yl)

    def side(k, z):
        if z < 0:
            return corner_ref[pl.ds(k, 1), :]
        if z >= zl:
            return corner_ref[pl.ds(LEVELS + k, 1), :]
        return side_ref[pl.ds(2 * zl * k + z, 1), :]

    picture_at = pl.ds(2 * LEVELS * yl, yl)
    for n, (z, kept, pic) in enumerate((
        (-1, at_z > 0, low_ref[picture_at, :]), (zl, at_z < gz - 1, high_ref[picture_at, :])
    )):
        here = [level(k, z) for k in range(LEVELS)]
        near = [
            level(k, z - 1) + level(k, z + 1) + along_x(here[k]) + along_y(here[k], side(k, z))
            for k in range(LEVELS)
        ]
        value = advance(here, near, pic)
        for k in range(LEVELS):
            outer[pl.ds((2 * k + n) * yl, yl), :] = jnp.where(kept, value[k], 0.0)

    strip[...] = jnp.zeros_like(strip)
    around[...] = jnp.zeros_like(around)
    for k in range(LEVELS):
        for z in range(-1, zl + 1):
            strip[pl.ds(8 * k + z + 1, 1), :] = side(k, z)
        for z in range(zl):
            around[pl.ds(8 * k + z + 1, 1), :] = (
                lev_ref[pl.ds(k * plane + z * yl + edge, 1), :]
                + side_ref[pl.ds(2 * zl * k + zl + z, 1), :]
            )
    for z in range(zl):
        strip[pl.ds(8 * LEVELS + z + 1, 1), :] = side_ref[pl.ds(2 * zl * LEVELS + z, 1), :]
    here = [strip[pl.ds(8 * k, 8), :] for k in range(LEVELS)]
    near = [
        pltpu.roll(u, 7, 0) + pltpu.roll(u, 1, 0) + along_x(u) + around[pl.ds(8 * k, 8), :]
        for k, u in enumerate(here)
    ]
    value = advance(here, near, strip[pl.ds(8 * LEVELS, 8), :])
    for k in range(LEVELS):
        strip_first[pl.ds(8 * k, 8), :] = value[k]

    def after(k, z):
        if z < 0 or z >= zl:
            return outer[pl.ds((2 * k + (z >= zl)) * yl, yl), :]
        return inner_ref[pl.ds((k * zl + z) * yl, yl), :]

    for z in range(zl):
        here = [after(k, z) for k in range(LEVELS)]
        near = [
            after(k, z - 1) + after(k, z + 1) + along_x(here[k])
            + along_y(here[k], strip_first[pl.ds(8 * k + z + 1, 1), :])
            for k in range(LEVELS)
        ]
        value = advance(here, near, ct_ref[pl.ds(z * yl, yl), :])
        for k in range(LEVELS):
            out_ref[pl.ds(k * plane + z * yl, yl), :] = value[k]


def split_body(levels, ct_image, region_means):
    gz, gy = lax.axis_size("gz"), lax.axis_size("gy")
    _, zl, yl, width = levels.shape
    parts = gz * gy
    share = width // parts
    halo, quarter = share + 4, (share + 4) // 4
    chunk = halo + quarter
    f32 = jnp.float32
    vmem = pl.BlockSpec(memory_space=pltpu.VMEM)
    smem = pl.BlockSpec(memory_space=pltpu.SMEM)
    anywhere = pl.BlockSpec(memory_space=pl.ANY)
    params = pltpu.CompilerParams(vmem_limit_bytes=24 * 1024 * 1024)
    scratch = lambda *dims: pltpu.VMEM(dims, f32)
    shape = lambda rows: jax.ShapeDtypeStruct((rows, width), f32)
    message = (2 * LEVELS + 1) * yl
    packed, lines, image, up, down, side = pl.pallas_call(
        functools.partial(pack_kernel, share, zl, yl),
        out_shape=(
            jax.ShapeDtypeStruct((parts * chunk, LANES), f32),
            shape(LANES), shape(zl * yl), shape(message), shape(message),
            shape(2 * zl * LEVELS + zl),
        ),
        in_specs=[pl.BlockSpec(memory_space=pltpu.HBM)] * 2,
        out_specs=(anywhere,) + (vmem,) * 5,
        scratch_shapes=[
            scratch(width + 16, LANES),
            scratch(width, LANES),
            scratch(width, LANES),
            scratch(parts * chunk, LANES),
            pltpu.SemaphoreType.DMA((1 + 2 * width // LANES,)),
        ],
        compiler_params=params,
        name="pack",
    )(
        pltpu.with_memory_space_constraint(levels.reshape(LANES, width), pltpu.HBM),
        pltpu.with_memory_space_constraint(ct_image.reshape(zl * yl, width), pltpu.HBM),
    )
    arrived = lax.all_to_all(
        packed.reshape(parts, chunk, 1, LANES), ("gy", "gz"), split_axis=0, concat_axis=0, tiled=True
    ).reshape(parts * chunk, LANES)

    low = lax.ppermute(up, "gz", [(i, i + 1) for i in range(gz - 1)])
    high = lax.ppermute(down, "gz", [(i + 1, i) for i in range(gz - 1)])
    side = lax.ppermute(side, "gy", [(0, 1), (1, 0)])

    lanes = lambda rows: jax.ShapeDtypeStruct((rows, LANES), f32)
    coefs, penalties = pl.pallas_call(
        functools.partial(tables_kernel, gy, zl, yl),
        out_shape=(lanes(16), lanes(8 * yl * (2 * gy - 1))),
        in_specs=[smem],
        out_specs=(vmem, vmem),
        compiler_params=params,
        name="tables",
    )(region_means)
    slots = gy * (gz + 2) * SLOT
    blocks = gy * (gz + 2) * share
    passed = pl.pallas_call(
        functools.partial(middle_kernel, share, gz, gy, zl, yl),
        out_shape=jax.ShapeDtypeStruct((width, LANES), f32),
        in_specs=[vmem] * 3,
        out_specs=anywhere,
        scratch_shapes=[
            scratch(slots, LANES),
            scratch(slots, LANES),
            scratch(slots, LANES),
            scratch(blocks, LANES),
            scratch(zl - 1, blocks, LANES),
            scratch(width, LANES),
            scratch(width, LANES),
            pltpu.SemaphoreType.DMA((gy * gz // 4,)),
        ],
        compiler_params=params,
        name="middle",
    )(coefs, penalties, arrived)
    passed, low, high, side = lax.optimization_barrier((passed, low, high, side))
    passed = lax.all_to_all(
        passed.reshape(parts, share, LANES), ("gy", "gz"), split_axis=0, concat_axis=0, tiled=True
    ).reshape(width, LANES)

    corner = pl.pallas_call(
        functools.partial(corners_kernel, yl),
        out_shape=shape(2 * LEVELS),
        in_specs=[vmem, vmem],
        out_specs=vmem,
        compiler_params=params,
        name="corners",
    )(low, high)
    corner = lax.ppermute(corner, "gy", [(0, 1), (1, 0)])
    cost = pl.CostEstimate(flops=5_000_000, bytes_accessed=1_000_000, transcendentals=0)
    inner = pl.pallas_call(
        functools.partial(inner_kernel, zl, yl),
        out_shape=shape(LANES),
        in_specs=[smem] + [vmem] * 5,
        out_specs=vmem,
        compiler_params=params,
        cost_estimate=cost,
        name="inner",
    )(region_means, lines, image, low, high, side)
    evolved = pl.pallas_call(
        functools.partial(outer_kernel, zl, yl, gz),
        out_shape=shape(LANES),
        in_specs=[smem] + [vmem] * 7,
        out_specs=vmem,
        scratch_shapes=[
            scratch(2 * LEVELS * yl, width),
            scratch(8 * (LEVELS + 1), width),
            scratch(8 * LEVELS, width),
            scratch(8 * LEVELS, width),
        ],
        compiler_params=params,
        cost_estimate=cost,
        name="outer",
    )(region_means, lines, image, low, high, side, corner, inner)

    regularized = pl.pallas_call(
        functools.partial(finish_kernel, yl),
        out_shape=shape(LANES),
        in_specs=[vmem],
        out_specs=anywhere,
        scratch_shapes=[
            scratch(32, LANES),
            scratch(width, LANES),
            pltpu.SemaphoreType.DMA((width // LANES,)),
        ],
        compiler_params=params,
        name="finish",
    )(passed)
    return evolved.reshape(levels.shape), regularized.reshape(levels.shape)


def body(levels, ct_image, region_means):
    gz, gy = lax.axis_size("gz"), lax.axis_size("gy")
    parts = gz * gy
    count, zl, yl, width = levels.shape
    fits = count == LEVELS and count * zl * yl == LANES and yl == 8 and zl >= 2
    fits = fits and gy == 2 and gz % 8 == 0 and gz * zl <= KERNEL
    fits = fits and width % LANES == 0 and width % parts == 0 and width // parts % 8 == 0
    if fits:
        return split_body(levels, ct_image, region_means)
    return portable_body(levels, ct_image, region_means)


def solution(mesh):
    return jax.shard_map(
        body,
        mesh=mesh,
        in_specs=(P(None, "gz", "gy", None), P("gz", "gy", None), P()),
        out_specs=(P(None, "gz", "gy", None), P(None, "gz", "gy", None)),
        check_vma=False,
    )
```

```python
import functools
import math

import jax
import jax.numpy as jnp
import numpy as np
from jax import lax
from jax.experimental import pallas as pl
from jax.experimental.pallas import tpu as pltpu
from jax.sharding import PartitionSpec as P

LEVELS = 4
PHASES = 16
UPDATES = 2
KERNEL = 200
LANES = 128


PENALTY = 0.0005
STEP_SIZE = 0.5
FAR = 1e30


def with_halo(block, sides, width):
    for axis, dim in sides:
        count = lax.axis_size(axis)
        forward = [(i, i + 1) for i in range(count - 1)]
        backward = [(target, source) for source, target in forward]
        low = lax.ppermute(
            lax.slice_in_dim(block, block.shape[dim] - width, None, axis=dim), axis, forward
        )
        high = lax.ppermute(lax.slice_in_dim(block, 0, width, axis=dim), axis, backward)
        block = jnp.concatenate([low, block, high], axis=dim)
    return block


def evolve(level_pad, picture, region_means):
    interior = level_pad[:, 1:-1, 1:-1, :]
    side_x = jnp.pad(interior, ((0, 0), (0, 0), (0, 0), (1, 1)))
    laplace = level_pad[:, 2:, 1:-1, :] + level_pad[:, :-2, 1:-1, :]
    laplace = laplace + level_pad[:, 1:-1, 2:, :] + level_pad[:, 1:-1, :-2, :]
    laplace = laplace + side_x[..., 2:] + side_x[..., :-2] - 6.0 * interior
    heaviside = 0.5 + jnp.arctan(interior) / math.pi
    delta_term = 1.0 / (math.pi * (1.0 + interior * interior))
    forces = [jnp.zeros_like(interior[0]) for level_id in range(LEVELS)]
    for phase_id in range(PHASES):
        differ = picture - region_means[phase_id]
        energy = differ * differ
        factors = []
        for level_id in range(LEVELS):
            if phase_id >> level_id & 1:
                factors.append(heaviside[level_id])
            else:
                factors.append(1.0 - heaviside[level_id])
        for level_id in range(LEVELS):
            sign_value = 1.0 if phase_id >> level_id & 1 else -1.0
            others = energy
            for other_id in range(LEVELS):
                if other_id != level_id:
                    others = others * factors[other_id]
            forces[level_id] = forces[level_id] + sign_value * others
    force_all = jnp.stack(forces, axis=0)
    return interior + STEP_SIZE * delta_term * (laplace - force_all)


def minplus_lines(field_in, line_axis, kernel_reach):
    moved_field = jnp.moveaxis(field_in, line_axis, -1)
    line_shape = moved_field.shape
    line_len = line_shape[-1]
    line_rows = moved_field.reshape(-1, line_len)
    row_count = line_rows.shape[0]
    positions = jnp.arange(line_len, dtype=jnp.float32)
    distance = positions[:, None] - positions[None, :]
    penalty_table = jnp.where(
        jnp.abs(distance) <= kernel_reach, PENALTY * (distance * distance), jnp.inf
    )
    row_limit = max(1, 1048576 // (line_len * line_len))
    row_block = 1
    while row_block * 2 <= row_limit and row_count % (row_block * 2) == 0:
        row_block = row_block * 2
    grouped = line_rows.reshape(row_count // row_block, row_block, line_len)

    def block_min(block_rows):
        return jnp.min(block_rows[:, None, :] + penalty_table[None, :, :], axis=2)

    result_rows = lax.map(block_min, grouped)
    return jnp.moveaxis(result_rows.reshape(line_shape), -1, line_axis)


def portable_body(levels, ct_image, region_means):
    current = levels
    for _ in range(UPDATES):
        padded = with_halo(current, (("gz", 1), ("gy", 2)), 1)
        current = evolve(padded, ct_image, region_means)
    field = minplus_lines(current, 3, KERNEL)
    for axis, dim in (("gz", 1), ("gy", 2)):
        lines = lax.all_to_all(field, axis, split_axis=3, concat_axis=dim, tiled=True)
        lines = minplus_lines(lines, dim, KERNEL)
        field = lax.all_to_all(lines, axis, split_axis=dim, concat_axis=3, tiled=True)
    return current, field


def pack_kernel(share, zl, yl, lev_hbm, ct_hbm, out_hbm, lev, ct_ref, up_ref, down_ref, side_ref,
                stage, lines, turned, picture, out_ref, sems):
    width = lev.shape[1]
    parts = width // share
    blocks = width // LANES
    halo, quarter = share + 4, (share + 4) // 4
    chunk = halo + quarter
    count = LEVELS * zl
    tile = zl * yl
    arriving = [pltpu.make_async_copy(ct_hbm, ct_ref, sems.at[0])]
    for b in range(blocks):
        here = stage.at[pl.ds(b * LANES, LANES), :]
        source = lev_hbm.at[:, pl.ds(b * LANES, LANES)]
        arriving.append(pltpu.make_async_copy(source, here, sems.at[1 + b]))
    whole = pltpu.make_async_copy(lev_hbm, lev, sems.at[1 + 2 * blocks])
    for copy in arriving + [whole]:
        copy.start()
    lines[pl.ds(0, 8), :] = jnp.zeros((8, LANES), jnp.float32)
    lines[pl.ds(8 + width, 8), :] = jnp.zeros((8, LANES), jnp.float32)

    arriving[0].wait()
    across = jnp.concatenate([ct_ref[:, b * LANES:(b + 1) * LANES] for b in range(blocks)], axis=0).T
    for n in range(blocks):
        turn = lambda rows, by: pltpu.roll(rows, by % blocks * tile, 1) if by % blocks else rows
        turned[n, pl.ds(0, 8), :] = turn(across[LANES - 8:], n + 1)
        turned[n, pl.ds(8, LANES), :] = turn(across, n)
        turned[n, pl.ds(8 + LANES, 8), :] = turn(across[:8], n - 1)
    group = lax.broadcasted_iota(jnp.int32, (8, LANES), 1) // tile
    each = LANES // share
    for r in range(parts):
        b, at = r // each, 8 + r % each * share - 2
        value = None
        for t in range(4):
            run = turned[(t - b) % blocks, pl.ds(at + quarter * t, 8), :]
            value = run if value is None else jnp.where(group >= t, run, value)
        picture[pl.ds(8 * r, 8), :] = value
    leaving = []
    sub = lax.broadcasted_iota(jnp.int32, (8, LANES), 0)

    def out_tile(tile):
        value = None
        for r in range(8 * tile // chunk, min((8 * tile + 7) // chunk + 1, parts)):
            for source, begin, length, origin in (
                (picture, r * chunk, quarter, 8 * r),
                (lines, r * chunk + quarter, halo, 6 + r * share),
            ):
                if begin + length <= 8 * tile or begin >= 8 * tile + 8:
                    continue
                piece = source[pl.ds(8 * tile - begin + origin, 8), :]
                value = piece if value is None else jnp.where(sub >= begin - 8 * tile, piece, value)
        return value

    start = 0
    for b in range(blocks):
        arriving[1 + b].wait()
        block = [stage[pl.ds(b * LANES + y, count, stride=yl), :] for y in range(yl)]
        lines[pl.ds(8 + b * LANES, LANES), :] = jnp.concatenate(block, axis=0).T
        known = parts if b + 1 == blocks else (b + 1) * LANES // share - 1
        stop = known * chunk // 8 * 8
        for tile in range(start // 8, stop // 8):
            out_ref[pl.ds(8 * tile, 8), :] = out_tile(tile)
        rows = pl.ds(start, stop - start)
        leaving.append(
            pltpu.make_async_copy(out_ref.at[rows, :], out_hbm.at[rows, :], sems.at[1 + blocks + b])
        )
        leaving[-1].start()
        start = stop
    whole.wait()
    plane = zl * yl
    for k in range(LEVELS):
        at = pl.ds(2 * k * yl, 2 * yl)
        up_ref[at, :] = lev[pl.ds((k + 1) * plane - 2 * yl, 2 * yl), :]
        down_ref[at, :] = lev[pl.ds(k * plane, 2 * yl), :]
    at = pl.ds(2 * LEVELS * yl, yl)
    up_ref[at, :] = ct_ref[pl.ds(plane - yl, yl), :]
    down_ref[at, :] = ct_ref[pl.ds(0, yl), :]
    upper = lax.axis_index("gy") == 0
    near = jnp.where(upper, yl - 1, 0)
    next_near = jnp.where(upper, yl - 2, 1)
    for k in range(LEVELS):
        for z in range(zl):
            base = k * plane + z * yl
            side_ref[pl.ds(2 * zl * k + z, 1), :] = lev[pl.ds(base + near, 1), :]
            side_ref[pl.ds(2 * zl * k + zl + z, 1), :] = lev[pl.ds(base + next_near, 1), :]
    for z in range(zl):
        side_ref[pl.ds(2 * zl * LEVELS + z, 1), :] = ct_ref[pl.ds(z * yl + near, 1), :]
    for copy in leaving:
        copy.wait()


HALF_ANGLE = (
    0.6366196870803833, -0.21219870448112488, 0.12714172899723053, -0.0893140509724617,
    0.06329755485057831, -0.03813650459051132, 0.015633534640073776, -0.0030433274805545807,
)


def heaviside_and_rate(u):
    s = 1.0 + u * u
    q = lax.rsqrt(s)
    r = u / (1.0 + s * q)
    y = r * r
    p = HALF_ANGLE[-1]
    for c in HALF_ANGLE[-2::-1]:
        p = p * y + c
    return 0.5 + r * p, (q * q) * (STEP_SIZE / math.pi)


def cost_of(d):
    return float(np.float32(PENALTY) * np.float32(d * d))


def tables_kernel(gy, zl, yl, mean_ref, coef_ref, ypen):
    lane = lax.broadcasted_iota(jnp.int32, (1, LANES), 1)
    level = lane // zl % LEVELS
    y = lane // (LEVELS * zl)

    def mean_of(bits, own):
        value = jnp.zeros((1, LANES), jnp.float32)
        for k in range(LEVELS):
            phase = own << k
            for n in range(3):
                phase |= (bits >> n & 1) << ((k + 1 + n) % LEVELS)
            value = jnp.where(level == k, mean_ref[phase], value)
        return value

    slope, const = [], []
    for bits in range(8):
        low, high = mean_of(bits, 0), mean_of(bits, 1)
        slope.append(-2.0 * (high - low))
        const.append((high - low) * (high + low))
    for n in range(3):
        for bits in range(8):
            if bits >> n & 1:
                slope[bits] = slope[bits] - slope[bits ^ (1 << n)]
                const[bits] = const[bits] - const[bits ^ (1 << n)]
    for n in range(8):
        coef_ref[pl.ds(n, 1), :] = slope[n]
        coef_ref[pl.ds(8 + n, 1), :] = const[n]

    for gap in range(-(gy - 1), gy):
        for turn in range(yl):
            d = (yl * gap + y - (y + turn) % yl).astype(jnp.float32)
            pen = jnp.where(jnp.abs(d) <= KERNEL, PENALTY * (d * d), FAR)
            ypen[pl.ds(8 * ((gap + gy - 1) * yl + turn), 8), :] = jnp.broadcast_to(pen, (8, LANES))


SLOT = 32


def middle_kernel(share, gz, gy, zl, yl, coef_ref, ypen, in_ref, out_ref, levels, picture,
                  first, evolved, shifted, zdone, done, sems):
    parts = gz * gy
    halo, quarter = share + 4, (share + 4) // 4
    chunk = halo + quarter
    tile = zl * yl
    deep = gz + 2
    me = lax.axis_index("gy") * gz + lax.axis_index("gz")

    lane = lax.broadcasted_iota(jnp.int32, (1, LANES), 1)
    level = lane // zl % LEVELS
    z = lane % zl
    y = lane // (LEVELS * zl)

    def moved(value, index):
        return jnp.take_along_axis(
            value, jnp.broadcast_to(index, value.shape), axis=1, mode="promise_in_bounds"
        )

    def z_turned(value, turn):
        return moved(value, lane + (z + turn) % zl - z)

    def level_turned(value, turn):
        return moved(value, lane + ((level + turn) % LEVELS - level) * zl)

    def y_turned(value, turn):
        return pltpu.roll(value, LANES - turn * LEVELS * zl, 1)

    def stacked(blocks):
        return jnp.concatenate(blocks, axis=0)

    def row_of(a, b, x):
        return (b * deep + a + 1) * SLOT + 8 + x

    zero = jnp.zeros((SLOT, LANES), jnp.float32)
    for b in range(gy):
        for a in (-1, gz):
            levels[pl.ds(row_of(a, b, -8), SLOT), :] = zero
            first[pl.ds(row_of(a, b, -8), SLOT), :] = zero
        for a in range(gz):
            source = (b * gz + a) * chunk + quarter
            levels[pl.ds(row_of(a, b, -2), halo), :] = in_ref[pl.ds(source, halo), :]
        for a in range(0, gz, 4):
            batch = range(a, a + 4)
            packed = stacked([in_ref[pl.ds((b * gz + n) * chunk, 8), :] for n in batch])
            for t in range(4):
                run = moved(packed, t * tile + z * yl + y)
                for n in batch:
                    at = 8 * (n - a)
                    rows = pl.ds(row_of(n, b, t * quarter - 2), quarter)
                    picture[rows, :] = run[at:at + quarter]

    coefs = [coef_ref[pl.ds(n, 1), :] for n in range(16)]
    slope, const = coefs[:8], coefs[8:]

    def step(read, tiles, pic):
        def beside(dz, dy):
            none = jnp.zeros_like(read(0, 0, 0))
            return stacked([
                read(a + dz, b + dy, 0) if 0 <= b + dy < gy else none for a, b in tiles
            ])

        here = beside(0, 0)
        h, rate = heaviside_and_rate(here)
        near = stacked([read(a, b, -1) + read(a, b, 1) for a, b in tiles]) - 6.0 * here
        near = near + z_turned(jnp.where(z == 0, beside(1, 0), here), 1)
        near = near + z_turned(jnp.where(z == zl - 1, beside(-1, 0), here), zl - 1)
        near = near + y_turned(jnp.where(y == 0, beside(0, 1), here), 1)
        near = near + y_turned(jnp.where(y == yl - 1, beside(0, -1), here), yl - 1)
        h1, h2, h3 = (level_turned(h, turn) for turn in (1, 2, 3))
        f = lambda bits: slope[bits] * pic + const[bits]
        g = lambda bits: f(bits) + h1 * f(bits | 1)
        force = (g(0) + h2 * g(2)) + h3 * (g(4) + h2 * g(6))
        return here + rate * (near - force)

    def run_of(ref):
        return lambda a, b, dx: ref[pl.ds(row_of(a, b, dx), share), :]

    for x, outside in ((-1, me == 0), (share, me == parts - 1)):
        across = lambda ref, a, b, dx: ref[pl.ds(row_of(a, b, x + dx), gz, stride=SLOT), :]
        rows = [(0, b) for b in range(gy)]
        pic = stacked([across(picture, 0, b, 0) for _, b in rows])
        value = step(lambda a, b, dx: across(levels, a, b, dx), rows, pic)
        value = jnp.where(outside, 0.0, value)
        for b in range(gy):
            first[pl.ds(row_of(0, b, x), gz, stride=SLOT), :] = value[b * gz:(b + 1) * gz]
    batches = [[(a + n, b) for n in range(4)] for b in range(gy) for a in range(0, gz, 4)]
    for tiles in batches:
        pic = stacked([run_of(picture)(a, b, 0) for a, b in tiles])
        value = step(run_of(levels), tiles, pic)
        for n, (a, b) in enumerate(tiles):
            first[pl.ds(row_of(a, b, 0), share), :] = value[n * share:(n + 1) * share]

    def block_of(a, b):
        return (b * deep + a + 1) * share

    far = jnp.full((share, LANES), FAR, jnp.float32)
    for b in range(gy):
        for a in (-1, gz):
            evolved[pl.ds(block_of(a, b), share), :] = far
    for tiles in batches:
        pic = stacked([run_of(picture)(a, b, 0) for a, b in tiles])
        evolved[pl.ds(block_of(*tiles[0]), 4 * share), :] = step(run_of(first), tiles, pic)

    for b in range(gy):
        for a in range(-1, gz, 4):
            count = min(4, gz - a) * share
            here = evolved[pl.ds(block_of(a, b), count), :]
            above = evolved[pl.ds(block_of(a + 1, b), count), :]
            for turn in range(1, zl):
                value = z_turned(jnp.where(z < turn, above, here), turn)
                shifted[turn - 1, pl.ds(block_of(a, b), count), :] = value

    def z_unit(half, b, low):
        count = 8

        def at(d, n):
            a, turn = low + n + d // zl, d % zl
            if a < (-1 if turn else 0) or a >= gz:
                return None
            if (a, turn) not in loaded:
                rows = pl.ds(block_of(a, b) + 8 * half, 8)
                loaded[a, turn] = shifted[turn - 1, rows, :] if turn else evolved[rows, :]
            return loaded[a, turn]

        loaded = {}
        best = [at(0, n) for n in range(count)]
        for turn in range(zl):
            loaded = {}
            for d in range(turn or zl, min(gz * zl, KERNEL + 1), zl):
                for n in range(count):
                    pair = [v for v in (at(d, n), at(-d, n)) if v is not None]
                    if pair:
                        value = pair[0] if len(pair) == 1 else jnp.minimum(pair[0], pair[1])
                        best[n] = jnp.minimum(best[n], value + cost_of(d))
        for n in range(count):
            zdone[pl.ds((b * gz + low + n) * share + 8 * half, 8), :] = best[n]

    def y_unit(half, low):
        count = 4
        best = [None] * gy
        for other in range(gy):
            starts = [(other * gz + low + n) * share + 8 * half for n in range(count)]
            whole = stacked([zdone[pl.ds(at, 8), :] for at in starts])
            for turn in range(yl):
                value = y_turned(whole, turn) if turn else whole
                for b in range(gy):
                    at = (b - other + gy - 1) * yl + turn
                    new = value + stacked([ypen[pl.ds(8 * at, 8), :]] * count)
                    best[b] = new if best[b] is None else jnp.minimum(best[b], new)
        for b in range(gy):
            for n in range(count):
                rows = pl.ds((b * gz + low + n) * share + 8 * half, 8)
                done[rows, :] = best[b][8 * n:8 * n + 8]

    halves = share // 8
    copies = []
    for half in range(halves + 1):
        z_units = [(b, low) for b in range(gy) for low in range(0, gz, 8)] if half < halves else []
        y_units = list(range(0, gz, 4)) if half else []
        for n in range(max(len(z_units), len(y_units))):
            if n < len(z_units):
                z_unit(half, *z_units[n])
            if n < len(y_units):
                y_unit(half - 1, y_units[n])
                if half == halves:
                    for b in range(gy):
                        rows = pl.ds((b * gz + y_units[n]) * share, 4 * share)
                        sem = sems.at[len(copies)]
                        copies.append(pltpu.make_async_copy(done.at[rows, :], out_ref.at[rows, :], sem))
                        copies[-1].start()
    for copy in copies:
        copy.wait()


def finish_kernel(yl, in_ref, reg_ref, edge, done, sems):
    width = in_ref.shape[0]
    count = width // 8
    group = 8
    far = jnp.full((8, LANES), FAR, jnp.float32)
    edge[pl.ds(0, 8), :] = far
    edge[pl.ds(8, 8), :] = in_ref[pl.ds(0, 8), :]
    edge[pl.ds(16, 8), :] = in_ref[pl.ds(width - 8, 8), :]
    edge[pl.ds(24, 8), :] = far

    def rows(at):
        if at < 0:
            return edge[pl.ds(8 + at, 8), :]
        if at > width - 8:
            return edge[pl.ds(16 + at - (width - 8), 8), :]
        return in_ref[pl.ds(at, 8), :]

    copies = []
    for c in range(width // LANES):
        for low in range(c * LANES // 8, (c + 1) * LANES // 8, group):
            best = [rows(8 * (low + n)) for n in range(group)]
            for rho in range(1, 9):
                plus, minus = {}, {}
                for e in range((KERNEL - rho) // 8 + 1):
                    cost = cost_of(8 * e + rho)
                    for n in range(group):
                        up, down = low + n + e, low + n - e
                        pair = []
                        if 8 * up + rho < width:
                            if up not in plus:
                                plus[up] = rows(8 * up + rho)
                            pair.append(plus[up])
                        if 8 * down - rho > -8:
                            if down not in minus:
                                minus[down] = rows(8 * down - rho)
                            pair.append(minus[down])
                        if not pair:
                            continue
                        value = pair[0] if len(pair) == 1 else jnp.minimum(pair[0], pair[1])
                        best[n] = jnp.minimum(best[n], value + cost)
            for n in range(group):
                done[pl.ds(8 * (low + n), 8), :] = best[n]
        cols = pl.ds(c * LANES, LANES)
        block = done[cols, :].T
        each = LANES // yl
        for y in range(yl):
            done[pl.ds(c * LANES + y, each, stride=yl), :] = block[y * each:(y + 1) * each]
        copies.append(pltpu.make_async_copy(done.at[cols, :], reg_ref.at[:, cols], sems.at[c]))
        copies[-1].start()
    for copy in copies:
        copy.wait()


def corners_kernel(yl, low_ref, high_ref, corner_ref):
    near = jnp.where(lax.axis_index("gy") == 0, yl - 1, 0)
    rows = [low_ref[pl.ds((2 * k + 1) * yl + near, 1), :] for k in range(LEVELS)]
    rows += [high_ref[pl.ds(2 * k * yl + near, 1), :] for k in range(LEVELS)]
    corner_ref[...] = jnp.concatenate(rows, axis=0)


def tile_tools(mean_ref, yl, width):
    upper = lax.axis_index("gy") == 0

    const = [mean_ref[p] * mean_ref[p] for p in range(PHASES)]
    slope = [-2.0 * mean_ref[p] for p in range(PHASES)]
    for k in range(LEVELS):
        for p in range(PHASES):
            if p >> k & 1:
                const[p] = const[p] - const[p ^ (1 << k)]
                slope[p] = slope[p] - slope[p ^ (1 << k)]

    def forces(h, pic):
        c = [None] + [slope[p] * pic + const[p] for p in range(1, PHASES)]
        out = []
        for k in range(LEVELS):
            others = [n for n in range(LEVELS) if n != k]
            part = [c[1 << k | sum((bits >> i & 1) << n for i, n in enumerate(others))]
                    for bits in range(8)]
            for n in others:
                part = [part[i] + h[n] * part[i + 1] for i in range(0, len(part), 2)]
            out.append(part[0])
        return out

    column = lax.broadcasted_iota(jnp.int32, (8, width), 1)
    sub = lax.broadcasted_iota(jnp.int32, (8, width), 0)

    def along_x(u):
        left = jnp.where(column == 0, 0.0, pltpu.roll(u, 1, 1))
        right = jnp.where(column == width - 1, 0.0, pltpu.roll(u, width - 1, 1))
        return left + right

    def advance(here, near, pic):
        pairs = [heaviside_and_rate(u) for u in here]
        force = forces([h for h, _ in pairs], pic)
        return [
            u + rate * (n - 6.0 * u - f)
            for u, n, (_, rate), f in zip(here, near, pairs, force)
        ]

    def along_y(u, row):
        row_up = jnp.where(upper, row, 0.0)
        row_down = jnp.where(upper, 0.0, row)
        above = jnp.where(sub == yl - 1, row_up, pltpu.roll(u, yl - 1, 0))
        below = jnp.where(sub == 0, row_down, pltpu.roll(u, 1, 0))
        return above + below

    return advance, along_x, along_y


def add_neighbours(lev_ref, low_ref, high_ref, zl, yl):
    def level(k, z):
        if z < 0:
            return low_ref[pl.ds((2 * k + 2 + z) * yl, yl), :]
        if z >= zl:
            return high_ref[pl.ds((2 * k + z - zl) * yl, yl), :]
        return lev_ref[pl.ds((k * zl + z) * yl, yl), :]

    return level


def inner_kernel(zl, yl, mean_ref, lev_ref, ct_ref, low_ref, high_ref, side_ref, out_ref):
    advance, along_x, along_y = tile_tools(mean_ref, yl, lev_ref.shape[1])
    level = add_neighbours(lev_ref, low_ref, high_ref, zl, yl)
    for z in range(zl):
        here = [level(k, z) for k in range(LEVELS)]
        near = [
            level(k, z - 1) + level(k, z + 1) + along_x(here[k])
            + along_y(here[k], side_ref[pl.ds(2 * zl * k + z, 1), :])
            for k in range(LEVELS)
        ]
        value = advance(here, near, ct_ref[pl.ds(z * yl, yl), :])
        for k in range(LEVELS):
            out_ref[pl.ds((k * zl + z) * yl, yl), :] = value[k]


def outer_kernel(zl, yl, gz, mean_ref, lev_ref, ct_ref, low_ref, high_ref, side_ref,
                 corner_ref, inner_ref, out_ref, outer, strip, around, strip_first):
    at_z = lax.axis_index("gz")
    edge = jnp.where(lax.axis_index("gy") == 0, yl - 1, 0)
    plane = zl * yl
    advance, along_x, along_y = tile_tools(mean_ref, yl, lev_ref.shape[1])
    level = add_neighbours(lev_ref, low_ref, high_ref, zl, yl)

    def side(k, z):
        if z < 0:
            return corner_ref[pl.ds(k, 1), :]
        if z >= zl:
            return corner_ref[pl.ds(LEVELS + k, 1), :]
        return side_ref[pl.ds(2 * zl * k + z, 1), :]

    picture_at = pl.ds(2 * LEVELS * yl, yl)
    for n, (z, kept, pic) in enumerate((
        (-1, at_z > 0, low_ref[picture_at, :]), (zl, at_z < gz - 1, high_ref[picture_at, :])
    )):
        here = [level(k, z) for k in range(LEVELS)]
        near = [
            level(k, z - 1) + level(k, z + 1) + along_x(here[k]) + along_y(here[k], side(k, z))
            for k in range(LEVELS)
        ]
        value = advance(here, near, pic)
        for k in range(LEVELS):
            outer[pl.ds((2 * k + n) * yl, yl), :] = jnp.where(kept, value[k], 0.0)

    strip[...] = jnp.zeros_like(strip)
    around[...] = jnp.zeros_like(around)
    for k in range(LEVELS):
        for z in range(-1, zl + 1):
            strip[pl.ds(8 * k + z + 1, 1), :] = side(k, z)
        for z in range(zl):
            around[pl.ds(8 * k + z + 1, 1), :] = (
                lev_ref[pl.ds(k * plane + z * yl + edge, 1), :]
                + side_ref[pl.ds(2 * zl * k + zl + z, 1), :]
            )
    for z in range(zl):
        strip[pl.ds(8 * LEVELS + z + 1, 1), :] = side_ref[pl.ds(2 * zl * LEVELS + z, 1), :]
    here = [strip[pl.ds(8 * k, 8), :] for k in range(LEVELS)]
    near = [
        pltpu.roll(u, 7, 0) + pltpu.roll(u, 1, 0) + along_x(u) + around[pl.ds(8 * k, 8), :]
        for k, u in enumerate(here)
    ]
    value = advance(here, near, strip[pl.ds(8 * LEVELS, 8), :])
    for k in range(LEVELS):
        strip_first[pl.ds(8 * k, 8), :] = value[k]

    def after(k, z):
        if z < 0 or z >= zl:
            return outer[pl.ds((2 * k + (z >= zl)) * yl, yl), :]
        return inner_ref[pl.ds((k * zl + z) * yl, yl), :]

    for z in range(zl):
        here = [after(k, z) for k in range(LEVELS)]
        near = [
            after(k, z - 1) + after(k, z + 1) + along_x(here[k])
            + along_y(here[k], strip_first[pl.ds(8 * k + z + 1, 1), :])
            for k in range(LEVELS)
        ]
        value = advance(here, near, ct_ref[pl.ds(z * yl, yl), :])
        for k in range(LEVELS):
            out_ref[pl.ds(k * plane + z * yl, yl), :] = value[k]


def split_body(levels, ct_image, region_means):
    gz, gy = lax.axis_size("gz"), lax.axis_size("gy")
    _, zl, yl, width = levels.shape
    parts = gz * gy
    share = width // parts
    halo, quarter = share + 4, (share + 4) // 4
    chunk = halo + quarter
    f32 = jnp.float32
    vmem = pl.BlockSpec(memory_space=pltpu.VMEM)
    smem = pl.BlockSpec(memory_space=pltpu.SMEM)
    anywhere = pl.BlockSpec(memory_space=pl.ANY)
    params = pltpu.CompilerParams(vmem_limit_bytes=24 * 1024 * 1024)
    scratch = lambda *dims: pltpu.VMEM(dims, f32)
    shape = lambda rows: jax.ShapeDtypeStruct((rows, width), f32)
    message = (2 * LEVELS + 1) * yl
    packed, lines, image, up, down, side = pl.pallas_call(
        functools.partial(pack_kernel, share, zl, yl),
        out_shape=(
            jax.ShapeDtypeStruct((parts * chunk, LANES), f32),
            shape(LANES), shape(zl * yl), shape(message), shape(message),
            shape(2 * zl * LEVELS + zl),
        ),
        in_specs=[pl.BlockSpec(memory_space=pltpu.HBM)] * 2,
        out_specs=(anywhere,) + (vmem,) * 5,
        scratch_shapes=[
            scratch(width + 8, LANES),
            scratch(width + 16, LANES),
            scratch(4, LANES + 16, LANES),
            scratch(8 * parts + 8, LANES),
            scratch(parts * chunk, LANES),
            pltpu.SemaphoreType.DMA((2 + 2 * width // LANES,)),
        ],
        compiler_params=params,
        name="pack",
    )(
        pltpu.with_memory_space_constraint(levels.reshape(LANES, width), pltpu.HBM),
        pltpu.with_memory_space_constraint(ct_image.reshape(zl * yl, width), pltpu.HBM),
    )
    arrived = lax.all_to_all(
        packed.reshape(parts, chunk, 1, LANES), ("gy", "gz"), split_axis=0, concat_axis=0, tiled=True
    ).reshape(parts * chunk, LANES)

    low = lax.ppermute(up, "gz", [(i, i + 1) for i in range(gz - 1)])
    high = lax.ppermute(down, "gz", [(i + 1, i) for i in range(gz - 1)])
    side = lax.ppermute(side, "gy", [(0, 1), (1, 0)])

    lanes = lambda rows: jax.ShapeDtypeStruct((rows, LANES), f32)
    coefs, penalties = pl.pallas_call(
        functools.partial(tables_kernel, gy, zl, yl),
        out_shape=(lanes(16), lanes(8 * yl * (2 * gy - 1))),
        in_specs=[smem],
        out_specs=(vmem, vmem),
        compiler_params=params,
        name="tables",
    )(region_means)
    slots = (gy * (gz + 2) + 1) * SLOT
    blocks = gy * (gz + 2) * share
    passed = pl.pallas_call(
        functools.partial(middle_kernel, share, gz, gy, zl, yl),
        out_shape=jax.ShapeDtypeStruct((width, LANES), f32),
        in_specs=[vmem] * 3,
        out_specs=anywhere,
        scratch_shapes=[
            scratch(slots, LANES),
            scratch(slots, LANES),
            scratch(slots, LANES),
            scratch(blocks, LANES),
            scratch(zl - 1, blocks, LANES),
            scratch(width, LANES),
            scratch(width, LANES),
            pltpu.SemaphoreType.DMA((gy * gz // 4,)),
        ],
        compiler_params=params,
        name="middle",
    )(coefs, penalties, arrived)
    passed, low, high, side = lax.optimization_barrier((passed, low, high, side))
    passed = lax.all_to_all(
        passed.reshape(parts, share, LANES), ("gy", "gz"), split_axis=0, concat_axis=0, tiled=True
    ).reshape(width, LANES)

    corner = pl.pallas_call(
        functools.partial(corners_kernel, yl),
        out_shape=shape(2 * LEVELS),
        in_specs=[vmem, vmem],
        out_specs=vmem,
        compiler_params=params,
        name="corners",
    )(low, high)
    corner = lax.ppermute(corner, "gy", [(0, 1), (1, 0)])
    cost = pl.CostEstimate(flops=5_000_000, bytes_accessed=1_000_000, transcendentals=0)
    inner = pl.pallas_call(
        functools.partial(inner_kernel, zl, yl),
        out_shape=shape(LANES),
        in_specs=[smem] + [vmem] * 5,
        out_specs=vmem,
        compiler_params=params,
        cost_estimate=cost,
        name="inner",
    )(region_means, lines, image, low, high, side)
    evolved = pl.pallas_call(
        functools.partial(outer_kernel, zl, yl, gz),
        out_shape=shape(LANES),
        in_specs=[smem] + [vmem] * 7,
        out_specs=vmem,
        scratch_shapes=[
            scratch(2 * LEVELS * yl, width),
            scratch(8 * (LEVELS + 1), width),
            scratch(8 * LEVELS, width),
            scratch(8 * LEVELS, width),
        ],
        compiler_params=params,
        cost_estimate=cost,
        name="outer",
    )(region_means, lines, image, low, high, side, corner, inner)

    regularized = pl.pallas_call(
        functools.partial(finish_kernel, yl),
        out_shape=shape(LANES),
        in_specs=[vmem],
        out_specs=anywhere,
        scratch_shapes=[
            scratch(32, LANES),
            scratch(width + 8, LANES),
            pltpu.SemaphoreType.DMA((width // LANES,)),
        ],
        compiler_params=params,
        name="finish",
    )(passed)
    return evolved.reshape(levels.shape), regularized.reshape(levels.shape)


def body(levels, ct_image, region_means):
    gz, gy = lax.axis_size("gz"), lax.axis_size("gy")
    parts = gz * gy
    count, zl, yl, width = levels.shape
    fits = count == LEVELS and count * zl * yl == LANES and yl == 8 and zl >= 2
    fits = fits and gy == 2 and gz % 8 == 0 and gz * zl <= KERNEL
    fits = fits and width == 4 * LANES and parts == 32
    if fits:
        return split_body(levels, ct_image, region_means)
    return portable_body(levels, ct_image, region_means)


def solution(mesh):
    return jax.shard_map(
        body,
        mesh=mesh,
        in_specs=(P(None, "gz", "gy", None), P("gz", "gy", None), P()),
        out_specs=(P(None, "gz", "gy", None), P(None, "gz", "gy", None)),
        check_vma=False,
    )
```

```python
import functools
import math

import jax
import jax.numpy as jnp
import numpy as np
from jax import lax
from jax.experimental import pallas as pl
from jax.experimental.pallas import tpu as pltpu
from jax.sharding import PartitionSpec as P

LEVELS = 4
PHASES = 16
UPDATES = 2
KERNEL = 200
LANES = 128


PENALTY = 0.0005
STEP_SIZE = 0.5
FAR = 1e30


def with_halo(block, sides, width):
    for axis, dim in sides:
        count = lax.axis_size(axis)
        forward = [(i, i + 1) for i in range(count - 1)]
        backward = [(target, source) for source, target in forward]
        low = lax.ppermute(
            lax.slice_in_dim(block, block.shape[dim] - width, None, axis=dim), axis, forward
        )
        high = lax.ppermute(lax.slice_in_dim(block, 0, width, axis=dim), axis, backward)
        block = jnp.concatenate([low, block, high], axis=dim)
    return block


def evolve(level_pad, picture, region_means):
    interior = level_pad[:, 1:-1, 1:-1, :]
    side_x = jnp.pad(interior, ((0, 0), (0, 0), (0, 0), (1, 1)))
    laplace = level_pad[:, 2:, 1:-1, :] + level_pad[:, :-2, 1:-1, :]
    laplace = laplace + level_pad[:, 1:-1, 2:, :] + level_pad[:, 1:-1, :-2, :]
    laplace = laplace + side_x[..., 2:] + side_x[..., :-2] - 6.0 * interior
    heaviside = 0.5 + jnp.arctan(interior) / math.pi
    delta_term = 1.0 / (math.pi * (1.0 + interior * interior))
    forces = [jnp.zeros_like(interior[0]) for level_id in range(LEVELS)]
    for phase_id in range(PHASES):
        differ = picture - region_means[phase_id]
        energy = differ * differ
        factors = []
        for level_id in range(LEVELS):
            if phase_id >> level_id & 1:
                factors.append(heaviside[level_id])
            else:
                factors.append(1.0 - heaviside[level_id])
        for level_id in range(LEVELS):
            sign_value = 1.0 if phase_id >> level_id & 1 else -1.0
            others = energy
            for other_id in range(LEVELS):
                if other_id != level_id:
                    others = others * factors[other_id]
            forces[level_id] = forces[level_id] + sign_value * others
    force_all = jnp.stack(forces, axis=0)
    return interior + STEP_SIZE * delta_term * (laplace - force_all)


def minplus_lines(field_in, line_axis, kernel_reach):
    moved_field = jnp.moveaxis(field_in, line_axis, -1)
    line_shape = moved_field.shape
    line_len = line_shape[-1]
    line_rows = moved_field.reshape(-1, line_len)
    row_count = line_rows.shape[0]
    positions = jnp.arange(line_len, dtype=jnp.float32)
    distance = positions[:, None] - positions[None, :]
    penalty_table = jnp.where(
        jnp.abs(distance) <= kernel_reach, PENALTY * (distance * distance), jnp.inf
    )
    row_limit = max(1, 1048576 // (line_len * line_len))
    row_block = 1
    while row_block * 2 <= row_limit and row_count % (row_block * 2) == 0:
        row_block = row_block * 2
    grouped = line_rows.reshape(row_count // row_block, row_block, line_len)

    def block_min(block_rows):
        return jnp.min(block_rows[:, None, :] + penalty_table[None, :, :], axis=2)

    result_rows = lax.map(block_min, grouped)
    return jnp.moveaxis(result_rows.reshape(line_shape), -1, line_axis)


def portable_body(levels, ct_image, region_means):
    current = levels
    for _ in range(UPDATES):
        padded = with_halo(current, (("gz", 1), ("gy", 2)), 1)
        current = evolve(padded, ct_image, region_means)
    field = minplus_lines(current, 3, KERNEL)
    for axis, dim in (("gz", 1), ("gy", 2)):
        lines = lax.all_to_all(field, axis, split_axis=3, concat_axis=dim, tiled=True)
        lines = minplus_lines(lines, dim, KERNEL)
        field = lax.all_to_all(lines, axis, split_axis=dim, concat_axis=3, tiled=True)
    return current, field


def pack_kernel(share, zl, yl, lev_hbm, ct_hbm, out_hbm, lev, ct_ref, up_ref, down_ref, side_ref,
                stage, lines, turned, picture, out_ref, sems):
    width = lev.shape[1]
    parts = width // share
    blocks = width // LANES
    halo, quarter = share + 4, (share + 4) // 4
    chunk = halo + quarter
    count = LEVELS * zl
    tile = zl * yl
    arriving = [pltpu.make_async_copy(ct_hbm, ct_ref, sems.at[0])]
    for b in range(blocks):
        here = stage.at[pl.ds(b * LANES, LANES), :]
        source = lev_hbm.at[:, pl.ds(b * LANES, LANES)]
        arriving.append(pltpu.make_async_copy(source, here, sems.at[1 + b]))
    whole = pltpu.make_async_copy(lev_hbm, lev, sems.at[1 + 2 * blocks])
    for copy in arriving + [whole]:
        copy.start()
    lines[pl.ds(0, 8), :] = jnp.zeros((8, LANES), jnp.float32)
    lines[pl.ds(8 + width, 8), :] = jnp.zeros((8, LANES), jnp.float32)

    arriving[0].wait()
    across = jnp.concatenate([ct_ref[:, b * LANES:(b + 1) * LANES] for b in range(blocks)], axis=0).T
    for n in range(blocks):
        turn = lambda rows, by: pltpu.roll(rows, by % blocks * tile, 1) if by % blocks else rows
        turned[n, pl.ds(0, 8), :] = turn(across[LANES - 8:], n + 1)
        turned[n, pl.ds(8, LANES), :] = turn(across, n)
        turned[n, pl.ds(8 + LANES, 8), :] = turn(across[:8], n - 1)
    group = lax.broadcasted_iota(jnp.int32, (8, LANES), 1) // tile
    each = LANES // share
    for r in range(parts):
        b, at = r // each, 8 + r % each * share - 2
        value = None
        for t in range(4):
            run = turned[(t - b) % blocks, pl.ds(at + quarter * t, 8), :]
            value = run if value is None else jnp.where(group >= t, run, value)
        picture[pl.ds(8 * r, 8), :] = value
    leaving = []
    sub = lax.broadcasted_iota(jnp.int32, (8, LANES), 0)

    def out_tile(tile):
        value = None
        for r in range(8 * tile // chunk, min((8 * tile + 7) // chunk + 1, parts)):
            for source, begin, length, origin in (
                (picture, r * chunk, quarter, 8 * r),
                (lines, r * chunk + quarter, halo, 6 + r * share),
            ):
                if begin + length <= 8 * tile or begin >= 8 * tile + 8:
                    continue
                piece = source[pl.ds(8 * tile - begin + origin, 8), :]
                value = piece if value is None else jnp.where(sub >= begin - 8 * tile, piece, value)
        return value

    start = 0
    for b in range(blocks):
        arriving[1 + b].wait()
        block = [stage[pl.ds(b * LANES + y, count, stride=yl), :] for y in range(yl)]
        lines[pl.ds(8 + b * LANES, LANES), :] = jnp.concatenate(block, axis=0).T
        known = parts if b + 1 == blocks else (b + 1) * LANES // share - 1
        stop = known * chunk // 8 * 8
        for tile in range(start // 8, stop // 8):
            out_ref[pl.ds(8 * tile, 8), :] = out_tile(tile)
        rows = pl.ds(start, stop - start)
        leaving.append(
            pltpu.make_async_copy(out_ref.at[rows, :], out_hbm.at[rows, :], sems.at[1 + blocks + b])
        )
        leaving[-1].start()
        start = stop
    whole.wait()
    plane = zl * yl
    for k in range(LEVELS):
        at = pl.ds(2 * k * yl, 2 * yl)
        up_ref[at, :] = lev[pl.ds((k + 1) * plane - 2 * yl, 2 * yl), :]
        down_ref[at, :] = lev[pl.ds(k * plane, 2 * yl), :]
    at = pl.ds(2 * LEVELS * yl, yl)
    up_ref[at, :] = ct_ref[pl.ds(plane - yl, yl), :]
    down_ref[at, :] = ct_ref[pl.ds(0, yl), :]
    upper = lax.axis_index("gy") == 0
    near = jnp.where(upper, yl - 1, 0)
    next_near = jnp.where(upper, yl - 2, 1)
    for k in range(LEVELS):
        for z in range(zl):
            base = k * plane + z * yl
            side_ref[pl.ds(2 * zl * k + z, 1), :] = lev[pl.ds(base + near, 1), :]
            side_ref[pl.ds(2 * zl * k + zl + z, 1), :] = lev[pl.ds(base + next_near, 1), :]
    for z in range(zl):
        side_ref[pl.ds(2 * zl * LEVELS + z, 1), :] = ct_ref[pl.ds(z * yl + near, 1), :]
    for copy in leaving:
        copy.wait()


HALF_ANGLE = (
    0.6366196870803833, -0.21219870448112488, 0.12714172899723053, -0.0893140509724617,
    0.06329755485057831, -0.03813650459051132, 0.015633534640073776, -0.0030433274805545807,
)


def heaviside_and_rate(u):
    s = 1.0 + u * u
    q = lax.rsqrt(s)
    r = u / (1.0 + s * q)
    y = r * r
    p = HALF_ANGLE[-1]
    for c in HALF_ANGLE[-2::-1]:
        p = p * y + c
    return 0.5 + r * p, (q * q) * (STEP_SIZE / math.pi)


def cost_of(d):
    return float(np.float32(PENALTY) * np.float32(d * d))


def tables_kernel(gy, zl, yl, mean_ref, coef_ref, ypen):
    lane = lax.broadcasted_iota(jnp.int32, (1, LANES), 1)
    level = lane // zl % LEVELS
    y = lane // (LEVELS * zl)

    def mean_of(bits, own):
        value = jnp.zeros((1, LANES), jnp.float32)
        for k in range(LEVELS):
            phase = own << k
            for n in range(3):
                phase |= (bits >> n & 1) << ((k + 1 + n) % LEVELS)
            value = jnp.where(level == k, mean_ref[phase], value)
        return value

    slope, const = [], []
    for bits in range(8):
        low, high = mean_of(bits, 0), mean_of(bits, 1)
        slope.append(-2.0 * (high - low))
        const.append((high - low) * (high + low))
    for n in range(3):
        for bits in range(8):
            if bits >> n & 1:
                slope[bits] = slope[bits] - slope[bits ^ (1 << n)]
                const[bits] = const[bits] - const[bits ^ (1 << n)]
    for n in range(8):
        coef_ref[pl.ds(n, 1), :] = slope[n]
        coef_ref[pl.ds(8 + n, 1), :] = const[n]

    for gap in range(-(gy - 1), gy):
        for turn in range(yl):
            d = (yl * gap + y - (y + turn) % yl).astype(jnp.float32)
            pen = jnp.where(jnp.abs(d) <= KERNEL, PENALTY * (d * d), FAR)
            ypen[pl.ds(8 * ((gap + gy - 1) * yl + turn), 8), :] = jnp.broadcast_to(pen, (8, LANES))


SLOT = 32


def middle_kernel(share, gz, gy, zl, yl, coef_ref, ypen, in_ref, out_ref, levels, picture,
                  first, evolved, shifted, zdone, done, kept, sems):
    parts = gz * gy
    halo, quarter = share + 4, (share + 4) // 4
    chunk = halo + quarter
    tile = zl * yl
    deep = gz + 2
    me = lax.axis_index("gy") * gz + lax.axis_index("gz")

    lane = lax.broadcasted_iota(jnp.int32, (1, LANES), 1)
    level = lane // zl % LEVELS
    z = lane % zl
    y = lane // (LEVELS * zl)

    def moved(value, index):
        return jnp.take_along_axis(
            value, jnp.broadcast_to(index, value.shape), axis=1, mode="promise_in_bounds"
        )

    def z_turned(value, turn):
        return moved(value, lane + (z + turn) % zl - z)

    def level_turned(value, turn):
        return moved(value, lane + ((level + turn) % LEVELS - level) * zl)

    def y_turned(value, turn):
        return pltpu.roll(value, LANES - turn * LEVELS * zl, 1)

    def stacked(blocks):
        return jnp.concatenate(blocks, axis=0)

    def row_of(a, b, x):
        return (b * deep + a + 1) * SLOT + 8 + x

    zero = jnp.zeros((SLOT, LANES), jnp.float32)
    for b in range(gy):
        for a in (-1, gz):
            levels[pl.ds(row_of(a, b, -8), SLOT), :] = zero
            first[pl.ds(row_of(a, b, -8), SLOT), :] = zero
        for a in range(gz):
            source = (b * gz + a) * chunk + quarter
            levels[pl.ds(row_of(a, b, -2), halo), :] = in_ref[pl.ds(source, halo), :]
        for a in range(0, gz, 4):
            batch = range(a, a + 4)
            packed = stacked([in_ref[pl.ds((b * gz + n) * chunk, 8), :] for n in batch])
            for t in range(4):
                run = moved(packed, t * tile + z * yl + y)
                for n in batch:
                    at = 8 * (n - a)
                    rows = pl.ds(row_of(n, b, t * quarter - 2), quarter)
                    picture[rows, :] = run[at:at + quarter]

    coefs = [coef_ref[pl.ds(n, 1), :] for n in range(16)]
    slope, const = coefs[:8], coefs[8:]

    def step(read, tiles, f):
        def beside(dz, dy):
            none = jnp.zeros_like(read(0, 0, 0))
            return stacked([
                read(a + dz, b + dy, 0) if 0 <= b + dy < gy else none for a, b in tiles
            ])

        here = beside(0, 0)
        h, rate = heaviside_and_rate(here)
        near = stacked([read(a, b, -1) + read(a, b, 1) for a, b in tiles]) - 6.0 * here
        near = near + z_turned(jnp.where(z == 0, beside(1, 0), here), 1)
        near = near + z_turned(jnp.where(z == zl - 1, beside(-1, 0), here), zl - 1)
        near = near + y_turned(jnp.where(y == 0, beside(0, 1), here), 1)
        near = near + y_turned(jnp.where(y == yl - 1, beside(0, -1), here), yl - 1)
        h1, h2, h3 = (level_turned(h, turn) for turn in (1, 2, 3))
        g = lambda bits: f(bits) + h1 * f(bits | 1)
        force = (g(0) + h2 * g(2)) + h3 * (g(4) + h2 * g(6))
        return here + rate * (near - force)

    def run_of(ref):
        return lambda a, b, dx: ref[pl.ds(row_of(a, b, dx), share), :]

    def terms(pic):
        return lambda bits: slope[bits] * pic + const[bits]

    for x, outside in ((-1, me == 0), (share, me == parts - 1)):
        across = lambda ref, a, b, dx: ref[pl.ds(row_of(a, b, x + dx), gz, stride=SLOT), :]
        rows = [(0, b) for b in range(gy)]
        pic = stacked([across(picture, 0, b, 0) for _, b in rows])
        value = step(lambda a, b, dx: across(levels, a, b, dx), rows, terms(pic))
        value = jnp.where(outside, 0.0, value)
        for b in range(gy):
            first[pl.ds(row_of(0, b, x), gz, stride=SLOT), :] = value[b * gz:(b + 1) * gz]
    batches = [[(a + n, b) for n in range(4)] for b in range(gy) for a in range(0, gz, 4)]
    for tiles in batches:
        pic = stacked([run_of(picture)(a, b, 0) for a, b in tiles])
        f = [terms(pic)(bits) for bits in range(8)]
        at = pl.ds((tiles[0][1] * gz + tiles[0][0]) * share, 4 * share)
        for bits in range(8):
            kept[bits, at, :] = f[bits]
        value = step(run_of(levels), tiles, lambda bits: f[bits])
        for n, (a, b) in enumerate(tiles):
            first[pl.ds(row_of(a, b, 0), share), :] = value[n * share:(n + 1) * share]

    def block_of(a, b):
        return (b * deep + a + 1) * share

    far = jnp.full((share, LANES), FAR, jnp.float32)
    for b in range(gy):
        for a in (-1, gz):
            evolved[pl.ds(block_of(a, b), share), :] = far
    for tiles in batches:
        at = pl.ds((tiles[0][1] * gz + tiles[0][0]) * share, 4 * share)
        f = lambda bits: kept[bits, at, :]
        evolved[pl.ds(block_of(*tiles[0]), 4 * share), :] = step(run_of(first), tiles, f)

    for b in range(gy):
        for a in range(-1, gz, 4):
            count = min(4, gz - a) * share
            here = evolved[pl.ds(block_of(a, b), count), :]
            above = evolved[pl.ds(block_of(a + 1, b), count), :]
            for turn in range(1, zl):
                value = z_turned(jnp.where(z < turn, above, here), turn)
                shifted[turn - 1, pl.ds(block_of(a, b), count), :] = value

    def z_unit(half, b, low):
        count = 8

        def at(d, n):
            a, turn = low + n + d // zl, d % zl
            if a < (-1 if turn else 0) or a >= gz:
                return None
            if (a, turn) not in loaded:
                rows = pl.ds(block_of(a, b) + 8 * half, 8)
                loaded[a, turn] = shifted[turn - 1, rows, :] if turn else evolved[rows, :]
            return loaded[a, turn]

        loaded = {}
        best = [at(0, n) for n in range(count)]
        for turn in range(zl):
            loaded = {}
            for d in range(turn or zl, min(gz * zl, KERNEL + 1), zl):
                for n in range(count):
                    pair = [v for v in (at(d, n), at(-d, n)) if v is not None]
                    if pair:
                        value = pair[0] if len(pair) == 1 else jnp.minimum(pair[0], pair[1])
                        best[n] = jnp.minimum(best[n], value + cost_of(d))
        for n in range(count):
            zdone[pl.ds((b * gz + low + n) * share + 8 * half, 8), :] = best[n]

    def y_unit(half, low):
        count = 4
        best = [None] * gy
        for other in range(gy):
            starts = [(other * gz + low + n) * share + 8 * half for n in range(count)]
            whole = stacked([zdone[pl.ds(at, 8), :] for at in starts])
            for turn in range(yl):
                value = y_turned(whole, turn) if turn else whole
                for b in range(gy):
                    at = (b - other + gy - 1) * yl + turn
                    new = value + stacked([ypen[pl.ds(8 * at, 8), :]] * count)
                    best[b] = new if best[b] is None else jnp.minimum(best[b], new)
        for b in range(gy):
            for n in range(count):
                rows = pl.ds((b * gz + low + n) * share + 8 * half, 8)
                done[rows, :] = best[b][8 * n:8 * n + 8]

    halves = share // 8
    copies = []
    for half in range(halves + 1):
        z_units = [(b, low) for b in range(gy) for low in range(0, gz, 8)] if half < halves else []
        y_units = list(range(0, gz, 4)) if half else []
        for n in range(max(len(z_units), len(y_units))):
            if n < len(z_units):
                z_unit(half, *z_units[n])
            if n < len(y_units):
                y_unit(half - 1, y_units[n])
                if half == halves:
                    for b in range(gy):
                        rows = pl.ds((b * gz + y_units[n]) * share, 4 * share)
                        sem = sems.at[len(copies)]
                        copies.append(pltpu.make_async_copy(done.at[rows, :], out_ref.at[rows, :], sem))
                        copies[-1].start()
    for copy in copies:
        copy.wait()


def finish_kernel(yl, in_ref, reg_ref, edge, done, sems):
    width = in_ref.shape[0]
    count = width // 8
    group = 8
    far = jnp.full((8, LANES), FAR, jnp.float32)
    edge[pl.ds(0, 8), :] = far
    edge[pl.ds(8, 8), :] = in_ref[pl.ds(0, 8), :]
    edge[pl.ds(16, 8), :] = in_ref[pl.ds(width - 8, 8), :]
    edge[pl.ds(24, 8), :] = far

    def rows(at):
        if at < 0:
            return edge[pl.ds(8 + at, 8), :]
        if at > width - 8:
            return edge[pl.ds(16 + at - (width - 8), 8), :]
        return in_ref[pl.ds(at, 8), :]

    copies = []
    for c in range(width // LANES):
        for low in range(c * LANES // 8, (c + 1) * LANES // 8, group):
            best = [rows(8 * (low + n)) for n in range(group)]
            for rho in range(1, 9):
                plus, minus = {}, {}
                for e in range((KERNEL - rho) // 8 + 1):
                    cost = cost_of(8 * e + rho)
                    for n in range(group):
                        up, down = low + n + e, low + n - e
                        pair = []
                        if 8 * up + rho < width:
                            if up not in plus:
                                plus[up] = rows(8 * up + rho)
                            pair.append(plus[up])
                        if 8 * down - rho > -8:
                            if down not in minus:
                                minus[down] = rows(8 * down - rho)
                            pair.append(minus[down])
                        if not pair:
                            continue
                        value = pair[0] if len(pair) == 1 else jnp.minimum(pair[0], pair[1])
                        best[n] = jnp.minimum(best[n], value + cost)
            for n in range(group):
                done[pl.ds(8 * (low + n), 8), :] = best[n]
        cols = pl.ds(c * LANES, LANES)
        block = done[cols, :].T
        each = LANES // yl
        for y in range(yl):
            done[pl.ds(c * LANES + y, each, stride=yl), :] = block[y * each:(y + 1) * each]
        copies.append(pltpu.make_async_copy(done.at[cols, :], reg_ref.at[:, cols], sems.at[c]))
        copies[-1].start()
    for copy in copies:
        copy.wait()


def corners_kernel(yl, low_ref, high_ref, corner_ref):
    near = jnp.where(lax.axis_index("gy") == 0, yl - 1, 0)
    rows = [low_ref[pl.ds((2 * k + 1) * yl + near, 1), :] for k in range(LEVELS)]
    rows += [high_ref[pl.ds(2 * k * yl + near, 1), :] for k in range(LEVELS)]
    corner_ref[...] = jnp.concatenate(rows, axis=0)


def tile_tools(mean_ref, yl, width):
    upper = lax.axis_index("gy") == 0

    const = [mean_ref[p] * mean_ref[p] for p in range(PHASES)]
    slope = [-2.0 * mean_ref[p] for p in range(PHASES)]
    for k in range(LEVELS):
        for p in range(PHASES):
            if p >> k & 1:
                const[p] = const[p] - const[p ^ (1 << k)]
                slope[p] = slope[p] - slope[p ^ (1 << k)]

    def forces(h, pic):
        c = [None] + [slope[p] * pic + const[p] for p in range(1, PHASES)]
        out = []
        for k in range(LEVELS):
            others = [n for n in range(LEVELS) if n != k]
            part = [c[1 << k | sum((bits >> i & 1) << n for i, n in enumerate(others))]
                    for bits in range(8)]
            for n in others:
                part = [part[i] + h[n] * part[i + 1] for i in range(0, len(part), 2)]
            out.append(part[0])
        return out

    column = lax.broadcasted_iota(jnp.int32, (8, width), 1)
    sub = lax.broadcasted_iota(jnp.int32, (8, width), 0)

    def along_x(u):
        left = jnp.where(column == 0, 0.0, pltpu.roll(u, 1, 1))
        right = jnp.where(column == width - 1, 0.0, pltpu.roll(u, width - 1, 1))
        return left + right

    def advance(here, near, pic):
        pairs = [heaviside_and_rate(u) for u in here]
        force = forces([h for h, _ in pairs], pic)
        return [
            u + rate * (n - 6.0 * u - f)
            for u, n, (_, rate), f in zip(here, near, pairs, force)
        ]

    def along_y(u, row):
        row_up = jnp.where(upper, row, 0.0)
        row_down = jnp.where(upper, 0.0, row)
        above = jnp.where(sub == yl - 1, row_up, pltpu.roll(u, yl - 1, 0))
        below = jnp.where(sub == 0, row_down, pltpu.roll(u, 1, 0))
        return above + below

    return advance, along_x, along_y


def add_neighbours(lev_ref, low_ref, high_ref, zl, yl):
    def level(k, z):
        if z < 0:
            return low_ref[pl.ds((2 * k + 2 + z) * yl, yl), :]
        if z >= zl:
            return high_ref[pl.ds((2 * k + z - zl) * yl, yl), :]
        return lev_ref[pl.ds((k * zl + z) * yl, yl), :]

    return level


def inner_kernel(zl, yl, mean_ref, lev_ref, ct_ref, low_ref, high_ref, side_ref, out_ref):
    advance, along_x, along_y = tile_tools(mean_ref, yl, lev_ref.shape[1])
    level = add_neighbours(lev_ref, low_ref, high_ref, zl, yl)
    for z in range(zl):
        here = [level(k, z) for k in range(LEVELS)]
        near = [
            level(k, z - 1) + level(k, z + 1) + along_x(here[k])
            + along_y(here[k], side_ref[pl.ds(2 * zl * k + z, 1), :])
            for k in range(LEVELS)
        ]
        value = advance(here, near, ct_ref[pl.ds(z * yl, yl), :])
        for k in range(LEVELS):
            out_ref[pl.ds((k * zl + z) * yl, yl), :] = value[k]


def outer_kernel(zl, yl, gz, mean_ref, lev_ref, ct_ref, low_ref, high_ref, side_ref,
                 corner_ref, inner_ref, out_ref, outer, strip, around, strip_first):
    at_z = lax.axis_index("gz")
    edge = jnp.where(lax.axis_index("gy") == 0, yl - 1, 0)
    plane = zl * yl
    advance, along_x, along_y = tile_tools(mean_ref, yl, lev_ref.shape[1])
    level = add_neighbours(lev_ref, low_ref, high_ref, zl, yl)

    def side(k, z):
        if z < 0:
            return corner_ref[pl.ds(k, 1), :]
        if z >= zl:
            return corner_ref[pl.ds(LEVELS + k, 1), :]
        return side_ref[pl.ds(2 * zl * k + z, 1), :]

    picture_at = pl.ds(2 * LEVELS * yl, yl)
    for n, (z, kept, pic) in enumerate((
        (-1, at_z > 0, low_ref[picture_at, :]), (zl, at_z < gz - 1, high_ref[picture_at, :])
    )):
        here = [level(k, z) for k in range(LEVELS)]
        near = [
            level(k, z - 1) + level(k, z + 1) + along_x(here[k]) + along_y(here[k], side(k, z))
            for k in range(LEVELS)
        ]
        value = advance(here, near, pic)
        for k in range(LEVELS):
            outer[pl.ds((2 * k + n) * yl, yl), :] = jnp.where(kept, value[k], 0.0)

    strip[...] = jnp.zeros_like(strip)
    around[...] = jnp.zeros_like(around)
    for k in range(LEVELS):
        for z in range(-1, zl + 1):
            strip[pl.ds(8 * k + z + 1, 1), :] = side(k, z)
        for z in range(zl):
            around[pl.ds(8 * k + z + 1, 1), :] = (
                lev_ref[pl.ds(k * plane + z * yl + edge, 1), :]
                + side_ref[pl.ds(2 * zl * k + zl + z, 1), :]
            )
    for z in range(zl):
        strip[pl.ds(8 * LEVELS + z + 1, 1), :] = side_ref[pl.ds(2 * zl * LEVELS + z, 1), :]
    here = [strip[pl.ds(8 * k, 8), :] for k in range(LEVELS)]
    near = [
        pltpu.roll(u, 7, 0) + pltpu.roll(u, 1, 0) + along_x(u) + around[pl.ds(8 * k, 8), :]
        for k, u in enumerate(here)
    ]
    value = advance(here, near, strip[pl.ds(8 * LEVELS, 8), :])
    for k in range(LEVELS):
        strip_first[pl.ds(8 * k, 8), :] = value[k]

    def after(k, z):
        if z < 0 or z >= zl:
            return outer[pl.ds((2 * k + (z >= zl)) * yl, yl), :]
        return inner_ref[pl.ds((k * zl + z) * yl, yl), :]

    for z in range(zl):
        here = [after(k, z) for k in range(LEVELS)]
        near = [
            after(k, z - 1) + after(k, z + 1) + along_x(here[k])
            + along_y(here[k], strip_first[pl.ds(8 * k + z + 1, 1), :])
            for k in range(LEVELS)
        ]
        value = advance(here, near, ct_ref[pl.ds(z * yl, yl), :])
        for k in range(LEVELS):
            out_ref[pl.ds(k * plane + z * yl, yl), :] = value[k]


def split_body(levels, ct_image, region_means):
    gz, gy = lax.axis_size("gz"), lax.axis_size("gy")
    _, zl, yl, width = levels.shape
    parts = gz * gy
    share = width // parts
    halo, quarter = share + 4, (share + 4) // 4
    chunk = halo + quarter
    f32 = jnp.float32
    vmem = pl.BlockSpec(memory_space=pltpu.VMEM)
    smem = pl.BlockSpec(memory_space=pltpu.SMEM)
    anywhere = pl.BlockSpec(memory_space=pl.ANY)
    params = pltpu.CompilerParams(vmem_limit_bytes=24 * 1024 * 1024)
    scratch = lambda *dims: pltpu.VMEM(dims, f32)
    shape = lambda rows: jax.ShapeDtypeStruct((rows, width), f32)
    message = (2 * LEVELS + 1) * yl
    packed, lines, image, up, down, side = pl.pallas_call(
        functools.partial(pack_kernel, share, zl, yl),
        out_shape=(
            jax.ShapeDtypeStruct((parts * chunk, LANES), f32),
            shape(LANES), shape(zl * yl), shape(message), shape(message),
            shape(2 * zl * LEVELS + zl),
        ),
        in_specs=[pl.BlockSpec(memory_space=pltpu.HBM)] * 2,
        out_specs=(anywhere,) + (vmem,) * 5,
        scratch_shapes=[
            scratch(width + 8, LANES),
            scratch(width + 16, LANES),
            scratch(4, LANES + 16, LANES),
            scratch(8 * parts + 8, LANES),
            scratch(parts * chunk, LANES),
            pltpu.SemaphoreType.DMA((2 + 2 * width // LANES,)),
        ],
        compiler_params=params,
        name="pack",
    )(
        pltpu.with_memory_space_constraint(levels.reshape(LANES, width), pltpu.HBM),
        pltpu.with_memory_space_constraint(ct_image.reshape(zl * yl, width), pltpu.HBM),
    )
    arrived = lax.all_to_all(
        packed.reshape(parts, chunk, 1, LANES), ("gy", "gz"), split_axis=0, concat_axis=0, tiled=True
    ).reshape(parts * chunk, LANES)

    low = lax.ppermute(up, "gz", [(i, i + 1) for i in range(gz - 1)])
    high = lax.ppermute(down, "gz", [(i + 1, i) for i in range(gz - 1)])
    side = lax.ppermute(side, "gy", [(0, 1), (1, 0)])

    lanes = lambda rows: jax.ShapeDtypeStruct((rows, LANES), f32)
    coefs, penalties = pl.pallas_call(
        functools.partial(tables_kernel, gy, zl, yl),
        out_shape=(lanes(16), lanes(8 * yl * (2 * gy - 1))),
        in_specs=[smem],
        out_specs=(vmem, vmem),
        compiler_params=params,
        name="tables",
    )(region_means)
    slots = (gy * (gz + 2) + 1) * SLOT
    blocks = gy * (gz + 2) * share
    passed = pl.pallas_call(
        functools.partial(middle_kernel, share, gz, gy, zl, yl),
        out_shape=jax.ShapeDtypeStruct((width, LANES), f32),
        in_specs=[vmem] * 3,
        out_specs=anywhere,
        scratch_shapes=[
            scratch(slots, LANES),
            scratch(slots, LANES),
            scratch(slots, LANES),
            scratch(blocks, LANES),
            scratch(zl - 1, blocks, LANES),
            scratch(width, LANES),
            scratch(width, LANES),
            scratch(8, width, LANES),
            pltpu.SemaphoreType.DMA((gy * gz // 4,)),
        ],
        compiler_params=params,
        name="middle",
    )(coefs, penalties, arrived)
    passed, low, high, side = lax.optimization_barrier((passed, low, high, side))
    passed = lax.all_to_all(
        passed.reshape(parts, share, LANES), ("gy", "gz"), split_axis=0, concat_axis=0, tiled=True
    ).reshape(width, LANES)

    corner = pl.pallas_call(
        functools.partial(corners_kernel, yl),
        out_shape=shape(2 * LEVELS),
        in_specs=[vmem, vmem],
        out_specs=vmem,
        compiler_params=params,
        name="corners",
    )(low, high)
    corner = lax.ppermute(corner, "gy", [(0, 1), (1, 0)])
    cost = pl.CostEstimate(flops=5_000_000, bytes_accessed=1_000_000, transcendentals=0)
    inner = pl.pallas_call(
        functools.partial(inner_kernel, zl, yl),
        out_shape=shape(LANES),
        in_specs=[smem] + [vmem] * 5,
        out_specs=vmem,
        compiler_params=params,
        cost_estimate=cost,
        name="inner",
    )(region_means, lines, image, low, high, side)
    evolved = pl.pallas_call(
        functools.partial(outer_kernel, zl, yl, gz),
        out_shape=shape(LANES),
        in_specs=[smem] + [vmem] * 7,
        out_specs=vmem,
        scratch_shapes=[
            scratch(2 * LEVELS * yl, width),
            scratch(8 * (LEVELS + 1), width),
            scratch(8 * LEVELS, width),
            scratch(8 * LEVELS, width),
        ],
        compiler_params=params,
        cost_estimate=cost,
        name="outer",
    )(region_means, lines, image, low, high, side, corner, inner)

    regularized = pl.pallas_call(
        functools.partial(finish_kernel, yl),
        out_shape=shape(LANES),
        in_specs=[vmem],
        out_specs=anywhere,
        scratch_shapes=[
            scratch(32, LANES),
            scratch(width + 8, LANES),
            pltpu.SemaphoreType.DMA((width // LANES,)),
        ],
        compiler_params=params,
        name="finish",
    )(passed)
    return evolved.reshape(levels.shape), regularized.reshape(levels.shape)


def body(levels, ct_image, region_means):
    gz, gy = lax.axis_size("gz"), lax.axis_size("gy")
    parts = gz * gy
    count, zl, yl, width = levels.shape
    fits = count == LEVELS and count * zl * yl == LANES and yl == 8 and zl >= 2
    fits = fits and gy == 2 and gz % 8 == 0 and gz * zl <= KERNEL
    fits = fits and width == 4 * LANES and parts == 32
    if fits:
        return split_body(levels, ct_image, region_means)
    return portable_body(levels, ct_image, region_means)


def solution(mesh):
    return jax.shard_map(
        body,
        mesh=mesh,
        in_specs=(P(None, "gz", "gy", None), P("gz", "gy", None), P()),
        out_specs=(P(None, "gz", "gy", None), P(None, "gz", "gy", None)),
        check_vma=False,
    )
```

```python
import functools
import math

import jax
import jax.numpy as jnp
import numpy as np
from jax import lax
from jax.experimental import pallas as pl
from jax.experimental.pallas import tpu as pltpu
from jax.sharding import PartitionSpec as P

LEVELS = 4
PHASES = 16
UPDATES = 2
KERNEL = 200
LANES = 128


PENALTY = 0.0005
STEP_SIZE = 0.5
FAR = 1e30


def with_halo(block, sides, width):
    for axis, dim in sides:
        count = lax.axis_size(axis)
        forward = [(i, i + 1) for i in range(count - 1)]
        backward = [(target, source) for source, target in forward]
        low = lax.ppermute(
            lax.slice_in_dim(block, block.shape[dim] - width, None, axis=dim), axis, forward
        )
        high = lax.ppermute(lax.slice_in_dim(block, 0, width, axis=dim), axis, backward)
        block = jnp.concatenate([low, block, high], axis=dim)
    return block


def evolve(level_pad, picture, region_means):
    interior = level_pad[:, 1:-1, 1:-1, :]
    side_x = jnp.pad(interior, ((0, 0), (0, 0), (0, 0), (1, 1)))
    laplace = level_pad[:, 2:, 1:-1, :] + level_pad[:, :-2, 1:-1, :]
    laplace = laplace + level_pad[:, 1:-1, 2:, :] + level_pad[:, 1:-1, :-2, :]
    laplace = laplace + side_x[..., 2:] + side_x[..., :-2] - 6.0 * interior
    heaviside = 0.5 + jnp.arctan(interior) / math.pi
    delta_term = 1.0 / (math.pi * (1.0 + interior * interior))
    forces = [jnp.zeros_like(interior[0]) for level_id in range(LEVELS)]
    for phase_id in range(PHASES):
        differ = picture - region_means[phase_id]
        energy = differ * differ
        factors = []
        for level_id in range(LEVELS):
            if phase_id >> level_id & 1:
                factors.append(heaviside[level_id])
            else:
                factors.append(1.0 - heaviside[level_id])
        for level_id in range(LEVELS):
            sign_value = 1.0 if phase_id >> level_id & 1 else -1.0
            others = energy
            for other_id in range(LEVELS):
                if other_id != level_id:
                    others = others * factors[other_id]
            forces[level_id] = forces[level_id] + sign_value * others
    force_all = jnp.stack(forces, axis=0)
    return interior + STEP_SIZE * delta_term * (laplace - force_all)


def minplus_lines(field_in, line_axis, kernel_reach):
    moved_field = jnp.moveaxis(field_in, line_axis, -1)
    line_shape = moved_field.shape
    line_len = line_shape[-1]
    line_rows = moved_field.reshape(-1, line_len)
    row_count = line_rows.shape[0]
    positions = jnp.arange(line_len, dtype=jnp.float32)
    distance = positions[:, None] - positions[None, :]
    penalty_table = jnp.where(
        jnp.abs(distance) <= kernel_reach, PENALTY * (distance * distance), jnp.inf
    )
    row_limit = max(1, 1048576 // (line_len * line_len))
    row_block = 1
    while row_block * 2 <= row_limit and row_count % (row_block * 2) == 0:
        row_block = row_block * 2
    grouped = line_rows.reshape(row_count // row_block, row_block, line_len)

    def block_min(block_rows):
        return jnp.min(block_rows[:, None, :] + penalty_table[None, :, :], axis=2)

    result_rows = lax.map(block_min, grouped)
    return jnp.moveaxis(result_rows.reshape(line_shape), -1, line_axis)


def portable_body(levels, ct_image, region_means):
    current = levels
    for _ in range(UPDATES):
        padded = with_halo(current, (("gz", 1), ("gy", 2)), 1)
        current = evolve(padded, ct_image, region_means)
    field = minplus_lines(current, 3, KERNEL)
    for axis, dim in (("gz", 1), ("gy", 2)):
        lines = lax.all_to_all(field, axis, split_axis=3, concat_axis=dim, tiled=True)
        lines = minplus_lines(lines, dim, KERNEL)
        field = lax.all_to_all(lines, axis, split_axis=dim, concat_axis=3, tiled=True)
    return current, field


def pack_kernel(share, zl, yl, lev_hbm, ct_hbm, out_hbm, lev, ct_ref, up_ref, down_ref, side_ref,
                stage, lines, turned, picture, out_ref, sems):
    width = lev.shape[1]
    parts = width // share
    blocks = width // LANES
    halo, quarter = share + 4, (share + 4) // 4
    chunk = halo + quarter
    count = LEVELS * zl
    tile = zl * yl
    arriving = [pltpu.make_async_copy(ct_hbm, ct_ref, sems.at[0])]
    for b in range(blocks):
        here = stage.at[pl.ds(b * LANES, LANES), :]
        source = lev_hbm.at[:, pl.ds(b * LANES, LANES)]
        arriving.append(pltpu.make_async_copy(source, here, sems.at[1 + b]))
    for copy in arriving:
        copy.start()
    lines[pl.ds(0, 8), :] = jnp.zeros((8, LANES), jnp.float32)
    lines[pl.ds(8 + width, 8), :] = jnp.zeros((8, LANES), jnp.float32)

    for copy in arriving:
        copy.wait()
    across = jnp.concatenate([ct_ref[:, b * LANES:(b + 1) * LANES] for b in range(blocks)], axis=0).T
    for n in range(blocks):
        turn = lambda rows, by: pltpu.roll(rows, by % blocks * tile, 1) if by % blocks else rows
        turned[n, pl.ds(0, 8), :] = turn(across[LANES - 8:], n + 1)
        turned[n, pl.ds(8, LANES), :] = turn(across, n)
        turned[n, pl.ds(8 + LANES, 8), :] = turn(across[:8], n - 1)
    group = lax.broadcasted_iota(jnp.int32, (8, LANES), 1) // tile
    each = LANES // share
    for r in range(parts):
        b, at = r // each, 8 + r % each * share - 2
        value = None
        for t in range(4):
            run = turned[(t - b) % blocks, pl.ds(at + quarter * t, 8), :]
            value = run if value is None else jnp.where(group >= t, run, value)
        picture[pl.ds(8 * r, 8), :] = value
    for b in range(blocks):
        block = [stage[pl.ds(b * LANES + y, count, stride=yl), :] for y in range(yl)]
        lines[pl.ds(8 + b * LANES, LANES), :] = jnp.concatenate(block, axis=0).T

    leaving = []
    sub = lax.broadcasted_iota(jnp.int32, (8, LANES), 0)

    def out_tile(tile):
        value = None
        for r in range(8 * tile // chunk, min((8 * tile + 7) // chunk + 1, parts)):
            for source, begin, length, origin in (
                (picture, r * chunk, quarter, 8 * r),
                (lines, r * chunk + quarter, halo, 6 + r * share),
            ):
                if begin + length <= 8 * tile or begin >= 8 * tile + 8:
                    continue
                piece = source[pl.ds(8 * tile - begin + origin, 8), :]
                value = piece if value is None else jnp.where(sub >= begin - 8 * tile, piece, value)
        return value

    start = 0
    for b in range(blocks):
        known = parts if b + 1 == blocks else (b + 1) * LANES // share - 1
        stop = known * chunk // 8 * 8
        for tile in range(start // 8, stop // 8):
            out_ref[pl.ds(8 * tile, 8), :] = out_tile(tile)
        rows = pl.ds(start, stop - start)
        leaving.append(
            pltpu.make_async_copy(out_ref.at[rows, :], out_hbm.at[rows, :], sems.at[1 + blocks + b])
        )
        leaving[-1].start()
        start = stop
    for b in range(blocks):
        lev[:, b * LANES:(b + 1) * LANES] = stage[pl.ds(b * LANES, LANES), :]
    plane = zl * yl
    for k in range(LEVELS):
        at = pl.ds(2 * k * yl, 2 * yl)
        up_ref[at, :] = lev[pl.ds((k + 1) * plane - 2 * yl, 2 * yl), :]
        down_ref[at, :] = lev[pl.ds(k * plane, 2 * yl), :]
    at = pl.ds(2 * LEVELS * yl, yl)
    up_ref[at, :] = ct_ref[pl.ds(plane - yl, yl), :]
    down_ref[at, :] = ct_ref[pl.ds(0, yl), :]
    upper = lax.axis_index("gy") == 0
    near = jnp.where(upper, yl - 1, 0)
    next_near = jnp.where(upper, yl - 2, 1)
    for k in range(LEVELS):
        for z in range(zl):
            base = k * plane + z * yl
            side_ref[pl.ds(2 * zl * k + z, 1), :] = lev[pl.ds(base + near, 1), :]
            side_ref[pl.ds(2 * zl * k + zl + z, 1), :] = lev[pl.ds(base + next_near, 1), :]
    for z in range(zl):
        side_ref[pl.ds(2 * zl * LEVELS + z, 1), :] = ct_ref[pl.ds(z * yl + near, 1), :]
    for copy in leaving:
        copy.wait()


HALF_ANGLE = (
    0.6366196870803833, -0.21219870448112488, 0.12714172899723053, -0.0893140509724617,
    0.06329755485057831, -0.03813650459051132, 0.015633534640073776, -0.0030433274805545807,
)


def heaviside_and_rate(u):
    s = 1.0 + u * u
    q = lax.rsqrt(s)
    r = u / (1.0 + s * q)
    y = r * r
    p = HALF_ANGLE[-1]
    for c in HALF_ANGLE[-2::-1]:
        p = p * y + c
    return 0.5 + r * p, (q * q) * (STEP_SIZE / math.pi)


def cost_of(d):
    return float(np.float32(PENALTY) * np.float32(d * d))


def tables_kernel(gy, zl, yl, mean_ref, coef_ref, ypen):
    lane = lax.broadcasted_iota(jnp.int32, (1, LANES), 1)
    level = lane // zl % LEVELS
    y = lane // (LEVELS * zl)

    def mean_of(bits, own):
        value = jnp.zeros((1, LANES), jnp.float32)
        for k in range(LEVELS):
            phase = own << k
            for n in range(3):
                phase |= (bits >> n & 1) << ((k + 1 + n) % LEVELS)
            value = jnp.where(level == k, mean_ref[phase], value)
        return value

    slope, const = [], []
    for bits in range(8):
        low, high = mean_of(bits, 0), mean_of(bits, 1)
        slope.append(-2.0 * (high - low))
        const.append((high - low) * (high + low))
    for n in range(3):
        for bits in range(8):
            if bits >> n & 1:
                slope[bits] = slope[bits] - slope[bits ^ (1 << n)]
                const[bits] = const[bits] - const[bits ^ (1 << n)]
    for n in range(8):
        coef_ref[pl.ds(n, 1), :] = slope[n]
        coef_ref[pl.ds(8 + n, 1), :] = const[n]

    for gap in range(-(gy - 1), gy):
        for turn in range(yl):
            d = (yl * gap + y - (y + turn) % yl).astype(jnp.float32)
            pen = jnp.where(jnp.abs(d) <= KERNEL, PENALTY * (d * d), FAR)
            ypen[pl.ds(8 * ((gap + gy - 1) * yl + turn), 8), :] = jnp.broadcast_to(pen, (8, LANES))


SLOT = 32


def middle_kernel(share, gz, gy, zl, yl, coef_ref, ypen, in_ref, out_ref, levels, picture,
                  first, evolved, shifted, zdone, done, kept, sems):
    parts = gz * gy
    halo, quarter = share + 4, (share + 4) // 4
    chunk = halo + quarter
    tile = zl * yl
    deep = gz + 2
    me = lax.axis_index("gy") * gz + lax.axis_index("gz")

    lane = lax.broadcasted_iota(jnp.int32, (1, LANES), 1)
    level = lane // zl % LEVELS
    z = lane % zl
    y = lane // (LEVELS * zl)

    def moved(value, index):
        return jnp.take_along_axis(
            value, jnp.broadcast_to(index, value.shape), axis=1, mode="promise_in_bounds"
        )

    def z_turned(value, turn):
        return moved(value, lane + (z + turn) % zl - z)

    def level_turned(value, turn):
        return moved(value, lane + ((level + turn) % LEVELS - level) * zl)

    def y_turned(value, turn):
        return pltpu.roll(value, LANES - turn * LEVELS * zl, 1)

    def stacked(blocks):
        return jnp.concatenate(blocks, axis=0)

    def row_of(a, b, x):
        return (b * deep + a + 1) * SLOT + 8 + x

    zero = jnp.zeros((SLOT, LANES), jnp.float32)
    for b in range(gy):
        for a in (-1, gz):
            levels[pl.ds(row_of(a, b, -8), SLOT), :] = zero
            first[pl.ds(row_of(a, b, -8), SLOT), :] = zero
        for a in range(gz):
            source = (b * gz + a) * chunk + quarter
            levels[pl.ds(row_of(a, b, -2), halo), :] = in_ref[pl.ds(source, halo), :]
        for a in range(0, gz, 4):
            batch = range(a, a + 4)
            packed = stacked([in_ref[pl.ds((b * gz + n) * chunk, 8), :] for n in batch])
            for t in range(4):
                run = moved(packed, t * tile + z * yl + y)
                for n in batch:
                    at = 8 * (n - a)
                    rows = pl.ds(row_of(n, b, t * quarter - 2), quarter)
                    picture[rows, :] = run[at:at + quarter]

    coefs = [coef_ref[pl.ds(n, 1), :] for n in range(16)]
    slope, const = coefs[:8], coefs[8:]

    def step(read, tiles, f):
        def beside(dz, dy):
            none = jnp.zeros_like(read(0, 0, 0))
            return stacked([
                read(a + dz, b + dy, 0) if 0 <= b + dy < gy else none for a, b in tiles
            ])

        here = beside(0, 0)
        h, rate = heaviside_and_rate(here)
        near = stacked([read(a, b, -1) + read(a, b, 1) for a, b in tiles]) - 6.0 * here
        near = near + z_turned(jnp.where(z == 0, beside(1, 0), here), 1)
        near = near + z_turned(jnp.where(z == zl - 1, beside(-1, 0), here), zl - 1)
        near = near + y_turned(jnp.where(y == 0, beside(0, 1), here), 1)
        near = near + y_turned(jnp.where(y == yl - 1, beside(0, -1), here), yl - 1)
        h1, h2, h3 = (level_turned(h, turn) for turn in (1, 2, 3))
        g = lambda bits: f(bits) + h1 * f(bits | 1)
        force = (g(0) + h2 * g(2)) + h3 * (g(4) + h2 * g(6))
        return here + rate * (near - force)

    def run_of(ref):
        return lambda a, b, dx: ref[pl.ds(row_of(a, b, dx), share), :]

    def terms(pic):
        return lambda bits: slope[bits] * pic + const[bits]

    for x, outside in ((-1, me == 0), (share, me == parts - 1)):
        across = lambda ref, a, b, dx: ref[pl.ds(row_of(a, b, x + dx), gz, stride=SLOT), :]
        rows = [(0, b) for b in range(gy)]
        pic = stacked([across(picture, 0, b, 0) for _, b in rows])
        value = step(lambda a, b, dx: across(levels, a, b, dx), rows, terms(pic))
        value = jnp.where(outside, 0.0, value)
        for b in range(gy):
            first[pl.ds(row_of(0, b, x), gz, stride=SLOT), :] = value[b * gz:(b + 1) * gz]
    batches = [[(a + n, b) for n in range(4)] for b in range(gy) for a in range(0, gz, 4)]
    for tiles in batches:
        pic = stacked([run_of(picture)(a, b, 0) for a, b in tiles])
        f = [terms(pic)(bits) for bits in range(8)]
        at = pl.ds((tiles[0][1] * gz + tiles[0][0]) * share, 4 * share)
        for bits in range(8):
            kept[bits, at, :] = f[bits]
        value = step(run_of(levels), tiles, lambda bits: f[bits])
        for n, (a, b) in enumerate(tiles):
            first[pl.ds(row_of(a, b, 0), share), :] = value[n * share:(n + 1) * share]

    def block_of(a, b):
        return (b * deep + a + 1) * share

    far = jnp.full((share, LANES), FAR, jnp.float32)
    for b in range(gy):
        for a in (-1, gz):
            evolved[pl.ds(block_of(a, b), share), :] = far
    for tiles in batches:
        at = pl.ds((tiles[0][1] * gz + tiles[0][0]) * share, 4 * share)
        f = lambda bits: kept[bits, at, :]
        evolved[pl.ds(block_of(*tiles[0]), 4 * share), :] = step(run_of(first), tiles, f)

    for b in range(gy):
        for a in range(-1, gz, 4):
            count = min(4, gz - a) * share
            here = evolved[pl.ds(block_of(a, b), count), :]
            above = evolved[pl.ds(block_of(a + 1, b), count), :]
            for turn in range(1, zl):
                value = z_turned(jnp.where(z < turn, above, here), turn)
                shifted[turn - 1, pl.ds(block_of(a, b), count), :] = value

    def z_unit(half, b, low):
        count = 8

        def at(d, n):
            a, turn = low + n + d // zl, d % zl
            if a < (-1 if turn else 0) or a >= gz:
                return None
            if (a, turn) not in loaded:
                rows = pl.ds(block_of(a, b) + 8 * half, 8)
                loaded[a, turn] = shifted[turn - 1, rows, :] if turn else evolved[rows, :]
            return loaded[a, turn]

        loaded = {}
        best = [at(0, n) for n in range(count)]
        for turn in range(zl):
            loaded = {}
            for d in range(turn or zl, min(gz * zl, KERNEL + 1), zl):
                for n in range(count):
                    pair = [v for v in (at(d, n), at(-d, n)) if v is not None]
                    if pair:
                        value = pair[0] if len(pair) == 1 else jnp.minimum(pair[0], pair[1])
                        best[n] = jnp.minimum(best[n], value + cost_of(d))
        for n in range(count):
            zdone[pl.ds((b * gz + low + n) * share + 8 * half, 8), :] = best[n]

    def y_unit(half, low):
        count = 4
        best = [None] * gy
        for other in range(gy):
            starts = [(other * gz + low + n) * share + 8 * half for n in range(count)]
            whole = stacked([zdone[pl.ds(at, 8), :] for at in starts])
            for turn in range(yl):
                value = y_turned(whole, turn) if turn else whole
                for b in range(gy):
                    at = (b - other + gy - 1) * yl + turn
                    new = value + stacked([ypen[pl.ds(8 * at, 8), :]] * count)
                    best[b] = new if best[b] is None else jnp.minimum(best[b], new)
        for b in range(gy):
            for n in range(count):
                rows = pl.ds((b * gz + low + n) * share + 8 * half, 8)
                done[rows, :] = best[b][8 * n:8 * n + 8]

    halves = share // 8
    copies = []
    for half in range(halves + 1):
        z_units = [(b, low) for b in range(gy) for low in range(0, gz, 8)] if half < halves else []
        y_units = list(range(0, gz, 4)) if half else []
        for n in range(max(len(z_units), len(y_units))):
            if n < len(z_units):
                z_unit(half, *z_units[n])
            if n < len(y_units):
                y_unit(half - 1, y_units[n])
                if half == halves:
                    for b in range(gy):
                        rows = pl.ds((b * gz + y_units[n]) * share, 4 * share)
                        sem = sems.at[len(copies)]
                        copies.append(pltpu.make_async_copy(done.at[rows, :], out_ref.at[rows, :], sem))
                        copies[-1].start()
    for copy in copies:
        copy.wait()


def finish_kernel(yl, in_ref, reg_ref, edge, done, sems):
    width = in_ref.shape[0]
    count = width // 8
    group = 8
    far = jnp.full((8, LANES), FAR, jnp.float32)
    edge[pl.ds(0, 8), :] = far
    edge[pl.ds(8, 8), :] = in_ref[pl.ds(0, 8), :]
    edge[pl.ds(16, 8), :] = in_ref[pl.ds(width - 8, 8), :]
    edge[pl.ds(24, 8), :] = far

    def rows(at):
        if at < 0:
            return edge[pl.ds(8 + at, 8), :]
        if at > width - 8:
            return edge[pl.ds(16 + at - (width - 8), 8), :]
        return in_ref[pl.ds(at, 8), :]

    copies = []
    for c in range(width // LANES):
        for low in range(c * LANES // 8, (c + 1) * LANES // 8, group):
            best = [rows(8 * (low + n)) for n in range(group)]
            for rho in range(1, 9):
                plus, minus = {}, {}
                for e in range((KERNEL - rho) // 8 + 1):
                    cost = cost_of(8 * e + rho)
                    for n in range(group):
                        up, down = low + n + e, low + n - e
                        pair = []
                        if 8 * up + rho < width:
                            if up not in plus:
                                plus[up] = rows(8 * up + rho)
                            pair.append(plus[up])
                        if 8 * down - rho > -8:
                            if down not in minus:
                                minus[down] = rows(8 * down - rho)
                            pair.append(minus[down])
                        if not pair:
                            continue
                        value = pair[0] if len(pair) == 1 else jnp.minimum(pair[0], pair[1])
                        best[n] = jnp.minimum(best[n], value + cost)
            for n in range(group):
                done[pl.ds(8 * (low + n), 8), :] = best[n]
        cols = pl.ds(c * LANES, LANES)
        block = done[cols, :].T
        each = LANES // yl
        for y in range(yl):
            done[pl.ds(c * LANES + y, each, stride=yl), :] = block[y * each:(y + 1) * each]
        copies.append(pltpu.make_async_copy(done.at[cols, :], reg_ref.at[:, cols], sems.at[c]))
        copies[-1].start()
    for copy in copies:
        copy.wait()


def corners_kernel(yl, low_ref, high_ref, corner_ref):
    near = jnp.where(lax.axis_index("gy") == 0, yl - 1, 0)
    rows = [low_ref[pl.ds((2 * k + 1) * yl + near, 1), :] for k in range(LEVELS)]
    rows += [high_ref[pl.ds(2 * k * yl + near, 1), :] for k in range(LEVELS)]
    corner_ref[...] = jnp.concatenate(rows, axis=0)


def tile_tools(mean_ref, yl, width):
    upper = lax.axis_index("gy") == 0

    const = [mean_ref[p] * mean_ref[p] for p in range(PHASES)]
    slope = [-2.0 * mean_ref[p] for p in range(PHASES)]
    for k in range(LEVELS):
        for p in range(PHASES):
            if p >> k & 1:
                const[p] = const[p] - const[p ^ (1 << k)]
                slope[p] = slope[p] - slope[p ^ (1 << k)]

    def forces(h, pic):
        c = [None] + [slope[p] * pic + const[p] for p in range(1, PHASES)]
        out = []
        for k in range(LEVELS):
            others = [n for n in range(LEVELS) if n != k]
            part = [c[1 << k | sum((bits >> i & 1) << n for i, n in enumerate(others))]
                    for bits in range(8)]
            for n in others:
                part = [part[i] + h[n] * part[i + 1] for i in range(0, len(part), 2)]
            out.append(part[0])
        return out

    column = lax.broadcasted_iota(jnp.int32, (8, width), 1)
    sub = lax.broadcasted_iota(jnp.int32, (8, width), 0)

    def along_x(u):
        left = jnp.where(column == 0, 0.0, pltpu.roll(u, 1, 1))
        right = jnp.where(column == width - 1, 0.0, pltpu.roll(u, width - 1, 1))
        return left + right

    def advance(here, near, pic):
        pairs = [heaviside_and_rate(u) for u in here]
        force = forces([h for h, _ in pairs], pic)
        return [
            u + rate * (n - 6.0 * u - f)
            for u, n, (_, rate), f in zip(here, near, pairs, force)
        ]

    def along_y(u, row):
        row_up = jnp.where(upper, row, 0.0)
        row_down = jnp.where(upper, 0.0, row)
        above = jnp.where(sub == yl - 1, row_up, pltpu.roll(u, yl - 1, 0))
        below = jnp.where(sub == 0, row_down, pltpu.roll(u, 1, 0))
        return above + below

    return advance, along_x, along_y


def add_neighbours(lev_ref, low_ref, high_ref, zl, yl):
    def level(k, z):
        if z < 0:
            return low_ref[pl.ds((2 * k + 2 + z) * yl, yl), :]
        if z >= zl:
            return high_ref[pl.ds((2 * k + z - zl) * yl, yl), :]
        return lev_ref[pl.ds((k * zl + z) * yl, yl), :]

    return level


def inner_kernel(zl, yl, mean_ref, lev_ref, ct_ref, low_ref, high_ref, side_ref, out_ref):
    advance, along_x, along_y = tile_tools(mean_ref, yl, lev_ref.shape[1])
    level = add_neighbours(lev_ref, low_ref, high_ref, zl, yl)
    for z in range(zl):
        here = [level(k, z) for k in range(LEVELS)]
        near = [
            level(k, z - 1) + level(k, z + 1) + along_x(here[k])
            + along_y(here[k], side_ref[pl.ds(2 * zl * k + z, 1), :])
            for k in range(LEVELS)
        ]
        value = advance(here, near, ct_ref[pl.ds(z * yl, yl), :])
        for k in range(LEVELS):
            out_ref[pl.ds((k * zl + z) * yl, yl), :] = value[k]


def outer_kernel(zl, yl, gz, mean_ref, lev_ref, ct_ref, low_ref, high_ref, side_ref,
                 corner_ref, inner_ref, out_ref, outer, strip, around, strip_first):
    at_z = lax.axis_index("gz")
    edge = jnp.where(lax.axis_index("gy") == 0, yl - 1, 0)
    plane = zl * yl
    advance, along_x, along_y = tile_tools(mean_ref, yl, lev_ref.shape[1])
    level = add_neighbours(lev_ref, low_ref, high_ref, zl, yl)

    def side(k, z):
        if z < 0:
            return corner_ref[pl.ds(k, 1), :]
        if z >= zl:
            return corner_ref[pl.ds(LEVELS + k, 1), :]
        return side_ref[pl.ds(2 * zl * k + z, 1), :]

    picture_at = pl.ds(2 * LEVELS * yl, yl)
    for n, (z, kept, pic) in enumerate((
        (-1, at_z > 0, low_ref[picture_at, :]), (zl, at_z < gz - 1, high_ref[picture_at, :])
    )):
        here = [level(k, z) for k in range(LEVELS)]
        near = [
            level(k, z - 1) + level(k, z + 1) + along_x(here[k]) + along_y(here[k], side(k, z))
            for k in range(LEVELS)
        ]
        value = advance(here, near, pic)
        for k in range(LEVELS):
            outer[pl.ds((2 * k + n) * yl, yl), :] = jnp.where(kept, value[k], 0.0)

    strip[...] = jnp.zeros_like(strip)
    around[...] = jnp.zeros_like(around)
    for k in range(LEVELS):
        for z in range(-1, zl + 1):
            strip[pl.ds(8 * k + z + 1, 1), :] = side(k, z)
        for z in range(zl):
            around[pl.ds(8 * k + z + 1, 1), :] = (
                lev_ref[pl.ds(k * plane + z * yl + edge, 1), :]
                + side_ref[pl.ds(2 * zl * k + zl + z, 1), :]
            )
    for z in range(zl):
        strip[pl.ds(8 * LEVELS + z + 1, 1), :] = side_ref[pl.ds(2 * zl * LEVELS + z, 1), :]
    here = [strip[pl.ds(8 * k, 8), :] for k in range(LEVELS)]
    near = [
        pltpu.roll(u, 7, 0) + pltpu.roll(u, 1, 0) + along_x(u) + around[pl.ds(8 * k, 8), :]
        for k, u in enumerate(here)
    ]
    value = advance(here, near, strip[pl.ds(8 * LEVELS, 8), :])
    for k in range(LEVELS):
        strip_first[pl.ds(8 * k, 8), :] = value[k]

    def after(k, z):
        if z < 0 or z >= zl:
            return outer[pl.ds((2 * k + (z >= zl)) * yl, yl), :]
        return inner_ref[pl.ds((k * zl + z) * yl, yl), :]

    for z in range(zl):
        here = [after(k, z) for k in range(LEVELS)]
        near = [
            after(k, z - 1) + after(k, z + 1) + along_x(here[k])
            + along_y(here[k], strip_first[pl.ds(8 * k + z + 1, 1), :])
            for k in range(LEVELS)
        ]
        value = advance(here, near, ct_ref[pl.ds(z * yl, yl), :])
        for k in range(LEVELS):
            out_ref[pl.ds(k * plane + z * yl, yl), :] = value[k]


def split_body(levels, ct_image, region_means):
    gz, gy = lax.axis_size("gz"), lax.axis_size("gy")
    _, zl, yl, width = levels.shape
    parts = gz * gy
    share = width // parts
    halo, quarter = share + 4, (share + 4) // 4
    chunk = halo + quarter
    f32 = jnp.float32
    vmem = pl.BlockSpec(memory_space=pltpu.VMEM)
    smem = pl.BlockSpec(memory_space=pltpu.SMEM)
    anywhere = pl.BlockSpec(memory_space=pl.ANY)
    params = pltpu.CompilerParams(vmem_limit_bytes=24 * 1024 * 1024)
    scratch = lambda *dims: pltpu.VMEM(dims, f32)
    shape = lambda rows: jax.ShapeDtypeStruct((rows, width), f32)
    message = (2 * LEVELS + 1) * yl
    packed, lines, image, up, down, side = pl.pallas_call(
        functools.partial(pack_kernel, share, zl, yl),
        out_shape=(
            jax.ShapeDtypeStruct((parts * chunk, LANES), f32),
            shape(LANES), shape(zl * yl), shape(message), shape(message),
            shape(2 * zl * LEVELS + zl),
        ),
        in_specs=[pl.BlockSpec(memory_space=pltpu.HBM)] * 2,
        out_specs=(anywhere,) + (vmem,) * 5,
        scratch_shapes=[
            scratch(width + 8, LANES),
            scratch(width + 16, LANES),
            scratch(4, LANES + 16, LANES),
            scratch(8 * parts + 8, LANES),
            scratch(parts * chunk, LANES),
            pltpu.SemaphoreType.DMA((1 + 2 * width // LANES,)),
        ],
        compiler_params=params,
        name="pack",
    )(
        pltpu.with_memory_space_constraint(levels.reshape(LANES, width), pltpu.HBM),
        pltpu.with_memory_space_constraint(ct_image.reshape(zl * yl, width), pltpu.HBM),
    )
    arrived = lax.all_to_all(
        packed.reshape(parts, chunk, 1, LANES), ("gy", "gz"), split_axis=0, concat_axis=0, tiled=True
    ).reshape(parts * chunk, LANES)

    low = lax.ppermute(up, "gz", [(i, i + 1) for i in range(gz - 1)])
    high = lax.ppermute(down, "gz", [(i + 1, i) for i in range(gz - 1)])
    side = lax.ppermute(side, "gy", [(0, 1), (1, 0)])

    lanes = lambda rows: jax.ShapeDtypeStruct((rows, LANES), f32)
    coefs, penalties = pl.pallas_call(
        functools.partial(tables_kernel, gy, zl, yl),
        out_shape=(lanes(16), lanes(8 * yl * (2 * gy - 1))),
        in_specs=[smem],
        out_specs=(vmem, vmem),
        compiler_params=params,
        name="tables",
    )(region_means)
    slots = (gy * (gz + 2) + 1) * SLOT
    blocks = gy * (gz + 2) * share
    passed = pl.pallas_call(
        functools.partial(middle_kernel, share, gz, gy, zl, yl),
        out_shape=jax.ShapeDtypeStruct((width, LANES), f32),
        in_specs=[vmem] * 3,
        out_specs=anywhere,
        scratch_shapes=[
            scratch(slots, LANES),
            scratch(slots, LANES),
            scratch(slots, LANES),
            scratch(blocks, LANES),
            scratch(zl - 1, blocks, LANES),
            scratch(width, LANES),
            scratch(width, LANES),
            scratch(8, width, LANES),
            pltpu.SemaphoreType.DMA((gy * gz // 4,)),
        ],
        compiler_params=params,
        name="middle",
    )(coefs, penalties, arrived)
    passed, low, high, side = lax.optimization_barrier((passed, low, high, side))
    passed = lax.all_to_all(
        passed.reshape(parts, share, LANES), ("gy", "gz"), split_axis=0, concat_axis=0, tiled=True
    ).reshape(width, LANES)

    corner = pl.pallas_call(
        functools.partial(corners_kernel, yl),
        out_shape=shape(2 * LEVELS),
        in_specs=[vmem, vmem],
        out_specs=vmem,
        compiler_params=params,
        name="corners",
    )(low, high)
    corner = lax.ppermute(corner, "gy", [(0, 1), (1, 0)])
    cost = pl.CostEstimate(flops=5_000_000, bytes_accessed=1_000_000, transcendentals=0)
    inner = pl.pallas_call(
        functools.partial(inner_kernel, zl, yl),
        out_shape=shape(LANES),
        in_specs=[smem] + [vmem] * 5,
        out_specs=vmem,
        compiler_params=params,
        cost_estimate=cost,
        name="inner",
    )(region_means, lines, image, low, high, side)
    evolved = pl.pallas_call(
        functools.partial(outer_kernel, zl, yl, gz),
        out_shape=shape(LANES),
        in_specs=[smem] + [vmem] * 7,
        out_specs=vmem,
        scratch_shapes=[
            scratch(2 * LEVELS * yl, width),
            scratch(8 * (LEVELS + 1), width),
            scratch(8 * LEVELS, width),
            scratch(8 * LEVELS, width),
        ],
        compiler_params=params,
        cost_estimate=cost,
        name="outer",
    )(region_means, lines, image, low, high, side, corner, inner)

    regularized = pl.pallas_call(
        functools.partial(finish_kernel, yl),
        out_shape=shape(LANES),
        in_specs=[vmem],
        out_specs=anywhere,
        scratch_shapes=[
            scratch(32, LANES),
            scratch(width + 8, LANES),
            pltpu.SemaphoreType.DMA((width // LANES,)),
        ],
        compiler_params=params,
        name="finish",
    )(passed)
    return evolved.reshape(levels.shape), regularized.reshape(levels.shape)


def body(levels, ct_image, region_means):
    gz, gy = lax.axis_size("gz"), lax.axis_size("gy")
    parts = gz * gy
    count, zl, yl, width = levels.shape
    fits = count == LEVELS and count * zl * yl == LANES and yl == 8 and zl >= 2
    fits = fits and gy == 2 and gz % 8 == 0 and gz * zl <= KERNEL
    fits = fits and width == 4 * LANES and parts == 32
    if fits:
        return split_body(levels, ct_image, region_means)
    return portable_body(levels, ct_image, region_means)


def solution(mesh):
    return jax.shard_map(
        body,
        mesh=mesh,
        in_specs=(P(None, "gz", "gy", None), P("gz", "gy", None), P()),
        out_specs=(P(None, "gz", "gy", None), P(None, "gz", "gy", None)),
        check_vma=False,
    )
```

```python
import functools
import math

import jax
import jax.numpy as jnp
import numpy as np
from jax import lax
from jax.experimental import pallas as pl
from jax.experimental.pallas import tpu as pltpu
from jax.sharding import PartitionSpec as P

LEVELS = 4
PHASES = 16
UPDATES = 2
KERNEL = 200
LANES = 128


PENALTY = 0.0005
STEP_SIZE = 0.5
FAR = 1e30


def with_halo(block, sides, width):
    for axis, dim in sides:
        count = lax.axis_size(axis)
        forward = [(i, i + 1) for i in range(count - 1)]
        backward = [(target, source) for source, target in forward]
        low = lax.ppermute(
            lax.slice_in_dim(block, block.shape[dim] - width, None, axis=dim), axis, forward
        )
        high = lax.ppermute(lax.slice_in_dim(block, 0, width, axis=dim), axis, backward)
        block = jnp.concatenate([low, block, high], axis=dim)
    return block


def evolve(level_pad, picture, region_means):
    interior = level_pad[:, 1:-1, 1:-1, :]
    side_x = jnp.pad(interior, ((0, 0), (0, 0), (0, 0), (1, 1)))
    laplace = level_pad[:, 2:, 1:-1, :] + level_pad[:, :-2, 1:-1, :]
    laplace = laplace + level_pad[:, 1:-1, 2:, :] + level_pad[:, 1:-1, :-2, :]
    laplace = laplace + side_x[..., 2:] + side_x[..., :-2] - 6.0 * interior
    heaviside = 0.5 + jnp.arctan(interior) / math.pi
    delta_term = 1.0 / (math.pi * (1.0 + interior * interior))
    forces = [jnp.zeros_like(interior[0]) for level_id in range(LEVELS)]
    for phase_id in range(PHASES):
        differ = picture - region_means[phase_id]
        energy = differ * differ
        factors = []
        for level_id in range(LEVELS):
            if phase_id >> level_id & 1:
                factors.append(heaviside[level_id])
            else:
                factors.append(1.0 - heaviside[level_id])
        for level_id in range(LEVELS):
            sign_value = 1.0 if phase_id >> level_id & 1 else -1.0
            others = energy
            for other_id in range(LEVELS):
                if other_id != level_id:
                    others = others * factors[other_id]
            forces[level_id] = forces[level_id] + sign_value * others
    force_all = jnp.stack(forces, axis=0)
    return interior + STEP_SIZE * delta_term * (laplace - force_all)


def minplus_lines(field_in, line_axis, kernel_reach):
    moved_field = jnp.moveaxis(field_in, line_axis, -1)
    line_shape = moved_field.shape
    line_len = line_shape[-1]
    line_rows = moved_field.reshape(-1, line_len)
    row_count = line_rows.shape[0]
    positions = jnp.arange(line_len, dtype=jnp.float32)
    distance = positions[:, None] - positions[None, :]
    penalty_table = jnp.where(
        jnp.abs(distance) <= kernel_reach, PENALTY * (distance * distance), jnp.inf
    )
    row_limit = max(1, 1048576 // (line_len * line_len))
    row_block = 1
    while row_block * 2 <= row_limit and row_count % (row_block * 2) == 0:
        row_block = row_block * 2
    grouped = line_rows.reshape(row_count // row_block, row_block, line_len)

    def block_min(block_rows):
        return jnp.min(block_rows[:, None, :] + penalty_table[None, :, :], axis=2)

    result_rows = lax.map(block_min, grouped)
    return jnp.moveaxis(result_rows.reshape(line_shape), -1, line_axis)


def portable_body(levels, ct_image, region_means):
    current = levels
    for _ in range(UPDATES):
        padded = with_halo(current, (("gz", 1), ("gy", 2)), 1)
        current = evolve(padded, ct_image, region_means)
    field = minplus_lines(current, 3, KERNEL)
    for axis, dim in (("gz", 1), ("gy", 2)):
        lines = lax.all_to_all(field, axis, split_axis=3, concat_axis=dim, tiled=True)
        lines = minplus_lines(lines, dim, KERNEL)
        field = lax.all_to_all(lines, axis, split_axis=dim, concat_axis=3, tiled=True)
    return current, field


def pack_kernel(share, zl, yl, lev_hbm, ct_hbm, out_hbm, lev, ct_ref, up_ref, down_ref, side_ref,
                stage, lines, turned, picture, out_ref, sems):
    width = lev.shape[1]
    parts = width // share
    blocks = width // LANES
    halo, quarter = share + 4, (share + 4) // 4
    chunk = halo + quarter
    count = LEVELS * zl
    tile = zl * yl
    arriving = [pltpu.make_async_copy(ct_hbm, ct_ref, sems.at[0])]
    for b in range(blocks):
        here = stage.at[pl.ds(b * LANES, LANES), :]
        source = lev_hbm.at[:, pl.ds(b * LANES, LANES)]
        arriving.append(pltpu.make_async_copy(source, here, sems.at[1 + b]))
    for copy in arriving:
        copy.start()
    lines[pl.ds(0, 8), :] = jnp.zeros((8, LANES), jnp.float32)
    lines[pl.ds(8 + width, 8), :] = jnp.zeros((8, LANES), jnp.float32)

    for copy in arriving:
        copy.wait()
    across = jnp.concatenate([ct_ref[:, b * LANES:(b + 1) * LANES] for b in range(blocks)], axis=0).T
    for n in range(blocks):
        turn = lambda rows, by: pltpu.roll(rows, by % blocks * tile, 1) if by % blocks else rows
        turned[n, pl.ds(0, 8), :] = turn(across[LANES - 8:], n + 1)
        turned[n, pl.ds(8, LANES), :] = turn(across, n)
        turned[n, pl.ds(8 + LANES, 8), :] = turn(across[:8], n - 1)
    group = lax.broadcasted_iota(jnp.int32, (8, LANES), 1) // tile
    each = LANES // share
    for r in range(parts):
        b, at = r // each, 8 + r % each * share - 2
        value = None
        for t in range(4):
            run = turned[(t - b) % blocks, pl.ds(at + quarter * t, 8), :]
            value = run if value is None else jnp.where(group >= t, run, value)
        picture[pl.ds(8 * r, 8), :] = value
    for b in range(blocks):
        block = [stage[pl.ds(b * LANES + y, count, stride=yl), :] for y in range(yl)]
        lines[pl.ds(8 + b * LANES, LANES), :] = jnp.concatenate(block, axis=0).T

    leaving = []
    sub = lax.broadcasted_iota(jnp.int32, (8, LANES), 0)

    def out_tile(tile):
        value = None
        for r in range(8 * tile // chunk, min((8 * tile + 7) // chunk + 1, parts)):
            for source, begin, length, origin in (
                (picture, r * chunk, quarter, 8 * r),
                (lines, r * chunk + quarter, halo, 6 + r * share),
            ):
                if begin + length <= 8 * tile or begin >= 8 * tile + 8:
                    continue
                piece = source[pl.ds(8 * tile - begin + origin, 8), :]
                value = piece if value is None else jnp.where(sub >= begin - 8 * tile, piece, value)
        return value

    start = 0
    for b in range(blocks):
        known = parts if b + 1 == blocks else (b + 1) * LANES // share - 1
        stop = known * chunk // 8 * 8
        for tile in range(start // 8, stop // 8):
            out_ref[pl.ds(8 * tile, 8), :] = out_tile(tile)
        rows = pl.ds(start, stop - start)
        leaving.append(
            pltpu.make_async_copy(out_ref.at[rows, :], out_hbm.at[rows, :], sems.at[1 + blocks + b])
        )
        leaving[-1].start()
        start = stop
    for b in range(blocks):
        lev[:, b * LANES:(b + 1) * LANES] = stage[pl.ds(b * LANES, LANES), :]
    plane = zl * yl
    for k in range(LEVELS):
        at = pl.ds(2 * k * yl, 2 * yl)
        up_ref[at, :] = lev[pl.ds((k + 1) * plane - 2 * yl, 2 * yl), :]
        down_ref[at, :] = lev[pl.ds(k * plane, 2 * yl), :]
    at = pl.ds(2 * LEVELS * yl, yl)
    up_ref[at, :] = ct_ref[pl.ds(plane - yl, yl), :]
    down_ref[at, :] = ct_ref[pl.ds(0, yl), :]
    upper = lax.axis_index("gy") == 0
    near = jnp.where(upper, yl - 1, 0)
    next_near = jnp.where(upper, yl - 2, 1)
    for k in range(LEVELS):
        for z in range(zl):
            base = k * plane + z * yl
            side_ref[pl.ds(2 * zl * k + z, 1), :] = lev[pl.ds(base + near, 1), :]
            side_ref[pl.ds(2 * zl * k + zl + z, 1), :] = lev[pl.ds(base + next_near, 1), :]
    for z in range(zl):
        side_ref[pl.ds(2 * zl * LEVELS + z, 1), :] = ct_ref[pl.ds(z * yl + near, 1), :]
    for copy in leaving:
        copy.wait()


HALF_ANGLE = (
    0.6366196870803833, -0.21219870448112488, 0.12714172899723053, -0.0893140509724617,
    0.06329755485057831, -0.03813650459051132, 0.015633534640073776, -0.0030433274805545807,
)


def heaviside_and_rate(u):
    s = 1.0 + u * u
    q = lax.rsqrt(s)
    r = u / (1.0 + s * q)
    y = r * r
    p = HALF_ANGLE[-1]
    for c in HALF_ANGLE[-2::-1]:
        p = p * y + c
    return 0.5 + r * p, (q * q) * (STEP_SIZE / math.pi)


def cost_of(d):
    return float(np.float32(PENALTY) * np.float32(d * d))


def tables_kernel(gy, zl, yl, mean_ref, coef_ref, ypen):
    lane = lax.broadcasted_iota(jnp.int32, (1, LANES), 1)
    level = lane // zl % LEVELS
    y = lane // (LEVELS * zl)

    def mean_of(bits, own):
        value = jnp.zeros((1, LANES), jnp.float32)
        for k in range(LEVELS):
            phase = own << k
            for n in range(3):
                phase |= (bits >> n & 1) << ((k + 1 + n) % LEVELS)
            value = jnp.where(level == k, mean_ref[phase], value)
        return value

    slope, const = [], []
    for bits in range(8):
        low, high = mean_of(bits, 0), mean_of(bits, 1)
        slope.append(-2.0 * (high - low))
        const.append((high - low) * (high + low))
    for n in range(3):
        for bits in range(8):
            if bits >> n & 1:
                slope[bits] = slope[bits] - slope[bits ^ (1 << n)]
                const[bits] = const[bits] - const[bits ^ (1 << n)]
    for n in range(8):
        coef_ref[pl.ds(n, 1), :] = slope[n]
        coef_ref[pl.ds(8 + n, 1), :] = const[n]

    for gap in range(-(gy - 1), gy):
        for turn in range(yl):
            d = (yl * gap + y - (y + turn) % yl).astype(jnp.float32)
            pen = jnp.where(jnp.abs(d) <= KERNEL, PENALTY * (d * d), FAR)
            ypen[pl.ds(8 * ((gap + gy - 1) * yl + turn), 8), :] = jnp.broadcast_to(pen, (8, LANES))


SLOT = 32


def middle_kernel(share, gz, gy, zl, yl, coef_ref, ypen, in_ref, out_ref, levels, picture,
                  first, evolved, shifted, zdone, done, kept, sems):
    parts = gz * gy
    halo, quarter = share + 4, (share + 4) // 4
    chunk = halo + quarter
    tile = zl * yl
    deep = gz + 2
    me = lax.axis_index("gy") * gz + lax.axis_index("gz")

    lane = lax.broadcasted_iota(jnp.int32, (1, LANES), 1)
    level = lane // zl % LEVELS
    z = lane % zl
    y = lane // (LEVELS * zl)

    def moved(value, index):
        return jnp.take_along_axis(
            value, jnp.broadcast_to(index, value.shape), axis=1, mode="promise_in_bounds"
        )

    def z_turned(value, turn):
        return moved(value, lane + (z + turn) % zl - z)

    def level_turned(value, turn):
        return moved(value, lane + ((level + turn) % LEVELS - level) * zl)

    def y_turned(value, turn):
        return pltpu.roll(value, LANES - turn * LEVELS * zl, 1)

    def stacked(blocks):
        return jnp.concatenate(blocks, axis=0)

    def row_of(a, b, x):
        return (b * deep + a + 1) * SLOT + 8 + x

    zero = jnp.zeros((SLOT, LANES), jnp.float32)
    for b in range(gy):
        for a in (-1, gz):
            levels[pl.ds(row_of(a, b, -8), SLOT), :] = zero
            first[pl.ds(row_of(a, b, -8), SLOT), :] = zero
        for a in range(gz):
            source = (b * gz + a) * chunk + quarter
            levels[pl.ds(row_of(a, b, -2), halo), :] = in_ref[pl.ds(source, halo), :]
        for a in range(0, gz, 4):
            batch = range(a, a + 4)
            packed = stacked([in_ref[pl.ds((b * gz + n) * chunk, 8), :] for n in batch])
            for t in range(4):
                run = moved(packed, t * tile + z * yl + y)
                for n in batch:
                    at = 8 * (n - a)
                    rows = pl.ds(row_of(n, b, t * quarter - 2), quarter)
                    picture[rows, :] = run[at:at + quarter]

    coefs = [coef_ref[pl.ds(n, 1), :] for n in range(16)]
    slope, const = coefs[:8], coefs[8:]

    def step(read, tiles, f):
        def beside(dz, dy):
            none = jnp.zeros_like(read(0, 0, 0))
            return stacked([
                read(a + dz, b + dy, 0) if 0 <= b + dy < gy else none for a, b in tiles
            ])

        here = beside(0, 0)
        h, rate = heaviside_and_rate(here)
        near = stacked([read(a, b, -1) + read(a, b, 1) for a, b in tiles]) - 6.0 * here
        near = near + z_turned(jnp.where(z == 0, beside(1, 0), here), 1)
        near = near + z_turned(jnp.where(z == zl - 1, beside(-1, 0), here), zl - 1)
        near = near + y_turned(jnp.where(y == 0, beside(0, 1), here), 1)
        near = near + y_turned(jnp.where(y == yl - 1, beside(0, -1), here), yl - 1)
        h1, h2, h3 = (level_turned(h, turn) for turn in (1, 2, 3))
        g = lambda bits: f(bits) + h1 * f(bits | 1)
        force = (g(0) + h2 * g(2)) + h3 * (g(4) + h2 * g(6))
        return here + rate * (near - force)

    def run_of(ref):
        return lambda a, b, dx: ref[pl.ds(row_of(a, b, dx), share), :]

    def terms(pic):
        return lambda bits: slope[bits] * pic + const[bits]

    for x, outside in ((-1, me == 0), (share, me == parts - 1)):
        across = lambda ref, a, b, dx: ref[pl.ds(row_of(a, b, x + dx), gz, stride=SLOT), :]
        rows = [(0, b) for b in range(gy)]
        pic = stacked([across(picture, 0, b, 0) for _, b in rows])
        value = step(lambda a, b, dx: across(levels, a, b, dx), rows, terms(pic))
        value = jnp.where(outside, 0.0, value)
        for b in range(gy):
            first[pl.ds(row_of(0, b, x), gz, stride=SLOT), :] = value[b * gz:(b + 1) * gz]
    batches = [[(a + n, b) for n in range(4)] for b in range(gy) for a in range(0, gz, 4)]
    for tiles in batches:
        pic = stacked([run_of(picture)(a, b, 0) for a, b in tiles])
        f = [terms(pic)(bits) for bits in range(8)]
        at = pl.ds((tiles[0][1] * gz + tiles[0][0]) * share, 4 * share)
        for bits in range(8):
            kept[bits, at, :] = f[bits]
        value = step(run_of(levels), tiles, lambda bits: f[bits])
        for n, (a, b) in enumerate(tiles):
            first[pl.ds(row_of(a, b, 0), share), :] = value[n * share:(n + 1) * share]

    def block_of(a, b):
        return (b * deep + a + 1) * share

    far = jnp.full((share, LANES), FAR, jnp.float32)
    for b in range(gy):
        for a in (-1, gz):
            evolved[pl.ds(block_of(a, b), share), :] = far
    for tiles in batches:
        at = pl.ds((tiles[0][1] * gz + tiles[0][0]) * share, 4 * share)
        f = lambda bits: kept[bits, at, :]
        evolved[pl.ds(block_of(*tiles[0]), 4 * share), :] = step(run_of(first), tiles, f)

    for b in range(gy):
        for a in range(-1, gz, 4):
            count = min(4, gz - a) * share
            here = evolved[pl.ds(block_of(a, b), count), :]
            above = evolved[pl.ds(block_of(a + 1, b), count), :]
            for turn in range(1, zl):
                value = z_turned(jnp.where(z < turn, above, here), turn)
                shifted[turn - 1, pl.ds(block_of(a, b), count), :] = value

    def z_unit(half, b, low):
        count = 8

        def at(d, n):
            a, turn = low + n + d // zl, d % zl
            if a < (-1 if turn else 0) or a >= gz:
                return None
            if (a, turn) not in loaded:
                rows = pl.ds(block_of(a, b) + 8 * half, 8)
                loaded[a, turn] = shifted[turn - 1, rows, :] if turn else evolved[rows, :]
            return loaded[a, turn]

        loaded = {}
        best = [at(0, n) for n in range(count)]
        for turn in range(zl):
            loaded = {}
            for d in range(turn or zl, min(gz * zl, KERNEL + 1), zl):
                for n in range(count):
                    pair = [v for v in (at(d, n), at(-d, n)) if v is not None]
                    if pair:
                        value = pair[0] if len(pair) == 1 else jnp.minimum(pair[0], pair[1])
                        best[n] = jnp.minimum(best[n], value + cost_of(d))
        for n in range(count):
            zdone[pl.ds((b * gz + low + n) * share + 8 * half, 8), :] = best[n]

    def y_unit(half, low):
        count = 4
        best = [None] * gy
        for other in range(gy):
            starts = [(other * gz + low + n) * share + 8 * half for n in range(count)]
            whole = stacked([zdone[pl.ds(at, 8), :] for at in starts])
            for turn in range(yl):
                value = y_turned(whole, turn) if turn else whole
                for b in range(gy):
                    at = (b - other + gy - 1) * yl + turn
                    new = value + stacked([ypen[pl.ds(8 * at, 8), :]] * count)
                    best[b] = new if best[b] is None else jnp.minimum(best[b], new)
        for b in range(gy):
            for n in range(count):
                rows = pl.ds((b * gz + low + n) * share + 8 * half, 8)
                done[rows, :] = best[b][8 * n:8 * n + 8]

    halves = share // 8
    copies = []
    for half in range(halves + 1):
        z_units = [(b, low) for b in range(gy) for low in range(0, gz, 8)] if half < halves else []
        y_units = list(range(0, gz, 4)) if half else []
        for n in range(max(len(z_units), len(y_units))):
            if n < len(z_units):
                z_unit(half, *z_units[n])
            if n < len(y_units):
                y_unit(half - 1, y_units[n])
                if half == halves:
                    for b in range(gy):
                        rows = pl.ds((b * gz + y_units[n]) * share, 4 * share)
                        sem = sems.at[len(copies)]
                        copies.append(pltpu.make_async_copy(done.at[rows, :], out_ref.at[rows, :], sem))
                        copies[-1].start()
    for copy in copies:
        copy.wait()


def finish_kernel(yl, in_ref, reg_ref, edge, passed, done, sems):
    width = in_ref.shape[0]
    count = width // 8
    group = 8
    far = jnp.full((8, LANES), FAR, jnp.float32)
    edge[pl.ds(0, 8), :] = far
    edge[pl.ds(8, 8), :] = in_ref[pl.ds(0, 8), :]
    edge[pl.ds(16, 8), :] = in_ref[pl.ds(width - 8, 8), :]
    edge[pl.ds(24, 8), :] = far

    def rows(at):
        if at < 0:
            return edge[pl.ds(8 + at, 8), :]
        if at > width - 8:
            return edge[pl.ds(16 + at - (width - 8), 8), :]
        return in_ref[pl.ds(at, 8), :]

    def x_pass(low):
        best = [rows(8 * (low + n)) for n in range(group)]
        for rho in range(1, 9):
            plus, minus = {}, {}
            for e in range((KERNEL - rho) // 8 + 1):
                cost = cost_of(8 * e + rho)
                for n in range(group):
                    up, down = low + n + e, low + n - e
                    pair = []
                    if 8 * up + rho < width:
                        if up not in plus:
                            plus[up] = rows(8 * up + rho)
                        pair.append(plus[up])
                    if 8 * down - rho > -8:
                        if down not in minus:
                            minus[down] = rows(8 * down - rho)
                        pair.append(minus[down])
                    if not pair:
                        continue
                    value = pair[0] if len(pair) == 1 else jnp.minimum(pair[0], pair[1])
                    best[n] = jnp.minimum(best[n], value + cost)
        for n in range(group):
            passed[pl.ds(8 * (low + n), 8), :] = best[n]

    copies = []
    each = LANES // yl

    def turn(c):
        block = passed[pl.ds(c * LANES, LANES), :].T
        for y in range(yl):
            done[pl.ds(c * LANES + y, each, stride=yl), :] = block[y * each:(y + 1) * each]

    def send(c):
        cols = pl.ds(c * LANES, LANES)
        copies.append(pltpu.make_async_copy(done.at[cols, :], reg_ref.at[:, cols], sems.at[c]))
        copies[-1].start()

    blocks = width // LANES
    for c in range(blocks):
        first = c * LANES // 8
        x_pass(first)
        if c:
            turn(c - 1)
        for low in range(first + group, first + LANES // 8, group):
            x_pass(low)
        if c:
            send(c - 1)
    turn(blocks - 1)
    send(blocks - 1)
    for copy in copies:
        copy.wait()


def corners_kernel(yl, low_ref, high_ref, corner_ref):
    near = jnp.where(lax.axis_index("gy") == 0, yl - 1, 0)
    rows = [low_ref[pl.ds((2 * k + 1) * yl + near, 1), :] for k in range(LEVELS)]
    rows += [high_ref[pl.ds(2 * k * yl + near, 1), :] for k in range(LEVELS)]
    corner_ref[...] = jnp.concatenate(rows, axis=0)


def tile_tools(mean_ref, yl, width):
    upper = lax.axis_index("gy") == 0

    const = [mean_ref[p] * mean_ref[p] for p in range(PHASES)]
    slope = [-2.0 * mean_ref[p] for p in range(PHASES)]
    for k in range(LEVELS):
        for p in range(PHASES):
            if p >> k & 1:
                const[p] = const[p] - const[p ^ (1 << k)]
                slope[p] = slope[p] - slope[p ^ (1 << k)]

    def forces(h, pic):
        c = [None] + [slope[p] * pic + const[p] for p in range(1, PHASES)]
        out = []
        for k in range(LEVELS):
            others = [n for n in range(LEVELS) if n != k]
            part = [c[1 << k | sum((bits >> i & 1) << n for i, n in enumerate(others))]
                    for bits in range(8)]
            for n in others:
                part = [part[i] + h[n] * part[i + 1] for i in range(0, len(part), 2)]
            out.append(part[0])
        return out

    column = lax.broadcasted_iota(jnp.int32, (8, width), 1)
    sub = lax.broadcasted_iota(jnp.int32, (8, width), 0)

    def along_x(u):
        left = jnp.where(column == 0, 0.0, pltpu.roll(u, 1, 1))
        right = jnp.where(column == width - 1, 0.0, pltpu.roll(u, width - 1, 1))
        return left + right

    def advance(here, near, pic):
        pairs = [heaviside_and_rate(u) for u in here]
        force = forces([h for h, _ in pairs], pic)
        return [
            u + rate * (n - 6.0 * u - f)
            for u, n, (_, rate), f in zip(here, near, pairs, force)
        ]

    def along_y(u, row):
        row_up = jnp.where(upper, row, 0.0)
        row_down = jnp.where(upper, 0.0, row)
        above = jnp.where(sub == yl - 1, row_up, pltpu.roll(u, yl - 1, 0))
        below = jnp.where(sub == 0, row_down, pltpu.roll(u, 1, 0))
        return above + below

    return advance, along_x, along_y


def add_neighbours(lev_ref, low_ref, high_ref, zl, yl):
    def level(k, z):
        if z < 0:
            return low_ref[pl.ds((2 * k + 2 + z) * yl, yl), :]
        if z >= zl:
            return high_ref[pl.ds((2 * k + z - zl) * yl, yl), :]
        return lev_ref[pl.ds((k * zl + z) * yl, yl), :]

    return level


def inner_kernel(zl, yl, mean_ref, lev_ref, ct_ref, low_ref, high_ref, side_ref, out_ref):
    advance, along_x, along_y = tile_tools(mean_ref, yl, lev_ref.shape[1])
    level = add_neighbours(lev_ref, low_ref, high_ref, zl, yl)
    for z in range(zl):
        here = [level(k, z) for k in range(LEVELS)]
        near = [
            level(k, z - 1) + level(k, z + 1) + along_x(here[k])
            + along_y(here[k], side_ref[pl.ds(2 * zl * k + z, 1), :])
            for k in range(LEVELS)
        ]
        value = advance(here, near, ct_ref[pl.ds(z * yl, yl), :])
        for k in range(LEVELS):
            out_ref[pl.ds((k * zl + z) * yl, yl), :] = value[k]


def outer_kernel(zl, yl, gz, mean_ref, lev_ref, ct_ref, low_ref, high_ref, side_ref,
                 corner_ref, inner_ref, out_ref, outer, strip, around, strip_first):
    at_z = lax.axis_index("gz")
    edge = jnp.where(lax.axis_index("gy") == 0, yl - 1, 0)
    plane = zl * yl
    advance, along_x, along_y = tile_tools(mean_ref, yl, lev_ref.shape[1])
    level = add_neighbours(lev_ref, low_ref, high_ref, zl, yl)

    def side(k, z):
        if z < 0:
            return corner_ref[pl.ds(k, 1), :]
        if z >= zl:
            return corner_ref[pl.ds(LEVELS + k, 1), :]
        return side_ref[pl.ds(2 * zl * k + z, 1), :]

    picture_at = pl.ds(2 * LEVELS * yl, yl)
    for n, (z, kept, pic) in enumerate((
        (-1, at_z > 0, low_ref[picture_at, :]), (zl, at_z < gz - 1, high_ref[picture_at, :])
    )):
        here = [level(k, z) for k in range(LEVELS)]
        near = [
            level(k, z - 1) + level(k, z + 1) + along_x(here[k]) + along_y(here[k], side(k, z))
            for k in range(LEVELS)
        ]
        value = advance(here, near, pic)
        for k in range(LEVELS):
            outer[pl.ds((2 * k + n) * yl, yl), :] = jnp.where(kept, value[k], 0.0)

    strip[...] = jnp.zeros_like(strip)
    around[...] = jnp.zeros_like(around)
    for k in range(LEVELS):
        for z in range(-1, zl + 1):
            strip[pl.ds(8 * k + z + 1, 1), :] = side(k, z)
        for z in range(zl):
            around[pl.ds(8 * k + z + 1, 1), :] = (
                lev_ref[pl.ds(k * plane + z * yl + edge, 1), :]
                + side_ref[pl.ds(2 * zl * k + zl + z, 1), :]
            )
    for z in range(zl):
        strip[pl.ds(8 * LEVELS + z + 1, 1), :] = side_ref[pl.ds(2 * zl * LEVELS + z, 1), :]
    here = [strip[pl.ds(8 * k, 8), :] for k in range(LEVELS)]
    near = [
        pltpu.roll(u, 7, 0) + pltpu.roll(u, 1, 0) + along_x(u) + around[pl.ds(8 * k, 8), :]
        for k, u in enumerate(here)
    ]
    value = advance(here, near, strip[pl.ds(8 * LEVELS, 8), :])
    for k in range(LEVELS):
        strip_first[pl.ds(8 * k, 8), :] = value[k]

    def after(k, z):
        if z < 0 or z >= zl:
            return outer[pl.ds((2 * k + (z >= zl)) * yl, yl), :]
        return inner_ref[pl.ds((k * zl + z) * yl, yl), :]

    for z in range(zl):
        here = [after(k, z) for k in range(LEVELS)]
        near = [
            after(k, z - 1) + after(k, z + 1) + along_x(here[k])
            + along_y(here[k], strip_first[pl.ds(8 * k + z + 1, 1), :])
            for k in range(LEVELS)
        ]
        value = advance(here, near, ct_ref[pl.ds(z * yl, yl), :])
        for k in range(LEVELS):
            out_ref[pl.ds(k * plane + z * yl, yl), :] = value[k]


def split_body(levels, ct_image, region_means):
    gz, gy = lax.axis_size("gz"), lax.axis_size("gy")
    _, zl, yl, width = levels.shape
    parts = gz * gy
    share = width // parts
    halo, quarter = share + 4, (share + 4) // 4
    chunk = halo + quarter
    f32 = jnp.float32
    vmem = pl.BlockSpec(memory_space=pltpu.VMEM)
    smem = pl.BlockSpec(memory_space=pltpu.SMEM)
    anywhere = pl.BlockSpec(memory_space=pl.ANY)
    params = pltpu.CompilerParams(vmem_limit_bytes=24 * 1024 * 1024)
    scratch = lambda *dims: pltpu.VMEM(dims, f32)
    shape = lambda rows: jax.ShapeDtypeStruct((rows, width), f32)
    message = (2 * LEVELS + 1) * yl
    packed, lines, image, up, down, side = pl.pallas_call(
        functools.partial(pack_kernel, share, zl, yl),
        out_shape=(
            jax.ShapeDtypeStruct((parts * chunk, LANES), f32),
            shape(LANES), shape(zl * yl), shape(message), shape(message),
            shape(2 * zl * LEVELS + zl),
        ),
        in_specs=[pl.BlockSpec(memory_space=pltpu.HBM)] * 2,
        out_specs=(anywhere,) + (vmem,) * 5,
        scratch_shapes=[
            scratch(width + 8, LANES),
            scratch(width + 16, LANES),
            scratch(4, LANES + 16, LANES),
            scratch(8 * parts + 8, LANES),
            scratch(parts * chunk, LANES),
            pltpu.SemaphoreType.DMA((1 + 2 * width // LANES,)),
        ],
        compiler_params=params,
        name="pack",
    )(
        pltpu.with_memory_space_constraint(levels.reshape(LANES, width), pltpu.HBM),
        pltpu.with_memory_space_constraint(ct_image.reshape(zl * yl, width), pltpu.HBM),
    )
    arrived = lax.all_to_all(
        packed.reshape(parts, chunk, 1, LANES), ("gy", "gz"), split_axis=0, concat_axis=0, tiled=True
    ).reshape(parts * chunk, LANES)

    low = lax.ppermute(up, "gz", [(i, i + 1) for i in range(gz - 1)])
    high = lax.ppermute(down, "gz", [(i + 1, i) for i in range(gz - 1)])
    side = lax.ppermute(side, "gy", [(0, 1), (1, 0)])

    lanes = lambda rows: jax.ShapeDtypeStruct((rows, LANES), f32)
    coefs, penalties = pl.pallas_call(
        functools.partial(tables_kernel, gy, zl, yl),
        out_shape=(lanes(16), lanes(8 * yl * (2 * gy - 1))),
        in_specs=[smem],
        out_specs=(vmem, vmem),
        compiler_params=params,
        name="tables",
    )(region_means)
    slots = (gy * (gz + 2) + 1) * SLOT
    blocks = gy * (gz + 2) * share
    passed = pl.pallas_call(
        functools.partial(middle_kernel, share, gz, gy, zl, yl),
        out_shape=jax.ShapeDtypeStruct((width, LANES), f32),
        in_specs=[vmem] * 3,
        out_specs=anywhere,
        scratch_shapes=[
            scratch(slots, LANES),
            scratch(slots, LANES),
            scratch(slots, LANES),
            scratch(blocks, LANES),
            scratch(zl - 1, blocks, LANES),
            scratch(width, LANES),
            scratch(width, LANES),
            scratch(8, width, LANES),
            pltpu.SemaphoreType.DMA((gy * gz // 4,)),
        ],
        compiler_params=params,
        name="middle",
    )(coefs, penalties, arrived)
    passed, low, high, side = lax.optimization_barrier((passed, low, high, side))
    passed = lax.all_to_all(
        passed.reshape(parts, share, LANES), ("gy", "gz"), split_axis=0, concat_axis=0, tiled=True
    ).reshape(width, LANES)

    corner = pl.pallas_call(
        functools.partial(corners_kernel, yl),
        out_shape=shape(2 * LEVELS),
        in_specs=[vmem, vmem],
        out_specs=vmem,
        compiler_params=params,
        name="corners",
    )(low, high)
    corner = lax.ppermute(corner, "gy", [(0, 1), (1, 0)])
    cost = pl.CostEstimate(flops=5_000_000, bytes_accessed=1_000_000, transcendentals=0)
    inner = pl.pallas_call(
        functools.partial(inner_kernel, zl, yl),
        out_shape=shape(LANES),
        in_specs=[smem] + [vmem] * 5,
        out_specs=vmem,
        compiler_params=params,
        cost_estimate=cost,
        name="inner",
    )(region_means, lines, image, low, high, side)
    evolved = pl.pallas_call(
        functools.partial(outer_kernel, zl, yl, gz),
        out_shape=shape(LANES),
        in_specs=[smem] + [vmem] * 7,
        out_specs=vmem,
        scratch_shapes=[
            scratch(2 * LEVELS * yl, width),
            scratch(8 * (LEVELS + 1), width),
            scratch(8 * LEVELS, width),
            scratch(8 * LEVELS, width),
        ],
        compiler_params=params,
        cost_estimate=cost,
        name="outer",
    )(region_means, lines, image, low, high, side, corner, inner)

    regularized = pl.pallas_call(
        functools.partial(finish_kernel, yl),
        out_shape=shape(LANES),
        in_specs=[vmem],
        out_specs=anywhere,
        scratch_shapes=[
            scratch(32, LANES),
            scratch(width, LANES),
            scratch(width + 8, LANES),
            pltpu.SemaphoreType.DMA((width // LANES,)),
        ],
        compiler_params=params,
        name="finish",
    )(passed)
    return evolved.reshape(levels.shape), regularized.reshape(levels.shape)


def body(levels, ct_image, region_means):
    gz, gy = lax.axis_size("gz"), lax.axis_size("gy")
    parts = gz * gy
    count, zl, yl, width = levels.shape
    fits = count == LEVELS and count * zl * yl == LANES and yl == 8 and zl >= 2
    fits = fits and gy == 2 and gz % 8 == 0 and gz * zl <= KERNEL
    fits = fits and width == 4 * LANES and parts == 32
    if fits:
        return split_body(levels, ct_image, region_means)
    return portable_body(levels, ct_image, region_means)


def solution(mesh):
    return jax.shard_map(
        body,
        mesh=mesh,
        in_specs=(P(None, "gz", "gy", None), P("gz", "gy", None), P()),
        out_specs=(P(None, "gz", "gy", None), P(None, "gz", "gy", None)),
        check_vma=False,
    )
```

```python
import functools
import math

import jax
import jax.numpy as jnp
import numpy as np
from jax import lax
from jax.experimental import pallas as pl
from jax.experimental.pallas import tpu as pltpu
from jax.sharding import PartitionSpec as P

LEVELS = 4
PHASES = 16
UPDATES = 2
KERNEL = 200
LANES = 128


PENALTY = 0.0005
STEP_SIZE = 0.5
FAR = 1e30


def with_halo(block, sides, width):
    for axis, dim in sides:
        count = lax.axis_size(axis)
        forward = [(i, i + 1) for i in range(count - 1)]
        backward = [(target, source) for source, target in forward]
        low = lax.ppermute(
            lax.slice_in_dim(block, block.shape[dim] - width, None, axis=dim), axis, forward
        )
        high = lax.ppermute(lax.slice_in_dim(block, 0, width, axis=dim), axis, backward)
        block = jnp.concatenate([low, block, high], axis=dim)
    return block


def evolve(level_pad, picture, region_means):
    interior = level_pad[:, 1:-1, 1:-1, :]
    side_x = jnp.pad(interior, ((0, 0), (0, 0), (0, 0), (1, 1)))
    laplace = level_pad[:, 2:, 1:-1, :] + level_pad[:, :-2, 1:-1, :]
    laplace = laplace + level_pad[:, 1:-1, 2:, :] + level_pad[:, 1:-1, :-2, :]
    laplace = laplace + side_x[..., 2:] + side_x[..., :-2] - 6.0 * interior
    heaviside = 0.5 + jnp.arctan(interior) / math.pi
    delta_term = 1.0 / (math.pi * (1.0 + interior * interior))
    forces = [jnp.zeros_like(interior[0]) for level_id in range(LEVELS)]
    for phase_id in range(PHASES):
        differ = picture - region_means[phase_id]
        energy = differ * differ
        factors = []
        for level_id in range(LEVELS):
            if phase_id >> level_id & 1:
                factors.append(heaviside[level_id])
            else:
                factors.append(1.0 - heaviside[level_id])
        for level_id in range(LEVELS):
            sign_value = 1.0 if phase_id >> level_id & 1 else -1.0
            others = energy
            for other_id in range(LEVELS):
                if other_id != level_id:
                    others = others * factors[other_id]
            forces[level_id] = forces[level_id] + sign_value * others
    force_all = jnp.stack(forces, axis=0)
    return interior + STEP_SIZE * delta_term * (laplace - force_all)


def minplus_lines(field_in, line_axis, kernel_reach):
    moved_field = jnp.moveaxis(field_in, line_axis, -1)
    line_shape = moved_field.shape
    line_len = line_shape[-1]
    line_rows = moved_field.reshape(-1, line_len)
    row_count = line_rows.shape[0]
    positions = jnp.arange(line_len, dtype=jnp.float32)
    distance = positions[:, None] - positions[None, :]
    penalty_table = jnp.where(
        jnp.abs(distance) <= kernel_reach, PENALTY * (distance * distance), jnp.inf
    )
    row_limit = max(1, 1048576 // (line_len * line_len))
    row_block = 1
    while row_block * 2 <= row_limit and row_count % (row_block * 2) == 0:
        row_block = row_block * 2
    grouped = line_rows.reshape(row_count // row_block, row_block, line_len)

    def block_min(block_rows):
        return jnp.min(block_rows[:, None, :] + penalty_table[None, :, :], axis=2)

    result_rows = lax.map(block_min, grouped)
    return jnp.moveaxis(result_rows.reshape(line_shape), -1, line_axis)


def portable_body(levels, ct_image, region_means):
    current = levels
    for _ in range(UPDATES):
        padded = with_halo(current, (("gz", 1), ("gy", 2)), 1)
        current = evolve(padded, ct_image, region_means)
    field = minplus_lines(current, 3, KERNEL)
    for axis, dim in (("gz", 1), ("gy", 2)):
        lines = lax.all_to_all(field, axis, split_axis=3, concat_axis=dim, tiled=True)
        lines = minplus_lines(lines, dim, KERNEL)
        field = lax.all_to_all(lines, axis, split_axis=dim, concat_axis=3, tiled=True)
    return current, field


def pack_kernel(share, zl, yl, lev_hbm, ct_hbm, out_hbm, lev, ct_ref, up_ref, down_ref, side_ref,
                stage, lines, turned, picture, out_ref, sems):
    width = lev.shape[1]
    parts = width // share
    blocks = width // LANES
    halo, quarter = share + 4, (share + 4) // 4
    chunk = halo + quarter
    count = LEVELS * zl
    tile = zl * yl
    arriving = [pltpu.make_async_copy(ct_hbm, ct_ref, sems.at[0])]
    for b in range(blocks):
        here = stage.at[pl.ds(b * LANES, LANES), :]
        source = lev_hbm.at[:, pl.ds(b * LANES, LANES)]
        arriving.append(pltpu.make_async_copy(source, here, sems.at[1 + b]))
    for copy in arriving:
        copy.start()
    lines[pl.ds(0, 8), :] = jnp.zeros((8, LANES), jnp.float32)
    lines[pl.ds(8 + width, 8), :] = jnp.zeros((8, LANES), jnp.float32)

    for copy in arriving:
        copy.wait()
    across = jnp.concatenate([ct_ref[:, b * LANES:(b + 1) * LANES] for b in range(blocks)], axis=0).T
    for n in range(blocks):
        turn = lambda rows, by: pltpu.roll(rows, by % blocks * tile, 1) if by % blocks else rows
        turned[n, pl.ds(0, 8), :] = turn(across[LANES - 8:], n + 1)
        turned[n, pl.ds(8, LANES), :] = turn(across, n)
        turned[n, pl.ds(8 + LANES, 8), :] = turn(across[:8], n - 1)
    group = lax.broadcasted_iota(jnp.int32, (8, LANES), 1) // tile
    each = LANES // share
    for r in range(parts):
        b, at = r // each, 8 + r % each * share - 2
        value = None
        for t in range(4):
            run = turned[(t - b) % blocks, pl.ds(at + quarter * t, 8), :]
            value = run if value is None else jnp.where(group >= t, run, value)
        picture[pl.ds(8 * r, 8), :] = value
    for b in range(blocks):
        block = [stage[pl.ds(b * LANES + y, count, stride=yl), :] for y in range(yl)]
        lines[pl.ds(8 + b * LANES, LANES), :] = jnp.concatenate(block, axis=0).T

    leaving = []
    sub = lax.broadcasted_iota(jnp.int32, (8, LANES), 0)

    def out_tile(tile):
        value = None
        for r in range(8 * tile // chunk, min((8 * tile + 7) // chunk + 1, parts)):
            for source, begin, length, origin in (
                (picture, r * chunk, quarter, 8 * r),
                (lines, r * chunk + quarter, halo, 6 + r * share),
            ):
                if begin + length <= 8 * tile or begin >= 8 * tile + 8:
                    continue
                piece = source[pl.ds(8 * tile - begin + origin, 8), :]
                value = piece if value is None else jnp.where(sub >= begin - 8 * tile, piece, value)
        return value

    start = 0
    for b in range(blocks):
        known = parts if b + 1 == blocks else (b + 1) * LANES // share - 1
        stop = known * chunk // 8 * 8
        for tile in range(start // 8, stop // 8):
            out_ref[pl.ds(8 * tile, 8), :] = out_tile(tile)
        rows = pl.ds(start, stop - start)
        leaving.append(
            pltpu.make_async_copy(out_ref.at[rows, :], out_hbm.at[rows, :], sems.at[1 + blocks + b])
        )
        leaving[-1].start()
        start = stop
    for b in range(blocks):
        lev[:, b * LANES:(b + 1) * LANES] = stage[pl.ds(b * LANES, LANES), :]
    plane = zl * yl
    for k in range(LEVELS):
        at = pl.ds(2 * k * yl, 2 * yl)
        up_ref[at, :] = lev[pl.ds((k + 1) * plane - 2 * yl, 2 * yl), :]
        down_ref[at, :] = lev[pl.ds(k * plane, 2 * yl), :]
    at = pl.ds(2 * LEVELS * yl, yl)
    up_ref[at, :] = ct_ref[pl.ds(plane - yl, yl), :]
    down_ref[at, :] = ct_ref[pl.ds(0, yl), :]
    upper = lax.axis_index("gy") == 0
    near = jnp.where(upper, yl - 1, 0)
    next_near = jnp.where(upper, yl - 2, 1)
    for k in range(LEVELS):
        for z in range(zl):
            base = k * plane + z * yl
            side_ref[pl.ds(2 * zl * k + z, 1), :] = lev[pl.ds(base + near, 1), :]
            side_ref[pl.ds(2 * zl * k + zl + z, 1), :] = lev[pl.ds(base + next_near, 1), :]
    for z in range(zl):
        side_ref[pl.ds(2 * zl * LEVELS + z, 1), :] = ct_ref[pl.ds(z * yl + near, 1), :]
    for copy in leaving:
        copy.wait()


HALF_ANGLE = (
    0.6366196870803833, -0.21219870448112488, 0.12714172899723053, -0.0893140509724617,
    0.06329755485057831, -0.03813650459051132, 0.015633534640073776, -0.0030433274805545807,
)


def heaviside_and_rate(u):
    s = 1.0 + u * u
    q = lax.rsqrt(s)
    r = u / (1.0 + s * q)
    y = r * r
    p = HALF_ANGLE[-1]
    for c in HALF_ANGLE[-2::-1]:
        p = p * y + c
    return 0.5 + r * p, (q * q) * (STEP_SIZE / math.pi)


def cost_of(d):
    return float(np.float32(PENALTY) * np.float32(d * d))


def tables_kernel(gy, zl, yl, mean_ref, coef_ref, ypen):
    lane = lax.broadcasted_iota(jnp.int32, (1, LANES), 1)
    level = lane // zl % LEVELS
    y = lane // (LEVELS * zl)

    def mean_of(bits, own):
        value = jnp.zeros((1, LANES), jnp.float32)
        for k in range(LEVELS):
            phase = own << k
            for n in range(3):
                phase |= (bits >> n & 1) << ((k + 1 + n) % LEVELS)
            value = jnp.where(level == k, mean_ref[phase], value)
        return value

    slope, const = [], []
    for bits in range(8):
        low, high = mean_of(bits, 0), mean_of(bits, 1)
        slope.append(-2.0 * (high - low))
        const.append((high - low) * (high + low))
    for n in range(3):
        for bits in range(8):
            if bits >> n & 1:
                slope[bits] = slope[bits] - slope[bits ^ (1 << n)]
                const[bits] = const[bits] - const[bits ^ (1 << n)]
    for n in range(8):
        coef_ref[pl.ds(n, 1), :] = slope[n]
        coef_ref[pl.ds(8 + n, 1), :] = const[n]

    for gap in range(-(gy - 1), gy):
        for turn in range(yl):
            d = (yl * gap + y - (y + turn) % yl).astype(jnp.float32)
            pen = jnp.where(jnp.abs(d) <= KERNEL, PENALTY * (d * d), FAR)
            ypen[pl.ds(8 * ((gap + gy - 1) * yl + turn), 8), :] = jnp.broadcast_to(pen, (8, LANES))


SLOT = 32


def middle_kernel(share, gz, gy, zl, yl, coef_ref, ypen, in_ref, out_ref, levels, picture,
                  first, evolved, shifted, zdone, done, kept, sems):
    parts = gz * gy
    halo, quarter = share + 4, (share + 4) // 4
    chunk = halo + quarter
    tile = zl * yl
    deep = gz + 2
    me = lax.axis_index("gy") * gz + lax.axis_index("gz")

    lane = lax.broadcasted_iota(jnp.int32, (1, LANES), 1)
    level = lane // zl % LEVELS
    z = lane % zl
    y = lane // (LEVELS * zl)

    def moved(value, index):
        return jnp.take_along_axis(
            value, jnp.broadcast_to(index, value.shape), axis=1, mode="promise_in_bounds"
        )

    def z_turned(value, turn):
        return moved(value, lane + (z + turn) % zl - z)

    def level_turned(value, turn):
        return moved(value, lane + ((level + turn) % LEVELS - level) * zl)

    def y_turned(value, turn):
        return pltpu.roll(value, LANES - turn * LEVELS * zl, 1)

    def stacked(blocks):
        return jnp.concatenate(blocks, axis=0)

    def row_of(a, b, x):
        return (b * deep + a + 1) * SLOT + 8 + x

    zero = jnp.zeros((SLOT, LANES), jnp.float32)
    for b in range(gy):
        for a in (-1, gz):
            levels[pl.ds(row_of(a, b, -8), SLOT), :] = zero
            first[pl.ds(row_of(a, b, -8), SLOT), :] = zero
        for a in range(gz):
            source = (b * gz + a) * chunk + quarter
            levels[pl.ds(row_of(a, b, -2), halo), :] = in_ref[pl.ds(source, halo), :]
        for a in range(0, gz, 4):
            batch = range(a, a + 4)
            packed = stacked([in_ref[pl.ds((b * gz + n) * chunk, 8), :] for n in batch])
            for t in range(4):
                run = moved(packed, t * tile + z * yl + y)
                for n in batch:
                    at = 8 * (n - a)
                    rows = pl.ds(row_of(n, b, t * quarter - 2), quarter)
                    picture[rows, :] = run[at:at + quarter]

    coefs = [coef_ref[pl.ds(n, 1), :] for n in range(16)]
    slope, const = coefs[:8], coefs[8:]

    def step(read, tiles, f):
        def beside(dz, dy):
            none = jnp.zeros_like(read(tiles[0], 0, 0, 0))
            return stacked([
                read(tile, dz, dy, 0) if 0 <= tile[1] + dy < gy else none for tile in tiles
            ])

        here = beside(0, 0)
        h, rate = heaviside_and_rate(here)
        near = stacked([read(t, 0, 0, -1) + read(t, 0, 0, 1) for t in tiles]) - 6.0 * here
        near = near + z_turned(jnp.where(z == 0, beside(1, 0), here), 1)
        near = near + z_turned(jnp.where(z == zl - 1, beside(-1, 0), here), zl - 1)
        near = near + y_turned(jnp.where(y == 0, beside(0, 1), here), 1)
        near = near + y_turned(jnp.where(y == yl - 1, beside(0, -1), here), yl - 1)
        h1, h2, h3 = (level_turned(h, turn) for turn in (1, 2, 3))
        g = lambda bits: f(bits) + h1 * f(bits | 1)
        force = (g(0) + h2 * g(2)) + h3 * (g(4) + h2 * g(6))
        return here + rate * (near - force)

    def run_of(ref):
        return lambda t, dz, dy, dx: ref[pl.ds(row_of(t[0] + dz, t[1] + dy, dx), share), :]

    def terms(pic):
        return lambda bits: slope[bits] * pic + const[bits]

    batches = [[(a + n, b) for n in range(4)] for b in range(gy) for a in range(0, gz, 4)]
    for tiles in batches:
        pic = stacked([run_of(picture)(t, 0, 0, 0) for t in tiles])
        f = [terms(pic)(bits) for bits in range(8)]
        at = pl.ds((tiles[0][1] * gz + tiles[0][0]) * share, 4 * share)
        for bits in range(8):
            kept[bits, at, :] = f[bits]
        value = step(run_of(levels), tiles, lambda bits: f[bits])
        for n, (a, b) in enumerate(tiles):
            first[pl.ds(row_of(a, b, 0), share), :] = value[n * share:(n + 1) * share]

    def across(ref):
        return lambda t, dz, dy, dx: ref[pl.ds(row_of(dz, t[1] + dy, t[0] + dx), gz, stride=SLOT), :]

    ends = [(x, b) for x in (-1, share) for b in range(gy)]
    pic = stacked([across(picture)(t, 0, 0, 0) for t in ends])
    value = step(across(levels), ends, terms(pic))
    for n, (x, b) in enumerate(ends):
        outside = (me == 0) if x < 0 else (me == parts - 1)
        rows = value[n * gz:(n + 1) * gz]
        first[pl.ds(row_of(0, b, x), gz, stride=SLOT), :] = jnp.where(outside, 0.0, rows)

    def block_of(a, b):
        return (b * deep + a + 1) * share

    far = jnp.full((share, LANES), FAR, jnp.float32)
    for b in range(gy):
        for a in (-1, gz):
            evolved[pl.ds(block_of(a, b), share), :] = far
    for tiles in batches:
        at = pl.ds((tiles[0][1] * gz + tiles[0][0]) * share, 4 * share)
        f = lambda bits: kept[bits, at, :]
        evolved[pl.ds(block_of(*tiles[0]), 4 * share), :] = step(run_of(first), tiles, f)

    for b in range(gy):
        for a in range(-1, gz, 4):
            count = min(4, gz - a) * share
            here = evolved[pl.ds(block_of(a, b), count), :]
            above = evolved[pl.ds(block_of(a + 1, b), count), :]
            for turn in range(1, zl):
                value = z_turned(jnp.where(z < turn, above, here), turn)
                shifted[turn - 1, pl.ds(block_of(a, b), count), :] = value

    def z_unit(half, b, low):
        count = 8

        def at(d, n):
            a, turn = low + n + d // zl, d % zl
            if a < (-1 if turn else 0) or a >= gz:
                return None
            if (a, turn) not in loaded:
                rows = pl.ds(block_of(a, b) + 8 * half, 8)
                loaded[a, turn] = shifted[turn - 1, rows, :] if turn else evolved[rows, :]
            return loaded[a, turn]

        loaded = {}
        best = [at(0, n) for n in range(count)]
        for turn in range(zl):
            loaded = {}
            for d in range(turn or zl, min(gz * zl, KERNEL + 1), zl):
                for n in range(count):
                    pair = [v for v in (at(d, n), at(-d, n)) if v is not None]
                    if pair:
                        value = pair[0] if len(pair) == 1 else jnp.minimum(pair[0], pair[1])
                        best[n] = jnp.minimum(best[n], value + cost_of(d))
        for n in range(count):
            zdone[pl.ds((b * gz + low + n) * share + 8 * half, 8), :] = best[n]

    def y_unit(half, low):
        count = 4
        best = [None] * gy
        for other in range(gy):
            starts = [(other * gz + low + n) * share + 8 * half for n in range(count)]
            whole = stacked([zdone[pl.ds(at, 8), :] for at in starts])
            for turn in range(yl):
                value = y_turned(whole, turn) if turn else whole
                for b in range(gy):
                    at = (b - other + gy - 1) * yl + turn
                    new = value + stacked([ypen[pl.ds(8 * at, 8), :]] * count)
                    best[b] = new if best[b] is None else jnp.minimum(best[b], new)
        for b in range(gy):
            for n in range(count):
                rows = pl.ds((b * gz + low + n) * share + 8 * half, 8)
                done[rows, :] = best[b][8 * n:8 * n + 8]

    halves = share // 8
    copies = []
    for half in range(halves + 1):
        z_units = [(b, low) for b in range(gy) for low in range(0, gz, 8)] if half < halves else []
        y_units = list(range(0, gz, 4)) if half else []
        for n in range(max(len(z_units), len(y_units))):
            if n < len(z_units):
                z_unit(half, *z_units[n])
            if n < len(y_units):
                y_unit(half - 1, y_units[n])
                if half == halves:
                    for b in range(gy):
                        rows = pl.ds((b * gz + y_units[n]) * share, 4 * share)
                        sem = sems.at[len(copies)]
                        copies.append(pltpu.make_async_copy(done.at[rows, :], out_ref.at[rows, :], sem))
                        copies[-1].start()
    for copy in copies:
        copy.wait()


def finish_kernel(yl, in_ref, reg_ref, edge, passed, done, sems):
    width = in_ref.shape[0]
    count = width // 8
    group = 8
    far = jnp.full((8, LANES), FAR, jnp.float32)
    edge[pl.ds(0, 8), :] = far
    edge[pl.ds(8, 8), :] = in_ref[pl.ds(0, 8), :]
    edge[pl.ds(16, 8), :] = in_ref[pl.ds(width - 8, 8), :]
    edge[pl.ds(24, 8), :] = far

    def rows(at):
        if at < 0:
            return edge[pl.ds(8 + at, 8), :]
        if at > width - 8:
            return edge[pl.ds(16 + at - (width - 8), 8), :]
        return in_ref[pl.ds(at, 8), :]

    def x_pass(low):
        best = [rows(8 * (low + n)) for n in range(group)]
        for rho in range(1, 9):
            plus, minus = {}, {}
            for e in range((KERNEL - rho) // 8 + 1):
                cost = cost_of(8 * e + rho)
                for n in range(group):
                    up, down = low + n + e, low + n - e
                    pair = []
                    if 8 * up + rho < width:
                        if up not in plus:
                            plus[up] = rows(8 * up + rho)
                        pair.append(plus[up])
                    if 8 * down - rho > -8:
                        if down not in minus:
                            minus[down] = rows(8 * down - rho)
                        pair.append(minus[down])
                    if not pair:
                        continue
                    value = pair[0] if len(pair) == 1 else jnp.minimum(pair[0], pair[1])
                    best[n] = jnp.minimum(best[n], value + cost)
        for n in range(group):
            passed[pl.ds(8 * (low + n), 8), :] = best[n]

    copies = []
    each = LANES // yl

    def turn(c):
        block = passed[pl.ds(c * LANES, LANES), :].T
        for y in range(yl):
            done[pl.ds(c * LANES + y, each, stride=yl), :] = block[y * each:(y + 1) * each]

    def send(c):
        cols = pl.ds(c * LANES, LANES)
        copies.append(pltpu.make_async_copy(done.at[cols, :], reg_ref.at[:, cols], sems.at[c]))
        copies[-1].start()

    blocks = width // LANES
    for c in range(blocks):
        first = c * LANES // 8
        x_pass(first)
        if c:
            turn(c - 1)
        for low in range(first + group, first + LANES // 8, group):
            x_pass(low)
        if c:
            send(c - 1)
    turn(blocks - 1)
    send(blocks - 1)
    for copy in copies:
        copy.wait()


def corners_kernel(yl, low_ref, high_ref, corner_ref):
    near = jnp.where(lax.axis_index("gy") == 0, yl - 1, 0)
    rows = [low_ref[pl.ds((2 * k + 1) * yl + near, 1), :] for k in range(LEVELS)]
    rows += [high_ref[pl.ds(2 * k * yl + near, 1), :] for k in range(LEVELS)]
    corner_ref[...] = jnp.concatenate(rows, axis=0)


def tile_tools(mean_ref, yl, width):
    upper = lax.axis_index("gy") == 0

    const = [mean_ref[p] * mean_ref[p] for p in range(PHASES)]
    slope = [-2.0 * mean_ref[p] for p in range(PHASES)]
    for k in range(LEVELS):
        for p in range(PHASES):
            if p >> k & 1:
                const[p] = const[p] - const[p ^ (1 << k)]
                slope[p] = slope[p] - slope[p ^ (1 << k)]

    def forces(h, pic):
        c = [None] + [slope[p] * pic + const[p] for p in range(1, PHASES)]
        out = []
        for k in range(LEVELS):
            others = [n for n in range(LEVELS) if n != k]
            part = [c[1 << k | sum((bits >> i & 1) << n for i, n in enumerate(others))]
                    for bits in range(8)]
            for n in others:
                part = [part[i] + h[n] * part[i + 1] for i in range(0, len(part), 2)]
            out.append(part[0])
        return out

    column = lax.broadcasted_iota(jnp.int32, (8, width), 1)
    sub = lax.broadcasted_iota(jnp.int32, (8, width), 0)

    def along_x(u):
        left = jnp.where(column == 0, 0.0, pltpu.roll(u, 1, 1))
        right = jnp.where(column == width - 1, 0.0, pltpu.roll(u, width - 1, 1))
        return left + right

    def advance(here, near, pic):
        pairs = [heaviside_and_rate(u) for u in here]
        force = forces([h for h, _ in pairs], pic)
        return [
            u + rate * (n - 6.0 * u - f)
            for u, n, (_, rate), f in zip(here, near, pairs, force)
        ]

    def along_y(u, row):
        row_up = jnp.where(upper, row, 0.0)
        row_down = jnp.where(upper, 0.0, row)
        above = jnp.where(sub == yl - 1, row_up, pltpu.roll(u, yl - 1, 0))
        below = jnp.where(sub == 0, row_down, pltpu.roll(u, 1, 0))
        return above + below

    return advance, along_x, along_y


def add_neighbours(lev_ref, low_ref, high_ref, zl, yl):
    def level(k, z):
        if z < 0:
            return low_ref[pl.ds((2 * k + 2 + z) * yl, yl), :]
        if z >= zl:
            return high_ref[pl.ds((2 * k + z - zl) * yl, yl), :]
        return lev_ref[pl.ds((k * zl + z) * yl, yl), :]

    return level


def inner_kernel(zl, yl, mean_ref, lev_ref, ct_ref, low_ref, high_ref, side_ref, out_ref):
    advance, along_x, along_y = tile_tools(mean_ref, yl, lev_ref.shape[1])
    level = add_neighbours(lev_ref, low_ref, high_ref, zl, yl)
    for z in range(zl):
        here = [level(k, z) for k in range(LEVELS)]
        near = [
            level(k, z - 1) + level(k, z + 1) + along_x(here[k])
            + along_y(here[k], side_ref[pl.ds(2 * zl * k + z, 1), :])
            for k in range(LEVELS)
        ]
        value = advance(here, near, ct_ref[pl.ds(z * yl, yl), :])
        for k in range(LEVELS):
            out_ref[pl.ds((k * zl + z) * yl, yl), :] = value[k]


def outer_kernel(zl, yl, gz, mean_ref, lev_ref, ct_ref, low_ref, high_ref, side_ref,
                 corner_ref, inner_ref, out_ref, outer, strip, around, strip_first):
    at_z = lax.axis_index("gz")
    edge = jnp.where(lax.axis_index("gy") == 0, yl - 1, 0)
    plane = zl * yl
    advance, along_x, along_y = tile_tools(mean_ref, yl, lev_ref.shape[1])
    level = add_neighbours(lev_ref, low_ref, high_ref, zl, yl)

    def side(k, z):
        if z < 0:
            return corner_ref[pl.ds(k, 1), :]
        if z >= zl:
            return corner_ref[pl.ds(LEVELS + k, 1), :]
        return side_ref[pl.ds(2 * zl * k + z, 1), :]

    picture_at = pl.ds(2 * LEVELS * yl, yl)
    for n, (z, kept, pic) in enumerate((
        (-1, at_z > 0, low_ref[picture_at, :]), (zl, at_z < gz - 1, high_ref[picture_at, :])
    )):
        here = [level(k, z) for k in range(LEVELS)]
        near = [
            level(k, z - 1) + level(k, z + 1) + along_x(here[k]) + along_y(here[k], side(k, z))
            for k in range(LEVELS)
        ]
        value = advance(here, near, pic)
        for k in range(LEVELS):
            outer[pl.ds((2 * k + n) * yl, yl), :] = jnp.where(kept, value[k], 0.0)

    strip[...] = jnp.zeros_like(strip)
    around[...] = jnp.zeros_like(around)
    for k in range(LEVELS):
        for z in range(-1, zl + 1):
            strip[pl.ds(8 * k + z + 1, 1), :] = side(k, z)
        for z in range(zl):
            around[pl.ds(8 * k + z + 1, 1), :] = (
                lev_ref[pl.ds(k * plane + z * yl + edge, 1), :]
                + side_ref[pl.ds(2 * zl * k + zl + z, 1), :]
            )
    for z in range(zl):
        strip[pl.ds(8 * LEVELS + z + 1, 1), :] = side_ref[pl.ds(2 * zl * LEVELS + z, 1), :]
    here = [strip[pl.ds(8 * k, 8), :] for k in range(LEVELS)]
    near = [
        pltpu.roll(u, 7, 0) + pltpu.roll(u, 1, 0) + along_x(u) + around[pl.ds(8 * k, 8), :]
        for k, u in enumerate(here)
    ]
    value = advance(here, near, strip[pl.ds(8 * LEVELS, 8), :])
    for k in range(LEVELS):
        strip_first[pl.ds(8 * k, 8), :] = value[k]

    def after(k, z):
        if z < 0 or z >= zl:
            return outer[pl.ds((2 * k + (z >= zl)) * yl, yl), :]
        return inner_ref[pl.ds((k * zl + z) * yl, yl), :]

    for z in range(zl):
        here = [after(k, z) for k in range(LEVELS)]
        near = [
            after(k, z - 1) + after(k, z + 1) + along_x(here[k])
            + along_y(here[k], strip_first[pl.ds(8 * k + z + 1, 1), :])
            for k in range(LEVELS)
        ]
        value = advance(here, near, ct_ref[pl.ds(z * yl, yl), :])
        for k in range(LEVELS):
            out_ref[pl.ds(k * plane + z * yl, yl), :] = value[k]


def split_body(levels, ct_image, region_means):
    gz, gy = lax.axis_size("gz"), lax.axis_size("gy")
    _, zl, yl, width = levels.shape
    parts = gz * gy
    share = width // parts
    halo, quarter = share + 4, (share + 4) // 4
    chunk = halo + quarter
    f32 = jnp.float32
    vmem = pl.BlockSpec(memory_space=pltpu.VMEM)
    smem = pl.BlockSpec(memory_space=pltpu.SMEM)
    anywhere = pl.BlockSpec(memory_space=pl.ANY)
    params = pltpu.CompilerParams(vmem_limit_bytes=24 * 1024 * 1024)
    scratch = lambda *dims: pltpu.VMEM(dims, f32)
    shape = lambda rows: jax.ShapeDtypeStruct((rows, width), f32)
    message = (2 * LEVELS + 1) * yl
    packed, lines, image, up, down, side = pl.pallas_call(
        functools.partial(pack_kernel, share, zl, yl),
        out_shape=(
            jax.ShapeDtypeStruct((parts * chunk, LANES), f32),
            shape(LANES), shape(zl * yl), shape(message), shape(message),
            shape(2 * zl * LEVELS + zl),
        ),
        in_specs=[pl.BlockSpec(memory_space=pltpu.HBM)] * 2,
        out_specs=(anywhere,) + (vmem,) * 5,
        scratch_shapes=[
            scratch(width + 8, LANES),
            scratch(width + 16, LANES),
            scratch(4, LANES + 16, LANES),
            scratch(8 * parts + 8, LANES),
            scratch(parts * chunk, LANES),
            pltpu.SemaphoreType.DMA((1 + 2 * width // LANES,)),
        ],
        compiler_params=params,
        name="pack",
    )(
        pltpu.with_memory_space_constraint(levels.reshape(LANES, width), pltpu.HBM),
        pltpu.with_memory_space_constraint(ct_image.reshape(zl * yl, width), pltpu.HBM),
    )
    arrived = lax.all_to_all(
        packed.reshape(parts, chunk, 1, LANES), ("gy", "gz"), split_axis=0, concat_axis=0, tiled=True
    ).reshape(parts * chunk, LANES)

    low = lax.ppermute(up, "gz", [(i, i + 1) for i in range(gz - 1)])
    high = lax.ppermute(down, "gz", [(i + 1, i) for i in range(gz - 1)])
    side = lax.ppermute(side, "gy", [(0, 1), (1, 0)])

    lanes = lambda rows: jax.ShapeDtypeStruct((rows, LANES), f32)
    coefs, penalties = pl.pallas_call(
        functools.partial(tables_kernel, gy, zl, yl),
        out_shape=(lanes(16), lanes(8 * yl * (2 * gy - 1))),
        in_specs=[smem],
        out_specs=(vmem, vmem),
        compiler_params=params,
        name="tables",
    )(region_means)
    slots = (gy * (gz + 2) + 1) * SLOT
    blocks = gy * (gz + 2) * share
    passed = pl.pallas_call(
        functools.partial(middle_kernel, share, gz, gy, zl, yl),
        out_shape=jax.ShapeDtypeStruct((width, LANES), f32),
        in_specs=[vmem] * 3,
        out_specs=anywhere,
        scratch_shapes=[
            scratch(slots, LANES),
            scratch(slots, LANES),
            scratch(slots, LANES),
            scratch(blocks, LANES),
            scratch(zl - 1, blocks, LANES),
            scratch(width, LANES),
            scratch(width, LANES),
            scratch(8, width, LANES),
            pltpu.SemaphoreType.DMA((gy * gz // 4,)),
        ],
        compiler_params=params,
        name="middle",
    )(coefs, penalties, arrived)
    passed, low, high, side = lax.optimization_barrier((passed, low, high, side))
    passed = lax.all_to_all(
        passed.reshape(parts, share, LANES), ("gy", "gz"), split_axis=0, concat_axis=0, tiled=True
    ).reshape(width, LANES)

    corner = pl.pallas_call(
        functools.partial(corners_kernel, yl),
        out_shape=shape(2 * LEVELS),
        in_specs=[vmem, vmem],
        out_specs=vmem,
        compiler_params=params,
        name="corners",
    )(low, high)
    corner = lax.ppermute(corner, "gy", [(0, 1), (1, 0)])
    cost = pl.CostEstimate(flops=5_000_000, bytes_accessed=1_000_000, transcendentals=0)
    inner = pl.pallas_call(
        functools.partial(inner_kernel, zl, yl),
        out_shape=shape(LANES),
        in_specs=[smem] + [vmem] * 5,
        out_specs=vmem,
        compiler_params=params,
        cost_estimate=cost,
        name="inner",
    )(region_means, lines, image, low, high, side)
    evolved = pl.pallas_call(
        functools.partial(outer_kernel, zl, yl, gz),
        out_shape=shape(LANES),
        in_specs=[smem] + [vmem] * 7,
        out_specs=vmem,
        scratch_shapes=[
            scratch(2 * LEVELS * yl, width),
            scratch(8 * (LEVELS + 1), width),
            scratch(8 * LEVELS, width),
            scratch(8 * LEVELS, width),
        ],
        compiler_params=params,
        cost_estimate=cost,
        name="outer",
    )(region_means, lines, image, low, high, side, corner, inner)

    regularized = pl.pallas_call(
        functools.partial(finish_kernel, yl),
        out_shape=shape(LANES),
        in_specs=[vmem],
        out_specs=anywhere,
        scratch_shapes=[
            scratch(32, LANES),
            scratch(width, LANES),
            scratch(width + 8, LANES),
            pltpu.SemaphoreType.DMA((width // LANES,)),
        ],
        compiler_params=params,
        name="finish",
    )(passed)
    return evolved.reshape(levels.shape), regularized.reshape(levels.shape)


def body(levels, ct_image, region_means):
    gz, gy = lax.axis_size("gz"), lax.axis_size("gy")
    parts = gz * gy
    count, zl, yl, width = levels.shape
    fits = count == LEVELS and count * zl * yl == LANES and yl == 8 and zl >= 2
    fits = fits and gy == 2 and gz % 8 == 0 and gz * zl <= KERNEL
    fits = fits and width == 4 * LANES and parts == 32
    if fits:
        return split_body(levels, ct_image, region_means)
    return portable_body(levels, ct_image, region_means)


def solution(mesh):
    return jax.shard_map(
        body,
        mesh=mesh,
        in_specs=(P(None, "gz", "gy", None), P("gz", "gy", None), P()),
        out_specs=(P(None, "gz", "gy", None), P(None, "gz", "gy", None)),
        check_vma=False,
    )
```

```python
import functools
import math

import jax
import jax.numpy as jnp
import numpy as np
from jax import lax
from jax.experimental import pallas as pl
from jax.experimental.pallas import tpu as pltpu
from jax.sharding import PartitionSpec as P

LEVELS = 4
PHASES = 16
UPDATES = 2
KERNEL = 200
LANES = 128


PENALTY = 0.0005
STEP_SIZE = 0.5
FAR = 1e30


def with_halo(block, sides, width):
    for axis, dim in sides:
        count = lax.axis_size(axis)
        forward = [(i, i + 1) for i in range(count - 1)]
        backward = [(target, source) for source, target in forward]
        low = lax.ppermute(
            lax.slice_in_dim(block, block.shape[dim] - width, None, axis=dim), axis, forward
        )
        high = lax.ppermute(lax.slice_in_dim(block, 0, width, axis=dim), axis, backward)
        block = jnp.concatenate([low, block, high], axis=dim)
    return block


def evolve(level_pad, picture, region_means):
    interior = level_pad[:, 1:-1, 1:-1, :]
    side_x = jnp.pad(interior, ((0, 0), (0, 0), (0, 0), (1, 1)))
    laplace = level_pad[:, 2:, 1:-1, :] + level_pad[:, :-2, 1:-1, :]
    laplace = laplace + level_pad[:, 1:-1, 2:, :] + level_pad[:, 1:-1, :-2, :]
    laplace = laplace + side_x[..., 2:] + side_x[..., :-2] - 6.0 * interior
    heaviside = 0.5 + jnp.arctan(interior) / math.pi
    delta_term = 1.0 / (math.pi * (1.0 + interior * interior))
    forces = [jnp.zeros_like(interior[0]) for level_id in range(LEVELS)]
    for phase_id in range(PHASES):
        differ = picture - region_means[phase_id]
        energy = differ * differ
        factors = []
        for level_id in range(LEVELS):
            if phase_id >> level_id & 1:
                factors.append(heaviside[level_id])
            else:
                factors.append(1.0 - heaviside[level_id])
        for level_id in range(LEVELS):
            sign_value = 1.0 if phase_id >> level_id & 1 else -1.0
            others = energy
            for other_id in range(LEVELS):
                if other_id != level_id:
                    others = others * factors[other_id]
            forces[level_id] = forces[level_id] + sign_value * others
    force_all = jnp.stack(forces, axis=0)
    return interior + STEP_SIZE * delta_term * (laplace - force_all)


def minplus_lines(field_in, line_axis, kernel_reach):
    moved_field = jnp.moveaxis(field_in, line_axis, -1)
    line_shape = moved_field.shape
    line_len = line_shape[-1]
    line_rows = moved_field.reshape(-1, line_len)
    row_count = line_rows.shape[0]
    positions = jnp.arange(line_len, dtype=jnp.float32)
    distance = positions[:, None] - positions[None, :]
    penalty_table = jnp.where(
        jnp.abs(distance) <= kernel_reach, PENALTY * (distance * distance), jnp.inf
    )
    row_limit = max(1, 1048576 // (line_len * line_len))
    row_block = 1
    while row_block * 2 <= row_limit and row_count % (row_block * 2) == 0:
        row_block = row_block * 2
    grouped = line_rows.reshape(row_count // row_block, row_block, line_len)

    def block_min(block_rows):
        return jnp.min(block_rows[:, None, :] + penalty_table[None, :, :], axis=2)

    result_rows = lax.map(block_min, grouped)
    return jnp.moveaxis(result_rows.reshape(line_shape), -1, line_axis)


def portable_body(levels, ct_image, region_means):
    current = levels
    for _ in range(UPDATES):
        padded = with_halo(current, (("gz", 1), ("gy", 2)), 1)
        current = evolve(padded, ct_image, region_means)
    field = minplus_lines(current, 3, KERNEL)
    for axis, dim in (("gz", 1), ("gy", 2)):
        lines = lax.all_to_all(field, axis, split_axis=3, concat_axis=dim, tiled=True)
        lines = minplus_lines(lines, dim, KERNEL)
        field = lax.all_to_all(lines, axis, split_axis=dim, concat_axis=3, tiled=True)
    return current, field


def pack_kernel(share, zl, yl, lev_hbm, ct_hbm, out_hbm, ct_ref, stage, lines, turned, picture, out_ref, sems):
    width = ct_ref.shape[1]
    parts = width // share
    blocks = width // LANES
    halo, quarter = share + 4, (share + 4) // 4
    chunk = halo + quarter
    count = LEVELS * zl
    tile = zl * yl
    arriving = [pltpu.make_async_copy(ct_hbm, ct_ref, sems.at[0])]
    for b in range(blocks):
        here = stage.at[pl.ds(b * LANES, LANES), :]
        source = lev_hbm.at[:, pl.ds(b * LANES, LANES)]
        arriving.append(pltpu.make_async_copy(source, here, sems.at[1 + b]))
    for copy in arriving:
        copy.start()
    lines[pl.ds(0, 8), :] = jnp.zeros((8, LANES), jnp.float32)
    lines[pl.ds(8 + width, 8), :] = jnp.zeros((8, LANES), jnp.float32)

    for copy in arriving:
        copy.wait()
    across = jnp.concatenate([ct_ref[:, b * LANES:(b + 1) * LANES] for b in range(blocks)], axis=0).T
    for n in range(blocks):
        turn = lambda rows, by: pltpu.roll(rows, by % blocks * tile, 1) if by % blocks else rows
        turned[n, pl.ds(0, 8), :] = turn(across[LANES - 8:], n + 1)
        turned[n, pl.ds(8, LANES), :] = turn(across, n)
        turned[n, pl.ds(8 + LANES, 8), :] = turn(across[:8], n - 1)
    group = lax.broadcasted_iota(jnp.int32, (8, LANES), 1) // tile
    each = LANES // share
    for r in range(parts):
        b, at = r // each, 8 + r % each * share - 2
        value = None
        for t in range(4):
            run = turned[(t - b) % blocks, pl.ds(at + quarter * t, 8), :]
            value = run if value is None else jnp.where(group >= t, run, value)
        picture[pl.ds(8 * r, 8), :] = value
    for b in range(blocks):
        block = [stage[pl.ds(b * LANES + y, count, stride=yl), :] for y in range(yl)]
        lines[pl.ds(8 + b * LANES, LANES), :] = jnp.concatenate(block, axis=0).T

    leaving = []
    sub = lax.broadcasted_iota(jnp.int32, (8, LANES), 0)

    def out_tile(tile):
        value = None
        for r in range(8 * tile // chunk, min((8 * tile + 7) // chunk + 1, parts)):
            for source, begin, length, origin in (
                (picture, r * chunk, quarter, 8 * r),
                (lines, r * chunk + quarter, halo, 6 + r * share),
            ):
                if begin + length <= 8 * tile or begin >= 8 * tile + 8:
                    continue
                piece = source[pl.ds(8 * tile - begin + origin, 8), :]
                value = piece if value is None else jnp.where(sub >= begin - 8 * tile, piece, value)
        return value

    start = 0
    for b in range(blocks):
        known = parts if b + 1 == blocks else (b + 1) * LANES // share - 1
        stop = known * chunk // 8 * 8
        for tile in range(start // 8, stop // 8):
            out_ref[pl.ds(8 * tile, 8), :] = out_tile(tile)
        rows = pl.ds(start, stop - start)
        leaving.append(
            pltpu.make_async_copy(out_ref.at[rows, :], out_hbm.at[rows, :], sems.at[1 + blocks + b])
        )
        leaving[-1].start()
        start = stop
    for copy in leaving:
        copy.wait()


HALF_ANGLE = (
    0.6366196870803833, -0.21219870448112488, 0.12714172899723053, -0.0893140509724617,
    0.06329755485057831, -0.03813650459051132, 0.015633534640073776, -0.0030433274805545807,
)


def heaviside_and_rate(u):
    s = 1.0 + u * u
    q = lax.rsqrt(s)
    r = u / (1.0 + s * q)
    y = r * r
    p = HALF_ANGLE[-1]
    for c in HALF_ANGLE[-2::-1]:
        p = p * y + c
    return 0.5 + r * p, (q * q) * (STEP_SIZE / math.pi)


def cost_of(d):
    return float(np.float32(PENALTY) * np.float32(d * d))


def tables_kernel(gy, zl, yl, mean_ref, coef_ref, ypen):
    lane = lax.broadcasted_iota(jnp.int32, (1, LANES), 1)
    level = lane // zl % LEVELS
    y = lane // (LEVELS * zl)

    def mean_of(bits, own):
        value = jnp.zeros((1, LANES), jnp.float32)
        for k in range(LEVELS):
            phase = own << k
            for n in range(3):
                phase |= (bits >> n & 1) << ((k + 1 + n) % LEVELS)
            value = jnp.where(level == k, mean_ref[phase], value)
        return value

    slope, const = [], []
    for bits in range(8):
        low, high = mean_of(bits, 0), mean_of(bits, 1)
        slope.append(-2.0 * (high - low))
        const.append((high - low) * (high + low))
    for n in range(3):
        for bits in range(8):
            if bits >> n & 1:
                slope[bits] = slope[bits] - slope[bits ^ (1 << n)]
                const[bits] = const[bits] - const[bits ^ (1 << n)]
    for n in range(8):
        coef_ref[pl.ds(n, 1), :] = slope[n]
        coef_ref[pl.ds(8 + n, 1), :] = const[n]

    for gap in range(-(gy - 1), gy):
        for turn in range(yl):
            d = (yl * gap + y - (y + turn) % yl).astype(jnp.float32)
            pen = jnp.where(jnp.abs(d) <= KERNEL, PENALTY * (d * d), FAR)
            ypen[pl.ds(8 * ((gap + gy - 1) * yl + turn), 8), :] = jnp.broadcast_to(pen, (8, LANES))


SLOT = 32


def middle_kernel(share, gz, gy, zl, yl, coef_ref, ypen, in_ref, out_ref, levels, picture,
                  first, evolved, shifted, zdone, done, kept, sems):
    parts = gz * gy
    halo, quarter = share + 4, (share + 4) // 4
    chunk = halo + quarter
    tile = zl * yl
    deep = gz + 2
    me = lax.axis_index("gy") * gz + lax.axis_index("gz")

    lane = lax.broadcasted_iota(jnp.int32, (1, LANES), 1)
    level = lane // zl % LEVELS
    z = lane % zl
    y = lane // (LEVELS * zl)

    def moved(value, index):
        return jnp.take_along_axis(
            value, jnp.broadcast_to(index, value.shape), axis=1, mode="promise_in_bounds"
        )

    def z_turned(value, turn):
        return moved(value, lane + (z + turn) % zl - z)

    def level_turned(value, turn):
        return moved(value, lane + ((level + turn) % LEVELS - level) * zl)

    def y_turned(value, turn):
        return pltpu.roll(value, LANES - turn * LEVELS * zl, 1)

    def stacked(blocks):
        return jnp.concatenate(blocks, axis=0)

    def row_of(a, b, x):
        return (b * deep + a + 1) * SLOT + 8 + x

    zero = jnp.zeros((SLOT, LANES), jnp.float32)
    for b in range(gy):
        for a in (-1, gz):
            levels[pl.ds(row_of(a, b, -8), SLOT), :] = zero
            first[pl.ds(row_of(a, b, -8), SLOT), :] = zero
        for a in range(gz):
            source = (b * gz + a) * chunk + quarter
            levels[pl.ds(row_of(a, b, -2), halo), :] = in_ref[pl.ds(source, halo), :]
        for a in range(0, gz, 4):
            batch = range(a, a + 4)
            packed = stacked([in_ref[pl.ds((b * gz + n) * chunk, 8), :] for n in batch])
            for t in range(4):
                run = moved(packed, t * tile + z * yl + y)
                for n in batch:
                    at = 8 * (n - a)
                    rows = pl.ds(row_of(n, b, t * quarter - 2), quarter)
                    picture[rows, :] = run[at:at + quarter]

    coefs = [coef_ref[pl.ds(n, 1), :] for n in range(16)]
    slope, const = coefs[:8], coefs[8:]

    def step(read, tiles, f):
        def beside(dz, dy):
            none = jnp.zeros_like(read(tiles[0], 0, 0, 0))
            return stacked([
                read(tile, dz, dy, 0) if 0 <= tile[1] + dy < gy else none for tile in tiles
            ])

        here = beside(0, 0)
        h, rate = heaviside_and_rate(here)
        near = stacked([read(t, 0, 0, -1) + read(t, 0, 0, 1) for t in tiles]) - 6.0 * here
        near = near + z_turned(jnp.where(z == 0, beside(1, 0), here), 1)
        near = near + z_turned(jnp.where(z == zl - 1, beside(-1, 0), here), zl - 1)
        near = near + y_turned(jnp.where(y == 0, beside(0, 1), here), 1)
        near = near + y_turned(jnp.where(y == yl - 1, beside(0, -1), here), yl - 1)
        h1, h2, h3 = (level_turned(h, turn) for turn in (1, 2, 3))
        g = lambda bits: f(bits) + h1 * f(bits | 1)
        force = (g(0) + h2 * g(2)) + h3 * (g(4) + h2 * g(6))
        return here + rate * (near - force)

    def run_of(ref):
        return lambda t, dz, dy, dx: ref[pl.ds(row_of(t[0] + dz, t[1] + dy, dx), share), :]

    def terms(pic):
        return lambda bits: slope[bits] * pic + const[bits]

    batches = [[(a + n, b) for n in range(4)] for b in range(gy) for a in range(0, gz, 4)]
    for tiles in batches:
        pic = stacked([run_of(picture)(t, 0, 0, 0) for t in tiles])
        f = [terms(pic)(bits) for bits in range(8)]
        at = pl.ds((tiles[0][1] * gz + tiles[0][0]) * share, 4 * share)
        for bits in range(8):
            kept[bits, at, :] = f[bits]
        value = step(run_of(levels), tiles, lambda bits: f[bits])
        for n, (a, b) in enumerate(tiles):
            first[pl.ds(row_of(a, b, 0), share), :] = value[n * share:(n + 1) * share]

    def across(ref):
        return lambda t, dz, dy, dx: ref[pl.ds(row_of(dz, t[1] + dy, t[0] + dx), gz, stride=SLOT), :]

    ends = [(x, b) for x in (-1, share) for b in range(gy)]
    pic = stacked([across(picture)(t, 0, 0, 0) for t in ends])
    value = step(across(levels), ends, terms(pic))
    for n, (x, b) in enumerate(ends):
        outside = (me == 0) if x < 0 else (me == parts - 1)
        rows = value[n * gz:(n + 1) * gz]
        first[pl.ds(row_of(0, b, x), gz, stride=SLOT), :] = jnp.where(outside, 0.0, rows)

    def block_of(a, b):
        return (b * deep + a + 1) * share

    far = jnp.full((share, LANES), FAR, jnp.float32)
    for b in range(gy):
        for a in (-1, gz):
            evolved[pl.ds(block_of(a, b), share), :] = far
    for tiles in batches:
        at = pl.ds((tiles[0][1] * gz + tiles[0][0]) * share, 4 * share)
        f = lambda bits: kept[bits, at, :]
        evolved[pl.ds(block_of(*tiles[0]), 4 * share), :] = step(run_of(first), tiles, f)

    for b in range(gy):
        for a in range(-1, gz, 4):
            count = min(4, gz - a) * share
            here = evolved[pl.ds(block_of(a, b), count), :]
            above = evolved[pl.ds(block_of(a + 1, b), count), :]
            for turn in range(1, zl):
                value = z_turned(jnp.where(z < turn, above, here), turn)
                shifted[turn - 1, pl.ds(block_of(a, b), count), :] = value

    def z_unit(half, b, low):
        count = 8

        def at(d, n):
            a, turn = low + n + d // zl, d % zl
            if a < (-1 if turn else 0) or a >= gz:
                return None
            if (a, turn) not in loaded:
                rows = pl.ds(block_of(a, b) + 8 * half, 8)
                loaded[a, turn] = shifted[turn - 1, rows, :] if turn else evolved[rows, :]
            return loaded[a, turn]

        loaded = {}
        best = [at(0, n) for n in range(count)]
        for turn in range(zl):
            loaded = {}
            for d in range(turn or zl, min(gz * zl, KERNEL + 1), zl):
                for n in range(count):
                    pair = [v for v in (at(d, n), at(-d, n)) if v is not None]
                    if pair:
                        value = pair[0] if len(pair) == 1 else jnp.minimum(pair[0], pair[1])
                        best[n] = jnp.minimum(best[n], value + cost_of(d))
        for n in range(count):
            zdone[pl.ds((b * gz + low + n) * share + 8 * half, 8), :] = best[n]

    def y_unit(half, low):
        count = 4
        best = [None] * gy
        for other in range(gy):
            starts = [(other * gz + low + n) * share + 8 * half for n in range(count)]
            whole = stacked([zdone[pl.ds(at, 8), :] for at in starts])
            for turn in range(yl):
                value = y_turned(whole, turn) if turn else whole
                for b in range(gy):
                    at = (b - other + gy - 1) * yl + turn
                    new = value + stacked([ypen[pl.ds(8 * at, 8), :]] * count)
                    best[b] = new if best[b] is None else jnp.minimum(best[b], new)
        for b in range(gy):
            for n in range(count):
                rows = pl.ds((b * gz + low + n) * share + 8 * half, 8)
                done[rows, :] = best[b][8 * n:8 * n + 8]

    halves = share // 8
    copies = []
    for half in range(halves + 1):
        z_units = [(b, low) for b in range(gy) for low in range(0, gz, 8)] if half < halves else []
        y_units = list(range(0, gz, 4)) if half else []
        for n in range(max(len(z_units), len(y_units))):
            if n < len(z_units):
                z_unit(half, *z_units[n])
            if n < len(y_units):
                y_unit(half - 1, y_units[n])
                if half == halves:
                    for b in range(gy):
                        rows = pl.ds((b * gz + y_units[n]) * share, 4 * share)
                        sem = sems.at[len(copies)]
                        copies.append(pltpu.make_async_copy(done.at[rows, :], out_ref.at[rows, :], sem))
                        copies[-1].start()
    for copy in copies:
        copy.wait()


def finish_kernel(yl, in_ref, reg_ref, edge, passed, done, sems):
    width = in_ref.shape[0]
    count = width // 8
    group = 8
    far = jnp.full((8, LANES), FAR, jnp.float32)
    edge[pl.ds(0, 8), :] = far
    edge[pl.ds(8, 8), :] = in_ref[pl.ds(0, 8), :]
    edge[pl.ds(16, 8), :] = in_ref[pl.ds(width - 8, 8), :]
    edge[pl.ds(24, 8), :] = far

    def rows(at):
        if at < 0:
            return edge[pl.ds(8 + at, 8), :]
        if at > width - 8:
            return edge[pl.ds(16 + at - (width - 8), 8), :]
        return in_ref[pl.ds(at, 8), :]

    def x_pass(low):
        best = [rows(8 * (low + n)) for n in range(group)]
        for rho in range(1, 9):
            plus, minus = {}, {}
            for e in range((KERNEL - rho) // 8 + 1):
                cost = cost_of(8 * e + rho)
                for n in range(group):
                    up, down = low + n + e, low + n - e
                    pair = []
                    if 8 * up + rho < width:
                        if up not in plus:
                            plus[up] = rows(8 * up + rho)
                        pair.append(plus[up])
                    if 8 * down - rho > -8:
                        if down not in minus:
                            minus[down] = rows(8 * down - rho)
                        pair.append(minus[down])
                    if not pair:
                        continue
                    value = pair[0] if len(pair) == 1 else jnp.minimum(pair[0], pair[1])
                    best[n] = jnp.minimum(best[n], value + cost)
        for n in range(group):
            passed[pl.ds(8 * (low + n), 8), :] = best[n]

    copies = []
    each = LANES // yl

    def turn(c):
        block = passed[pl.ds(c * LANES, LANES), :].T
        for y in range(yl):
            done[pl.ds(c * LANES + y, each, stride=yl), :] = block[y * each:(y + 1) * each]

    def send(c):
        cols = pl.ds(c * LANES, LANES)
        copies.append(pltpu.make_async_copy(done.at[cols, :], reg_ref.at[:, cols], sems.at[c]))
        copies[-1].start()

    blocks = width // LANES
    for c in range(blocks):
        first = c * LANES // 8
        x_pass(first)
        if c:
            turn(c - 1)
        for low in range(first + group, first + LANES // 8, group):
            x_pass(low)
        if c:
            send(c - 1)
    turn(blocks - 1)
    send(blocks - 1)
    for copy in copies:
        copy.wait()


def edges_kernel(zl, yl, lev_hbm, ct_hbm, lev, ct_ref, up_ref, down_ref, side_ref, sems):
    copies = [
        pltpu.make_async_copy(lev_hbm, lev, sems.at[0]),
        pltpu.make_async_copy(ct_hbm, ct_ref, sems.at[1]),
    ]
    for copy in copies:
        copy.start()
    for copy in copies:
        copy.wait()
    plane = zl * yl
    for k in range(LEVELS):
        at = pl.ds(2 * k * yl, 2 * yl)
        up_ref[at, :] = lev[pl.ds((k + 1) * plane - 2 * yl, 2 * yl), :]
        down_ref[at, :] = lev[pl.ds(k * plane, 2 * yl), :]
    at = pl.ds(2 * LEVELS * yl, yl)
    up_ref[at, :] = ct_ref[pl.ds(plane - yl, yl), :]
    down_ref[at, :] = ct_ref[pl.ds(0, yl), :]
    upper = lax.axis_index("gy") == 0
    near = jnp.where(upper, yl - 1, 0)
    next_near = jnp.where(upper, yl - 2, 1)
    for k in range(LEVELS):
        for z in range(zl):
            base = k * plane + z * yl
            side_ref[pl.ds(2 * zl * k + z, 1), :] = lev[pl.ds(base + near, 1), :]
            side_ref[pl.ds(2 * zl * k + zl + z, 1), :] = lev[pl.ds(base + next_near, 1), :]
    for z in range(zl):
        side_ref[pl.ds(2 * zl * LEVELS + z, 1), :] = ct_ref[pl.ds(z * yl + near, 1), :]


def corners_kernel(yl, low_ref, high_ref, corner_ref):
    near = jnp.where(lax.axis_index("gy") == 0, yl - 1, 0)
    rows = [low_ref[pl.ds((2 * k + 1) * yl + near, 1), :] for k in range(LEVELS)]
    rows += [high_ref[pl.ds(2 * k * yl + near, 1), :] for k in range(LEVELS)]
    corner_ref[...] = jnp.concatenate(rows, axis=0)


def tile_tools(mean_ref, yl, width):
    upper = lax.axis_index("gy") == 0

    const = [mean_ref[p] * mean_ref[p] for p in range(PHASES)]
    slope = [-2.0 * mean_ref[p] for p in range(PHASES)]
    for k in range(LEVELS):
        for p in range(PHASES):
            if p >> k & 1:
                const[p] = const[p] - const[p ^ (1 << k)]
                slope[p] = slope[p] - slope[p ^ (1 << k)]

    def forces(h, pic):
        c = [None] + [slope[p] * pic + const[p] for p in range(1, PHASES)]
        out = []
        for k in range(LEVELS):
            others = [n for n in range(LEVELS) if n != k]
            part = [c[1 << k | sum((bits >> i & 1) << n for i, n in enumerate(others))]
                    for bits in range(8)]
            for n in others:
                part = [part[i] + h[n] * part[i + 1] for i in range(0, len(part), 2)]
            out.append(part[0])
        return out

    column = lax.broadcasted_iota(jnp.int32, (8, width), 1)
    sub = lax.broadcasted_iota(jnp.int32, (8, width), 0)

    def along_x(u):
        left = jnp.where(column == 0, 0.0, pltpu.roll(u, 1, 1))
        right = jnp.where(column == width - 1, 0.0, pltpu.roll(u, width - 1, 1))
        return left + right

    def advance(here, near, pic):
        pairs = [heaviside_and_rate(u) for u in here]
        force = forces([h for h, _ in pairs], pic)
        return [
            u + rate * (n - 6.0 * u - f)
            for u, n, (_, rate), f in zip(here, near, pairs, force)
        ]

    def along_y(u, row):
        row_up = jnp.where(upper, row, 0.0)
        row_down = jnp.where(upper, 0.0, row)
        above = jnp.where(sub == yl - 1, row_up, pltpu.roll(u, yl - 1, 0))
        below = jnp.where(sub == 0, row_down, pltpu.roll(u, 1, 0))
        return above + below

    return advance, along_x, along_y


def add_neighbours(lev_ref, low_ref, high_ref, zl, yl):
    def level(k, z):
        if z < 0:
            return low_ref[pl.ds((2 * k + 2 + z) * yl, yl), :]
        if z >= zl:
            return high_ref[pl.ds((2 * k + z - zl) * yl, yl), :]
        return lev_ref[pl.ds((k * zl + z) * yl, yl), :]

    return level


def inner_kernel(zl, yl, mean_ref, lev_ref, ct_ref, low_ref, high_ref, side_ref, out_ref):
    advance, along_x, along_y = tile_tools(mean_ref, yl, lev_ref.shape[1])
    level = add_neighbours(lev_ref, low_ref, high_ref, zl, yl)
    for z in range(zl):
        here = [level(k, z) for k in range(LEVELS)]
        near = [
            level(k, z - 1) + level(k, z + 1) + along_x(here[k])
            + along_y(here[k], side_ref[pl.ds(2 * zl * k + z, 1), :])
            for k in range(LEVELS)
        ]
        value = advance(here, near, ct_ref[pl.ds(z * yl, yl), :])
        for k in range(LEVELS):
            out_ref[pl.ds((k * zl + z) * yl, yl), :] = value[k]


def outer_kernel(zl, yl, gz, mean_ref, lev_ref, ct_ref, low_ref, high_ref, side_ref,
                 corner_ref, inner_ref, out_ref, outer, strip, around, strip_first):
    at_z = lax.axis_index("gz")
    edge = jnp.where(lax.axis_index("gy") == 0, yl - 1, 0)
    plane = zl * yl
    advance, along_x, along_y = tile_tools(mean_ref, yl, lev_ref.shape[1])
    level = add_neighbours(lev_ref, low_ref, high_ref, zl, yl)

    def side(k, z):
        if z < 0:
            return corner_ref[pl.ds(k, 1), :]
        if z >= zl:
            return corner_ref[pl.ds(LEVELS + k, 1), :]
        return side_ref[pl.ds(2 * zl * k + z, 1), :]

    picture_at = pl.ds(2 * LEVELS * yl, yl)
    for n, (z, kept, pic) in enumerate((
        (-1, at_z > 0, low_ref[picture_at, :]), (zl, at_z < gz - 1, high_ref[picture_at, :])
    )):
        here = [level(k, z) for k in range(LEVELS)]
        near = [
            level(k, z - 1) + level(k, z + 1) + along_x(here[k]) + along_y(here[k], side(k, z))
            for k in range(LEVELS)
        ]
        value = advance(here, near, pic)
        for k in range(LEVELS):
            outer[pl.ds((2 * k + n) * yl, yl), :] = jnp.where(kept, value[k], 0.0)

    strip[...] = jnp.zeros_like(strip)
    around[...] = jnp.zeros_like(around)
    for k in range(LEVELS):
        for z in range(-1, zl + 1):
            strip[pl.ds(8 * k + z + 1, 1), :] = side(k, z)
        for z in range(zl):
            around[pl.ds(8 * k + z + 1, 1), :] = (
                lev_ref[pl.ds(k * plane + z * yl + edge, 1), :]
                + side_ref[pl.ds(2 * zl * k + zl + z, 1), :]
            )
    for z in range(zl):
        strip[pl.ds(8 * LEVELS + z + 1, 1), :] = side_ref[pl.ds(2 * zl * LEVELS + z, 1), :]
    here = [strip[pl.ds(8 * k, 8), :] for k in range(LEVELS)]
    near = [
        pltpu.roll(u, 7, 0) + pltpu.roll(u, 1, 0) + along_x(u) + around[pl.ds(8 * k, 8), :]
        for k, u in enumerate(here)
    ]
    value = advance(here, near, strip[pl.ds(8 * LEVELS, 8), :])
    for k in range(LEVELS):
        strip_first[pl.ds(8 * k, 8), :] = value[k]

    def after(k, z):
        if z < 0 or z >= zl:
            return outer[pl.ds((2 * k + (z >= zl)) * yl, yl), :]
        return inner_ref[pl.ds((k * zl + z) * yl, yl), :]

    for z in range(zl):
        here = [after(k, z) for k in range(LEVELS)]
        near = [
            after(k, z - 1) + after(k, z + 1) + along_x(here[k])
            + along_y(here[k], strip_first[pl.ds(8 * k + z + 1, 1), :])
            for k in range(LEVELS)
        ]
        value = advance(here, near, ct_ref[pl.ds(z * yl, yl), :])
        for k in range(LEVELS):
            out_ref[pl.ds(k * plane + z * yl, yl), :] = value[k]


def split_body(levels, ct_image, region_means):
    gz, gy = lax.axis_size("gz"), lax.axis_size("gy")
    _, zl, yl, width = levels.shape
    parts = gz * gy
    share = width // parts
    halo, quarter = share + 4, (share + 4) // 4
    chunk = halo + quarter
    f32 = jnp.float32
    vmem = pl.BlockSpec(memory_space=pltpu.VMEM)
    smem = pl.BlockSpec(memory_space=pltpu.SMEM)
    anywhere = pl.BlockSpec(memory_space=pl.ANY)
    params = pltpu.CompilerParams(vmem_limit_bytes=24 * 1024 * 1024)
    scratch = lambda *dims: pltpu.VMEM(dims, f32)
    shape = lambda rows: jax.ShapeDtypeStruct((rows, width), f32)
    in_hbm = lambda x: pltpu.with_memory_space_constraint(x, pltpu.HBM)
    lines, image = levels.reshape(LANES, width), ct_image.reshape(zl * yl, width)
    packed = pl.pallas_call(
        functools.partial(pack_kernel, share, zl, yl),
        out_shape=jax.ShapeDtypeStruct((parts * chunk, LANES), f32),
        in_specs=[pl.BlockSpec(memory_space=pltpu.HBM)] * 2,
        out_specs=anywhere,
        scratch_shapes=[
            scratch(zl * yl, width),
            scratch(width + 8, LANES),
            scratch(width + 16, LANES),
            scratch(4, LANES + 16, LANES),
            scratch(8 * parts + 8, LANES),
            scratch(parts * chunk, LANES),
            pltpu.SemaphoreType.DMA((1 + 2 * width // LANES,)),
        ],
        compiler_params=params,
        name="pack",
    )(in_hbm(lines), in_hbm(image))
    packed, lines, image = lax.optimization_barrier((packed, lines, image))
    arrived = lax.all_to_all(
        packed.reshape(parts, chunk, 1, LANES), ("gy", "gz"), split_axis=0, concat_axis=0, tiled=True
    ).reshape(parts * chunk, LANES)

    message = (2 * LEVELS + 1) * yl
    lines, image, up, down, side = pl.pallas_call(
        functools.partial(edges_kernel, zl, yl),
        out_shape=(shape(LANES), shape(zl * yl), shape(message), shape(message),
                   shape(2 * zl * LEVELS + zl)),
        in_specs=[pl.BlockSpec(memory_space=pltpu.HBM)] * 2,
        out_specs=(vmem,) * 5,
        scratch_shapes=[pltpu.SemaphoreType.DMA((2,))],
        compiler_params=params,
        name="edges",
    )(in_hbm(lines), in_hbm(image))
    low = lax.ppermute(up, "gz", [(i, i + 1) for i in range(gz - 1)])
    high = lax.ppermute(down, "gz", [(i + 1, i) for i in range(gz - 1)])
    side = lax.ppermute(side, "gy", [(0, 1), (1, 0)])

    lanes = lambda rows: jax.ShapeDtypeStruct((rows, LANES), f32)
    coefs, penalties = pl.pallas_call(
        functools.partial(tables_kernel, gy, zl, yl),
        out_shape=(lanes(16), lanes(8 * yl * (2 * gy - 1))),
        in_specs=[smem],
        out_specs=(vmem, vmem),
        compiler_params=params,
        name="tables",
    )(region_means)
    slots = (gy * (gz + 2) + 1) * SLOT
    blocks = gy * (gz + 2) * share
    passed = pl.pallas_call(
        functools.partial(middle_kernel, share, gz, gy, zl, yl),
        out_shape=jax.ShapeDtypeStruct((width, LANES), f32),
        in_specs=[vmem] * 3,
        out_specs=anywhere,
        scratch_shapes=[
            scratch(slots, LANES),
            scratch(slots, LANES),
            scratch(slots, LANES),
            scratch(blocks, LANES),
            scratch(zl - 1, blocks, LANES),
            scratch(width, LANES),
            scratch(width, LANES),
            scratch(8, width, LANES),
            pltpu.SemaphoreType.DMA((gy * gz // 4,)),
        ],
        compiler_params=params,
        name="middle",
    )(coefs, penalties, arrived)
    passed, low, high, side = lax.optimization_barrier((passed, low, high, side))
    passed = lax.all_to_all(
        passed.reshape(parts, share, LANES), ("gy", "gz"), split_axis=0, concat_axis=0, tiled=True
    ).reshape(width, LANES)

    corner = pl.pallas_call(
        functools.partial(corners_kernel, yl),
        out_shape=shape(2 * LEVELS),
        in_specs=[vmem, vmem],
        out_specs=vmem,
        compiler_params=params,
        name="corners",
    )(low, high)
    corner = lax.ppermute(corner, "gy", [(0, 1), (1, 0)])
    cost = pl.CostEstimate(flops=5_000_000, bytes_accessed=1_000_000, transcendentals=0)
    inner = pl.pallas_call(
        functools.partial(inner_kernel, zl, yl),
        out_shape=shape(LANES),
        in_specs=[smem] + [vmem] * 5,
        out_specs=vmem,
        compiler_params=params,
        cost_estimate=cost,
        name="inner",
    )(region_means, lines, image, low, high, side)
    evolved = pl.pallas_call(
        functools.partial(outer_kernel, zl, yl, gz),
        out_shape=shape(LANES),
        in_specs=[smem] + [vmem] * 7,
        out_specs=vmem,
        scratch_shapes=[
            scratch(2 * LEVELS * yl, width),
            scratch(8 * (LEVELS + 1), width),
            scratch(8 * LEVELS, width),
            scratch(8 * LEVELS, width),
        ],
        compiler_params=params,
        cost_estimate=cost,
        name="outer",
    )(region_means, lines, image, low, high, side, corner, inner)

    regularized = pl.pallas_call(
        functools.partial(finish_kernel, yl),
        out_shape=shape(LANES),
        in_specs=[vmem],
        out_specs=anywhere,
        scratch_shapes=[
            scratch(32, LANES),
            scratch(width, LANES),
            scratch(width + 8, LANES),
            pltpu.SemaphoreType.DMA((width // LANES,)),
        ],
        compiler_params=params,
        name="finish",
    )(passed)
    return evolved.reshape(levels.shape), regularized.reshape(levels.shape)


def body(levels, ct_image, region_means):
    gz, gy = lax.axis_size("gz"), lax.axis_size("gy")
    parts = gz * gy
    count, zl, yl, width = levels.shape
    fits = count == LEVELS and count * zl * yl == LANES and yl == 8 and zl >= 2
    fits = fits and gy == 2 and gz % 8 == 0 and gz * zl <= KERNEL
    fits = fits and width == 4 * LANES and parts == 32
    if fits:
        return split_body(levels, ct_image, region_means)
    return portable_body(levels, ct_image, region_means)


def solution(mesh):
    return jax.shard_map(
        body,
        mesh=mesh,
        in_specs=(P(None, "gz", "gy", None), P("gz", "gy", None), P()),
        out_specs=(P(None, "gz", "gy", None), P(None, "gz", "gy", None)),
        check_vma=False,
    )
```

```python
import functools
import math

import jax
import jax.numpy as jnp
import numpy as np
from jax import lax
from jax.experimental import pallas as pl
from jax.experimental.pallas import tpu as pltpu
from jax.sharding import PartitionSpec as P

LEVELS = 4
PHASES = 16
UPDATES = 2
KERNEL = 200
LANES = 128


PENALTY = 0.0005
STEP_SIZE = 0.5
FAR = 1e30


def with_halo(block, sides, width):
    for axis, dim in sides:
        count = lax.axis_size(axis)
        forward = [(i, i + 1) for i in range(count - 1)]
        backward = [(target, source) for source, target in forward]
        low = lax.ppermute(
            lax.slice_in_dim(block, block.shape[dim] - width, None, axis=dim), axis, forward
        )
        high = lax.ppermute(lax.slice_in_dim(block, 0, width, axis=dim), axis, backward)
        block = jnp.concatenate([low, block, high], axis=dim)
    return block


def evolve(level_pad, picture, region_means):
    interior = level_pad[:, 1:-1, 1:-1, :]
    side_x = jnp.pad(interior, ((0, 0), (0, 0), (0, 0), (1, 1)))
    laplace = level_pad[:, 2:, 1:-1, :] + level_pad[:, :-2, 1:-1, :]
    laplace = laplace + level_pad[:, 1:-1, 2:, :] + level_pad[:, 1:-1, :-2, :]
    laplace = laplace + side_x[..., 2:] + side_x[..., :-2] - 6.0 * interior
    heaviside = 0.5 + jnp.arctan(interior) / math.pi
    delta_term = 1.0 / (math.pi * (1.0 + interior * interior))
    forces = [jnp.zeros_like(interior[0]) for level_id in range(LEVELS)]
    for phase_id in range(PHASES):
        differ = picture - region_means[phase_id]
        energy = differ * differ
        factors = []
        for level_id in range(LEVELS):
            if phase_id >> level_id & 1:
                factors.append(heaviside[level_id])
            else:
                factors.append(1.0 - heaviside[level_id])
        for level_id in range(LEVELS):
            sign_value = 1.0 if phase_id >> level_id & 1 else -1.0
            others = energy
            for other_id in range(LEVELS):
                if other_id != level_id:
                    others = others * factors[other_id]
            forces[level_id] = forces[level_id] + sign_value * others
    force_all = jnp.stack(forces, axis=0)
    return interior + STEP_SIZE * delta_term * (laplace - force_all)


def minplus_lines(field_in, line_axis, kernel_reach):
    moved_field = jnp.moveaxis(field_in, line_axis, -1)
    line_shape = moved_field.shape
    line_len = line_shape[-1]
    line_rows = moved_field.reshape(-1, line_len)
    row_count = line_rows.shape[0]
    positions = jnp.arange(line_len, dtype=jnp.float32)
    distance = positions[:, None] - positions[None, :]
    penalty_table = jnp.where(
        jnp.abs(distance) <= kernel_reach, PENALTY * (distance * distance), jnp.inf
    )
    row_limit = max(1, 1048576 // (line_len * line_len))
    row_block = 1
    while row_block * 2 <= row_limit and row_count % (row_block * 2) == 0:
        row_block = row_block * 2
    grouped = line_rows.reshape(row_count // row_block, row_block, line_len)

    def block_min(block_rows):
        return jnp.min(block_rows[:, None, :] + penalty_table[None, :, :], axis=2)

    result_rows = lax.map(block_min, grouped)
    return jnp.moveaxis(result_rows.reshape(line_shape), -1, line_axis)


def portable_body(levels, ct_image, region_means):
    current = levels
    for _ in range(UPDATES):
        padded = with_halo(current, (("gz", 1), ("gy", 2)), 1)
        current = evolve(padded, ct_image, region_means)
    field = minplus_lines(current, 3, KERNEL)
    for axis, dim in (("gz", 1), ("gy", 2)):
        lines = lax.all_to_all(field, axis, split_axis=3, concat_axis=dim, tiled=True)
        lines = minplus_lines(lines, dim, KERNEL)
        field = lax.all_to_all(lines, axis, split_axis=dim, concat_axis=3, tiled=True)
    return current, field


def pack_kernel(share, zl, yl, lev_hbm, ct_hbm, out_hbm, lev, ct_ref, up_ref, down_ref, side_ref,
                stage, lines, turned, picture, out_ref, sems):
    width = lev.shape[1]
    parts = width // share
    blocks = width // LANES
    halo, quarter = share + 4, (share + 4) // 4
    chunk = halo + quarter
    count = LEVELS * zl
    tile = zl * yl
    arriving = [pltpu.make_async_copy(ct_hbm, ct_ref, sems.at[0])]
    for b in range(blocks):
        here = stage.at[pl.ds(b * LANES, LANES), :]
        source = lev_hbm.at[:, pl.ds(b * LANES, LANES)]
        arriving.append(pltpu.make_async_copy(source, here, sems.at[1 + b]))
    for copy in arriving:
        copy.start()
    lines[pl.ds(0, 8), :] = jnp.zeros((8, LANES), jnp.float32)
    lines[pl.ds(8 + width, 8), :] = jnp.zeros((8, LANES), jnp.float32)

    for copy in arriving:
        copy.wait()
    across = jnp.concatenate([ct_ref[:, b * LANES:(b + 1) * LANES] for b in range(blocks)], axis=0).T
    for n in range(blocks):
        turn = lambda rows, by: pltpu.roll(rows, by % blocks * tile, 1) if by % blocks else rows
        turned[n, pl.ds(0, 8), :] = turn(across[LANES - 8:], n + 1)
        turned[n, pl.ds(8, LANES), :] = turn(across, n)
        turned[n, pl.ds(8 + LANES, 8), :] = turn(across[:8], n - 1)
    group = lax.broadcasted_iota(jnp.int32, (8, LANES), 1) // tile
    each = LANES // share
    for r in range(parts):
        b, at = r // each, 8 + r % each * share - 2
        value = None
        for t in range(4):
            run = turned[(t - b) % blocks, pl.ds(at + quarter * t, 8), :]
            value = run if value is None else jnp.where(group >= t, run, value)
        picture[pl.ds(8 * r, 8), :] = value
    for b in range(blocks):
        block = [stage[pl.ds(b * LANES + y, count, stride=yl), :] for y in range(yl)]
        lines[pl.ds(8 + b * LANES, LANES), :] = jnp.concatenate(block, axis=0).T

    leaving = []
    sub = lax.broadcasted_iota(jnp.int32, (8, LANES), 0)

    def out_tile(tile):
        value = None
        for r in range(8 * tile // chunk, min((8 * tile + 7) // chunk + 1, parts)):
            for source, begin, length, origin in (
                (picture, r * chunk, quarter, 8 * r),
                (lines, r * chunk + quarter, halo, 6 + r * share),
            ):
                if begin + length <= 8 * tile or begin >= 8 * tile + 8:
                    continue
                piece = source[pl.ds(8 * tile - begin + origin, 8), :]
                value = piece if value is None else jnp.where(sub >= begin - 8 * tile, piece, value)
        return value

    start = 0
    for b in range(blocks):
        known = parts if b + 1 == blocks else (b + 1) * LANES // share - 1
        stop = known * chunk // 8 * 8
        for tile in range(start // 8, stop // 8):
            out_ref[pl.ds(8 * tile, 8), :] = out_tile(tile)
        rows = pl.ds(start, stop - start)
        leaving.append(
            pltpu.make_async_copy(out_ref.at[rows, :], out_hbm.at[rows, :], sems.at[1 + blocks + b])
        )
        leaving[-1].start()
        start = stop
    for b in range(blocks):
        lev[:, b * LANES:(b + 1) * LANES] = stage[pl.ds(b * LANES, LANES), :]
    plane = zl * yl
    for k in range(LEVELS):
        at = pl.ds(2 * k * yl, 2 * yl)
        up_ref[at, :] = lev[pl.ds((k + 1) * plane - 2 * yl, 2 * yl), :]
        down_ref[at, :] = lev[pl.ds(k * plane, 2 * yl), :]
    at = pl.ds(2 * LEVELS * yl, yl)
    up_ref[at, :] = ct_ref[pl.ds(plane - yl, yl), :]
    down_ref[at, :] = ct_ref[pl.ds(0, yl), :]
    upper = lax.axis_index("gy") == 0
    near = jnp.where(upper, yl - 1, 0)
    next_near = jnp.where(upper, yl - 2, 1)
    for k in range(LEVELS):
        for z in range(zl):
            base = k * plane + z * yl
            side_ref[pl.ds(2 * zl * k + z, 1), :] = lev[pl.ds(base + near, 1), :]
            side_ref[pl.ds(2 * zl * k + zl + z, 1), :] = lev[pl.ds(base + next_near, 1), :]
    for z in range(zl):
        side_ref[pl.ds(2 * zl * LEVELS + z, 1), :] = ct_ref[pl.ds(z * yl + near, 1), :]
    for copy in leaving:
        copy.wait()


HALF_ANGLE = (
    0.6366196870803833, -0.21219870448112488, 0.12714172899723053, -0.0893140509724617,
    0.06329755485057831, -0.03813650459051132, 0.015633534640073776, -0.0030433274805545807,
)


def heaviside_and_rate(u):
    s = 1.0 + u * u
    q = lax.rsqrt(s)
    r = u / (1.0 + s * q)
    y = r * r
    p = HALF_ANGLE[-1]
    for c in HALF_ANGLE[-2::-1]:
        p = p * y + c
    return 0.5 + r * p, (q * q) * (STEP_SIZE / math.pi)


def cost_of(d):
    return float(np.float32(PENALTY) * np.float32(d * d))


def tables_kernel(gy, zl, yl, mean_ref, coef_ref, ypen):
    lane = lax.broadcasted_iota(jnp.int32, (1, LANES), 1)
    level = lane // zl % LEVELS
    y = lane // (LEVELS * zl)

    def mean_of(bits, own):
        value = jnp.zeros((1, LANES), jnp.float32)
        for k in range(LEVELS):
            phase = own << k
            for n in range(3):
                phase |= (bits >> n & 1) << ((k + 1 + n) % LEVELS)
            value = jnp.where(level == k, mean_ref[phase], value)
        return value

    slope, const = [], []
    for bits in range(8):
        low, high = mean_of(bits, 0), mean_of(bits, 1)
        slope.append(-2.0 * (high - low))
        const.append((high - low) * (high + low))
    for n in range(3):
        for bits in range(8):
            if bits >> n & 1:
                slope[bits] = slope[bits] - slope[bits ^ (1 << n)]
                const[bits] = const[bits] - const[bits ^ (1 << n)]
    for n in range(8):
        coef_ref[pl.ds(n, 1), :] = slope[n]
        coef_ref[pl.ds(8 + n, 1), :] = const[n]

    for gap in range(-(gy - 1), gy):
        for turn in range(yl):
            d = (yl * gap + y - (y + turn) % yl).astype(jnp.float32)
            pen = jnp.where(jnp.abs(d) <= KERNEL, PENALTY * (d * d), FAR)
            ypen[pl.ds(8 * ((gap + gy - 1) * yl + turn), 8), :] = jnp.broadcast_to(pen, (8, LANES))


SLOT = 32


def middle_kernel(share, gz, gy, zl, yl, coef_ref, ypen, in_ref, out_ref, levels, picture,
                  first, evolved, shifted, zdone, done, kept, sems):
    parts = gz * gy
    halo, quarter = share + 4, (share + 4) // 4
    chunk = halo + quarter
    tile = zl * yl
    deep = gz + 2
    me = lax.axis_index("gy") * gz + lax.axis_index("gz")

    lane = lax.broadcasted_iota(jnp.int32, (1, LANES), 1)
    level = lane // zl % LEVELS
    z = lane % zl
    y = lane // (LEVELS * zl)

    def moved(value, index):
        return jnp.take_along_axis(
            value, jnp.broadcast_to(index, value.shape), axis=1, mode="promise_in_bounds"
        )

    def z_turned(value, turn):
        return moved(value, lane + (z + turn) % zl - z)

    def level_turned(value, turn):
        return moved(value, lane + ((level + turn) % LEVELS - level) * zl)

    def y_turned(value, turn):
        return pltpu.roll(value, LANES - turn * LEVELS * zl, 1)

    def stacked(blocks):
        return jnp.concatenate(blocks, axis=0)

    def row_of(a, b, x):
        return (b * deep + a + 1) * SLOT + 8 + x

    zero = jnp.zeros((SLOT, LANES), jnp.float32)
    for b in range(gy):
        for a in (-1, gz):
            levels[pl.ds(row_of(a, b, -8), SLOT), :] = zero
            first[pl.ds(row_of(a, b, -8), SLOT), :] = zero
        for a in range(gz):
            source = (b * gz + a) * chunk + quarter
            levels[pl.ds(row_of(a, b, -2), halo), :] = in_ref[pl.ds(source, halo), :]
        for a in range(0, gz, 4):
            batch = range(a, a + 4)
            packed = stacked([in_ref[pl.ds((b * gz + n) * chunk, 8), :] for n in batch])
            for t in range(4):
                run = moved(packed, t * tile + z * yl + y)
                for n in batch:
                    at = 8 * (n - a)
                    rows = pl.ds(row_of(n, b, t * quarter - 2), quarter)
                    picture[rows, :] = run[at:at + quarter]

    coefs = [coef_ref[pl.ds(n, 1), :] for n in range(16)]
    slope, const = coefs[:8], coefs[8:]

    def step(read, tiles, f):
        def beside(dz, dy):
            none = jnp.zeros_like(read(tiles[0], 0, 0, 0))
            return stacked([
                read(tile, dz, dy, 0) if 0 <= tile[1] + dy < gy else none for tile in tiles
            ])

        here = beside(0, 0)
        h, rate = heaviside_and_rate(here)
        near = stacked([read(t, 0, 0, -1) + read(t, 0, 0, 1) for t in tiles]) - 6.0 * here
        near = near + z_turned(jnp.where(z == 0, beside(1, 0), here), 1)
        near = near + z_turned(jnp.where(z == zl - 1, beside(-1, 0), here), zl - 1)
        near = near + y_turned(jnp.where(y == 0, beside(0, 1), here), 1)
        near = near + y_turned(jnp.where(y == yl - 1, beside(0, -1), here), yl - 1)
        h1, h2, h3 = (level_turned(h, turn) for turn in (1, 2, 3))
        g = lambda bits: f(bits) + h1 * f(bits | 1)
        force = (g(0) + h2 * g(2)) + h3 * (g(4) + h2 * g(6))
        return here + rate * (near - force)

    def run_of(ref):
        return lambda t, dz, dy, dx: ref[pl.ds(row_of(t[0] + dz, t[1] + dy, dx), share), :]

    def terms(pic):
        return lambda bits: slope[bits] * pic + const[bits]

    batches = [[(a + n, b) for n in range(4)] for b in range(gy) for a in range(0, gz, 4)]
    for tiles in batches:
        pic = stacked([run_of(picture)(t, 0, 0, 0) for t in tiles])
        f = [terms(pic)(bits) for bits in range(8)]
        at = pl.ds((tiles[0][1] * gz + tiles[0][0]) * share, 4 * share)
        for bits in range(8):
            kept[bits, at, :] = f[bits]
        value = step(run_of(levels), tiles, lambda bits: f[bits])
        for n, (a, b) in enumerate(tiles):
            first[pl.ds(row_of(a, b, 0), share), :] = value[n * share:(n + 1) * share]

    def across(ref):
        return lambda t, dz, dy, dx: ref[pl.ds(row_of(dz, t[1] + dy, t[0] + dx), gz, stride=SLOT), :]

    ends = [(x, b) for x in (-1, share) for b in range(gy)]
    pic = stacked([across(picture)(t, 0, 0, 0) for t in ends])
    value = step(across(levels), ends, terms(pic))
    for n, (x, b) in enumerate(ends):
        outside = (me == 0) if x < 0 else (me == parts - 1)
        rows = value[n * gz:(n + 1) * gz]
        first[pl.ds(row_of(0, b, x), gz, stride=SLOT), :] = jnp.where(outside, 0.0, rows)

    def block_of(a, b):
        return (b * deep + a + 1) * share

    far = jnp.full((share, LANES), FAR, jnp.float32)
    for b in range(gy):
        for a in (-1, gz):
            evolved[pl.ds(block_of(a, b), share), :] = far
    for tiles in batches:
        at = pl.ds((tiles[0][1] * gz + tiles[0][0]) * share, 4 * share)
        f = lambda bits: kept[bits, at, :]
        evolved[pl.ds(block_of(*tiles[0]), 4 * share), :] = step(run_of(first), tiles, f)

    for b in range(gy):
        for a in range(-1, gz, 4):
            count = min(4, gz - a) * share
            here = evolved[pl.ds(block_of(a, b), count), :]
            above = evolved[pl.ds(block_of(a + 1, b), count), :]
            for turn in range(1, zl):
                value = z_turned(jnp.where(z < turn, above, here), turn)
                shifted[turn - 1, pl.ds(block_of(a, b), count), :] = value

    def z_unit(half, b, low):
        count = 8

        def at(d, n):
            a, turn = low + n + d // zl, d % zl
            if a < (-1 if turn else 0) or a >= gz:
                return None
            if (a, turn) not in loaded:
                rows = pl.ds(block_of(a, b) + 8 * half, 8)
                loaded[a, turn] = shifted[turn - 1, rows, :] if turn else evolved[rows, :]
            return loaded[a, turn]

        loaded = {}
        best = [at(0, n) for n in range(count)]
        for turn in range(zl):
            loaded = {}
            for d in range(turn or zl, min(gz * zl, KERNEL + 1), zl):
                for n in range(count):
                    pair = [v for v in (at(d, n), at(-d, n)) if v is not None]
                    if pair:
                        value = pair[0] if len(pair) == 1 else jnp.minimum(pair[0], pair[1])
                        best[n] = jnp.minimum(best[n], value + cost_of(d))
        for n in range(count):
            zdone[pl.ds((b * gz + low + n) * share + 8 * half, 8), :] = best[n]

    def y_unit(half, low):
        count = 4
        best = [None] * gy
        for other in range(gy):
            starts = [(other * gz + low + n) * share + 8 * half for n in range(count)]
            whole = stacked([zdone[pl.ds(at, 8), :] for at in starts])
            for turn in range(yl):
                value = y_turned(whole, turn) if turn else whole
                for b in range(gy):
                    at = (b - other + gy - 1) * yl + turn
                    own = other == b and turn == 0
                    new = value if own else value + stacked([ypen[pl.ds(8 * at, 8), :]] * count)
                    best[b] = new if best[b] is None else jnp.minimum(best[b], new)
        for b in range(gy):
            for n in range(count):
                rows = pl.ds((b * gz + low + n) * share + 8 * half, 8)
                done[rows, :] = best[b][8 * n:8 * n + 8]

    halves = share // 8
    copies = []
    for half in range(halves + 1):
        z_units = [(b, low) for b in range(gy) for low in range(0, gz, 8)] if half < halves else []
        y_units = list(range(0, gz, 4)) if half else []
        for n in range(max(len(z_units), len(y_units))):
            if n < len(z_units):
                z_unit(half, *z_units[n])
            if n < len(y_units):
                y_unit(half - 1, y_units[n])
                if half == halves:
                    for b in range(gy):
                        rows = pl.ds((b * gz + y_units[n]) * share, 4 * share)
                        sem = sems.at[len(copies)]
                        copies.append(pltpu.make_async_copy(done.at[rows, :], out_ref.at[rows, :], sem))
                        copies[-1].start()
    for copy in copies:
        copy.wait()


def finish_kernel(yl, in_ref, reg_ref, edge, passed, done, sems):
    width = in_ref.shape[0]
    count = width // 8
    group = 8
    far = jnp.full((8, LANES), FAR, jnp.float32)
    edge[pl.ds(0, 8), :] = far
    edge[pl.ds(8, 8), :] = in_ref[pl.ds(0, 8), :]
    edge[pl.ds(16, 8), :] = in_ref[pl.ds(width - 8, 8), :]
    edge[pl.ds(24, 8), :] = far

    def rows(at):
        if at < 0:
            return edge[pl.ds(8 + at, 8), :]
        if at > width - 8:
            return edge[pl.ds(16 + at - (width - 8), 8), :]
        return in_ref[pl.ds(at, 8), :]

    def x_pass(low):
        best = [rows(8 * (low + n)) for n in range(group)]
        for rho in range(1, 9):
            plus, minus = {}, {}
            for e in range((KERNEL - rho) // 8 + 1):
                cost = cost_of(8 * e + rho)
                for n in range(group):
                    up, down = low + n + e, low + n - e
                    pair = []
                    if 8 * up + rho < width:
                        if up not in plus:
                            plus[up] = rows(8 * up + rho)
                        pair.append(plus[up])
                    if 8 * down - rho > -8:
                        if down not in minus:
                            minus[down] = rows(8 * down - rho)
                        pair.append(minus[down])
                    if not pair:
                        continue
                    value = pair[0] if len(pair) == 1 else jnp.minimum(pair[0], pair[1])
                    best[n] = jnp.minimum(best[n], value + cost)
        for n in range(group):
            passed[pl.ds(8 * (low + n), 8), :] = best[n]

    copies = []
    each = LANES // yl

    def turn(c):
        block = passed[pl.ds(c * LANES, LANES), :].T
        for y in range(yl):
            done[pl.ds(c * LANES + y, each, stride=yl), :] = block[y * each:(y + 1) * each]

    def send(c):
        cols = pl.ds(c * LANES, LANES)
        copies.append(pltpu.make_async_copy(done.at[cols, :], reg_ref.at[:, cols], sems.at[c]))
        copies[-1].start()

    blocks = width // LANES
    for c in range(blocks):
        first = c * LANES // 8
        x_pass(first)
        if c:
            turn(c - 1)
        for low in range(first + group, first + LANES // 8, group):
            x_pass(low)
        if c:
            send(c - 1)
    turn(blocks - 1)
    send(blocks - 1)
    for copy in copies:
        copy.wait()


def corners_kernel(yl, low_ref, high_ref, corner_ref):
    near = jnp.where(lax.axis_index("gy") == 0, yl - 1, 0)
    rows = [low_ref[pl.ds((2 * k + 1) * yl + near, 1), :] for k in range(LEVELS)]
    rows += [high_ref[pl.ds(2 * k * yl + near, 1), :] for k in range(LEVELS)]
    corner_ref[...] = jnp.concatenate(rows, axis=0)


def tile_tools(mean_ref, yl, width):
    upper = lax.axis_index("gy") == 0

    const = [mean_ref[p] * mean_ref[p] for p in range(PHASES)]
    slope = [-2.0 * mean_ref[p] for p in range(PHASES)]
    for k in range(LEVELS):
        for p in range(PHASES):
            if p >> k & 1:
                const[p] = const[p] - const[p ^ (1 << k)]
                slope[p] = slope[p] - slope[p ^ (1 << k)]

    def forces(h, pic):
        c = [None] + [slope[p] * pic + const[p] for p in range(1, PHASES)]
        out = []
        for k in range(LEVELS):
            others = [n for n in range(LEVELS) if n != k]
            part = [c[1 << k | sum((bits >> i & 1) << n for i, n in enumerate(others))]
                    for bits in range(8)]
            for n in others:
                part = [part[i] + h[n] * part[i + 1] for i in range(0, len(part), 2)]
            out.append(part[0])
        return out

    column = lax.broadcasted_iota(jnp.int32, (8, width), 1)
    sub = lax.broadcasted_iota(jnp.int32, (8, width), 0)

    def along_x(u):
        left = jnp.where(column == 0, 0.0, pltpu.roll(u, 1, 1))
        right = jnp.where(column == width - 1, 0.0, pltpu.roll(u, width - 1, 1))
        return left + right

    def advance(here, near, pic):
        pairs = [heaviside_and_rate(u) for u in here]
        force = forces([h for h, _ in pairs], pic)
        return [
            u + rate * (n - 6.0 * u - f)
            for u, n, (_, rate), f in zip(here, near, pairs, force)
        ]

    def along_y(u, row):
        row_up = jnp.where(upper, row, 0.0)
        row_down = jnp.where(upper, 0.0, row)
        above = jnp.where(sub == yl - 1, row_up, pltpu.roll(u, yl - 1, 0))
        below = jnp.where(sub == 0, row_down, pltpu.roll(u, 1, 0))
        return above + below

    return advance, along_x, along_y


def add_neighbours(lev_ref, low_ref, high_ref, zl, yl):
    def level(k, z):
        if z < 0:
            return low_ref[pl.ds((2 * k + 2 + z) * yl, yl), :]
        if z >= zl:
            return high_ref[pl.ds((2 * k + z - zl) * yl, yl), :]
        return lev_ref[pl.ds((k * zl + z) * yl, yl), :]

    return level


def inner_kernel(zl, yl, mean_ref, lev_ref, ct_ref, low_ref, high_ref, side_ref, out_ref):
    advance, along_x, along_y = tile_tools(mean_ref, yl, lev_ref.shape[1])
    level = add_neighbours(lev_ref, low_ref, high_ref, zl, yl)
    for z in range(zl):
        here = [level(k, z) for k in range(LEVELS)]
        near = [
            level(k, z - 1) + level(k, z + 1) + along_x(here[k])
            + along_y(here[k], side_ref[pl.ds(2 * zl * k + z, 1), :])
            for k in range(LEVELS)
        ]
        value = advance(here, near, ct_ref[pl.ds(z * yl, yl), :])
        for k in range(LEVELS):
            out_ref[pl.ds((k * zl + z) * yl, yl), :] = value[k]


def outer_kernel(zl, yl, gz, mean_ref, lev_ref, ct_ref, low_ref, high_ref, side_ref,
                 corner_ref, inner_ref, out_ref, outer, strip, around, strip_first):
    at_z = lax.axis_index("gz")
    edge = jnp.where(lax.axis_index("gy") == 0, yl - 1, 0)
    plane = zl * yl
    advance, along_x, along_y = tile_tools(mean_ref, yl, lev_ref.shape[1])
    level = add_neighbours(lev_ref, low_ref, high_ref, zl, yl)

    def side(k, z):
        if z < 0:
            return corner_ref[pl.ds(k, 1), :]
        if z >= zl:
            return corner_ref[pl.ds(LEVELS + k, 1), :]
        return side_ref[pl.ds(2 * zl * k + z, 1), :]

    picture_at = pl.ds(2 * LEVELS * yl, yl)
    for n, (z, kept, pic) in enumerate((
        (-1, at_z > 0, low_ref[picture_at, :]), (zl, at_z < gz - 1, high_ref[picture_at, :])
    )):
        here = [level(k, z) for k in range(LEVELS)]
        near = [
            level(k, z - 1) + level(k, z + 1) + along_x(here[k]) + along_y(here[k], side(k, z))
            for k in range(LEVELS)
        ]
        value = advance(here, near, pic)
        for k in range(LEVELS):
            outer[pl.ds((2 * k + n) * yl, yl), :] = jnp.where(kept, value[k], 0.0)

    strip[...] = jnp.zeros_like(strip)
    around[...] = jnp.zeros_like(around)
    for k in range(LEVELS):
        for z in range(-1, zl + 1):
            strip[pl.ds(8 * k + z + 1, 1), :] = side(k, z)
        for z in range(zl):
            around[pl.ds(8 * k + z + 1, 1), :] = (
                lev_ref[pl.ds(k * plane + z * yl + edge, 1), :]
                + side_ref[pl.ds(2 * zl * k + zl + z, 1), :]
            )
    for z in range(zl):
        strip[pl.ds(8 * LEVELS + z + 1, 1), :] = side_ref[pl.ds(2 * zl * LEVELS + z, 1), :]
    here = [strip[pl.ds(8 * k, 8), :] for k in range(LEVELS)]
    near = [
        pltpu.roll(u, 7, 0) + pltpu.roll(u, 1, 0) + along_x(u) + around[pl.ds(8 * k, 8), :]
        for k, u in enumerate(here)
    ]
    value = advance(here, near, strip[pl.ds(8 * LEVELS, 8), :])
    for k in range(LEVELS):
        strip_first[pl.ds(8 * k, 8), :] = value[k]

    def after(k, z):
        if z < 0 or z >= zl:
            return outer[pl.ds((2 * k + (z >= zl)) * yl, yl), :]
        return inner_ref[pl.ds((k * zl + z) * yl, yl), :]

    for z in range(zl):
        here = [after(k, z) for k in range(LEVELS)]
        near = [
            after(k, z - 1) + after(k, z + 1) + along_x(here[k])
            + along_y(here[k], strip_first[pl.ds(8 * k + z + 1, 1), :])
            for k in range(LEVELS)
        ]
        value = advance(here, near, ct_ref[pl.ds(z * yl, yl), :])
        for k in range(LEVELS):
            out_ref[pl.ds(k * plane + z * yl, yl), :] = value[k]


def split_body(levels, ct_image, region_means):
    gz, gy = lax.axis_size("gz"), lax.axis_size("gy")
    _, zl, yl, width = levels.shape
    parts = gz * gy
    share = width // parts
    halo, quarter = share + 4, (share + 4) // 4
    chunk = halo + quarter
    f32 = jnp.float32
    vmem = pl.BlockSpec(memory_space=pltpu.VMEM)
    smem = pl.BlockSpec(memory_space=pltpu.SMEM)
    anywhere = pl.BlockSpec(memory_space=pl.ANY)
    params = pltpu.CompilerParams(vmem_limit_bytes=24 * 1024 * 1024)
    scratch = lambda *dims: pltpu.VMEM(dims, f32)
    shape = lambda rows: jax.ShapeDtypeStruct((rows, width), f32)
    message = (2 * LEVELS + 1) * yl
    packed, lines, image, up, down, side = pl.pallas_call(
        functools.partial(pack_kernel, share, zl, yl),
        out_shape=(
            jax.ShapeDtypeStruct((parts * chunk, LANES), f32),
            shape(LANES), shape(zl * yl), shape(message), shape(message),
            shape(2 * zl * LEVELS + zl),
        ),
        in_specs=[pl.BlockSpec(memory_space=pltpu.HBM)] * 2,
        out_specs=(anywhere,) + (vmem,) * 5,
        scratch_shapes=[
            scratch(width + 8, LANES),
            scratch(width + 16, LANES),
            scratch(4, LANES + 16, LANES),
            scratch(8 * parts + 8, LANES),
            scratch(parts * chunk, LANES),
            pltpu.SemaphoreType.DMA((1 + 2 * width // LANES,)),
        ],
        compiler_params=params,
        name="pack",
    )(
        pltpu.with_memory_space_constraint(levels.reshape(LANES, width), pltpu.HBM),
        pltpu.with_memory_space_constraint(ct_image.reshape(zl * yl, width), pltpu.HBM),
    )
    arrived = lax.all_to_all(
        packed.reshape(parts, chunk, 1, LANES), ("gy", "gz"), split_axis=0, concat_axis=0, tiled=True
    ).reshape(parts * chunk, LANES)

    low = lax.ppermute(up, "gz", [(i, i + 1) for i in range(gz - 1)])
    high = lax.ppermute(down, "gz", [(i + 1, i) for i in range(gz - 1)])
    side = lax.ppermute(side, "gy", [(0, 1), (1, 0)])

    lanes = lambda rows: jax.ShapeDtypeStruct((rows, LANES), f32)
    coefs, penalties = pl.pallas_call(
        functools.partial(tables_kernel, gy, zl, yl),
        out_shape=(lanes(16), lanes(8 * yl * (2 * gy - 1))),
        in_specs=[smem],
        out_specs=(vmem, vmem),
        compiler_params=params,
        name="tables",
    )(region_means)
    slots = (gy * (gz + 2) + 1) * SLOT
    blocks = gy * (gz + 2) * share
    passed = pl.pallas_call(
        functools.partial(middle_kernel, share, gz, gy, zl, yl),
        out_shape=jax.ShapeDtypeStruct((width, LANES), f32),
        in_specs=[vmem] * 3,
        out_specs=anywhere,
        scratch_shapes=[
            scratch(slots, LANES),
            scratch(slots, LANES),
            scratch(slots, LANES),
            scratch(blocks, LANES),
            scratch(zl - 1, blocks, LANES),
            scratch(width, LANES),
            scratch(width, LANES),
            scratch(8, width, LANES),
            pltpu.SemaphoreType.DMA((gy * gz // 4,)),
        ],
        compiler_params=params,
        name="middle",
    )(coefs, penalties, arrived)
    passed, low, high, side = lax.optimization_barrier((passed, low, high, side))
    passed = lax.all_to_all(
        passed.reshape(parts, share, LANES), ("gy", "gz"), split_axis=0, concat_axis=0, tiled=True
    ).reshape(width, LANES)

    corner = pl.pallas_call(
        functools.partial(corners_kernel, yl),
        out_shape=shape(2 * LEVELS),
        in_specs=[vmem, vmem],
        out_specs=vmem,
        compiler_params=params,
        name="corners",
    )(low, high)
    corner = lax.ppermute(corner, "gy", [(0, 1), (1, 0)])
    cost = pl.CostEstimate(flops=5_000_000, bytes_accessed=1_000_000, transcendentals=0)
    inner = pl.pallas_call(
        functools.partial(inner_kernel, zl, yl),
        out_shape=shape(LANES),
        in_specs=[smem] + [vmem] * 5,
        out_specs=vmem,
        compiler_params=params,
        cost_estimate=cost,
        name="inner",
    )(region_means, lines, image, low, high, side)
    evolved = pl.pallas_call(
        functools.partial(outer_kernel, zl, yl, gz),
        out_shape=shape(LANES),
        in_specs=[smem] + [vmem] * 7,
        out_specs=vmem,
        scratch_shapes=[
            scratch(2 * LEVELS * yl, width),
            scratch(8 * (LEVELS + 1), width),
            scratch(8 * LEVELS, width),
            scratch(8 * LEVELS, width),
        ],
        compiler_params=params,
        cost_estimate=cost,
        name="outer",
    )(region_means, lines, image, low, high, side, corner, inner)

    regularized = pl.pallas_call(
        functools.partial(finish_kernel, yl),
        out_shape=shape(LANES),
        in_specs=[vmem],
        out_specs=anywhere,
        scratch_shapes=[
            scratch(32, LANES),
            scratch(width, LANES),
            scratch(width + 8, LANES),
            pltpu.SemaphoreType.DMA((width // LANES,)),
        ],
        compiler_params=params,
        name="finish",
    )(passed)
    return evolved.reshape(levels.shape), regularized.reshape(levels.shape)


def body(levels, ct_image, region_means):
    gz, gy = lax.axis_size("gz"), lax.axis_size("gy")
    parts = gz * gy
    count, zl, yl, width = levels.shape
    fits = count == LEVELS and count * zl * yl == LANES and yl == 8 and zl >= 2
    fits = fits and gy == 2 and gz % 8 == 0 and gz * zl <= KERNEL
    fits = fits and width == 4 * LANES and parts == 32
    if fits:
        return split_body(levels, ct_image, region_means)
    return portable_body(levels, ct_image, region_means)


def solution(mesh):
    return jax.shard_map(
        body,
        mesh=mesh,
        in_specs=(P(None, "gz", "gy", None), P("gz", "gy", None), P()),
        out_specs=(P(None, "gz", "gy", None), P(None, "gz", "gy", None)),
        check_vma=False,
    )
```
